32 devices in a mesh: dp: 8 (over z, y), expert: 4 (over x, core).
Axes of the slice: x: 2, y: 2, z: 4, core: 2. Of those that a mesh axis runs over, the one named last changes fastest.
Arguments:
- tokens: bfloat16 [50176, 384], P(('dp', 'expert')), may hold values from -6 to 6
- ln1_gain: float32 [384], replicated, may hold values from 0.5 to 1.5
- ln1_bias: float32 [384], replicated, may hold values from -1.75 to 1.75
- qkv_weight: bfloat16 [384, 1152], replicated, may hold values from -0.3125 to 0.3125
- q_bias: float32 [384], replicated, may hold values from -1.75 to 1.75
- v_bias: float32 [384], replicated, may hold values from -1.75 to 1.75
- bias_table: float32 [169, 12], replicated, may hold values from -6 to 6
- out_weight: bfloat16 [384, 384], replicated, may hold values from -0.625 to 0.625
- out_bias: float32 [384], replicated, may hold values from -1.75 to 1.75
- ln2_gain: float32 [384], replicated, may hold values from 0.5 to 1.5
- ln2_bias: float32 [384], replicated, may hold values from -1.75 to 1.75
- router_weight: float32 [384, 8], replicated, may hold values from -0.21875 to 0.21875
- up_weight: bfloat16 [8, 384, 1536], P('expert'), may hold values from -0.3125 to 0.3125
- up_bias: float32 [8, 1536], P('expert'), may hold values from -0.625 to 0.625
- down_weight: bfloat16 [8, 1536, 384], P('expert'), may hold values from -1.25 to 1.25
- down_bias: float32 [8, 384], P('expert'), may hold values from -2.5 to 2.5
- expert_of: int32 [50176], P(('dp', 'expert')), may hold values from 0 to 7, as said below
- slot_of: int32 [50176], P(('dp', 'expert')), may hold values from -1 to 244, as said below
- grad_output: bfloat16 [50176, 384], P(('dp', 'expert')), may hold values from -6 to 6
Outputs:
- output: bfloat16 [50176, 384], P(('dp', 'expert'))
- grad_tokens: float32 [50176, 384], P(('dp', 'expert'))
- grad_ln1_gain: float32 [384], replicated
- grad_ln1_bias: float32 [384], replicated
- grad_qkv_weight: float32 [384, 1152], replicated
- grad_q_bias: float32 [384], replicated
- grad_v_bias: float32 [384], replicated
- grad_bias_table: float32 [169, 12], replicated
- grad_out_weight: float32 [384, 384], replicated
- grad_out_bias: float32 [384], replicated
- grad_ln2_gain: float32 [384], replicated
- grad_ln2_bias: float32 [384], replicated
- grad_router_weight: float32 [384, 8], replicated
- grad_up_weight: float32 [8, 384, 1536], P('expert')
- grad_up_bias: float32 [8, 1536], P('expert')
- grad_down_weight: float32 [8, 1536, 384], P('expert')
- grad_down_bias: float32 [8, 384], P('expert')
The draws below stay inside these ranges and needn't reach their ends.
Inputs may be any that keep to these rules, and one draw needn't show every extreme that they name: `expert_of`: in every aligned block of 1568 tokens (one device's) some expert is named by more than 245 tokens. `slot_of`: the token's rank in token order among the tokens of its block of 1568 with the same expert, where that rank is below 245; -1 otherwise.
All inputs are finite; a program needn't handle non-finite values.
Results may differ from the reference program's by a relative error of at most 0.015.
Values may be sent and summed in bfloat16 or wider, within the bound.
A program may use at most 192 MiB of HBM per device.

```python
import jax
import jax.numpy as jnp
from jax import lax

D = 384
HEADS = 12
HEAD = 32
FF = 1536
EXPERTS = 8
WINDOW = 7
SIDE = 14
SHIFT = 3
TABLE = 169
TOK_DEV = 1568
CAP = 245
TOKENS = 50176


def routing(key):
    blocks = TOKENS // TOK_DEV
    key_common, key_busy, key_order, key_others = jax.random.split(key, 4)
    common = jax.random.randint(key_common, (), 0, EXPERTS)
    own_busy = jax.random.randint(key_busy, (blocks,), 0, EXPERTS)
    busy = jnp.where(jnp.arange(blocks) < EXPERTS, common, own_busy)
    orders = jax.vmap(lambda block_key: jax.random.permutation(block_key, TOK_DEV))(jax.random.split(key_order, blocks))
    others = jax.random.randint(key_others, (blocks, TOK_DEV), 0, EXPERTS)
    chosen = jnp.where(orders < CAP + TOK_DEV // 16, busy[:, None], others).astype(jnp.int32)
    onehot = (chosen[:, :, None] == jnp.arange(EXPERTS)).astype(jnp.int32)
    counts = jnp.cumsum(onehot, axis=1)
    rank_of = jnp.sum((counts - 1) * onehot, axis=2)
    slot_vals = jnp.where(rank_of < CAP, rank_of, -1).astype(jnp.int32)
    return (chosen.reshape(TOKENS), slot_vals.reshape(TOKENS))


def draw_expert_of(key, part):
    return routing(key)[0]


def draw_slot_of(key, part):
    return routing(key)[1]


def level_of(key, extent, shards, least, high):
    gain, own = 1.0, jax.random.fold_in(key, 6)
    for dim, parts in shards:
        draws = jnp.exp(jax.random.uniform(jax.random.fold_in(own, dim), (parts,), jnp.float32, least / len(shards), high / len(shards)))
        gain = gain * jnp.repeat(draws, extent[dim] // parts).reshape([-1 if axis == dim else 1 for axis in range(len(extent))])
    return gain


def scatter_about(rng, dims, deviation, most, cuts=(), kind=jnp.bfloat16):
    factor_of = level_of(rng, dims, cuts, -0.22, 0.18) if cuts else 1.0
    array = jax.random.normal(rng, dims, jnp.float32) * deviation * factor_of
    return jnp.minimum(jnp.maximum(array, -most), most).astype(kind)


def setup_inputs(seed: int = 0) -> dict:
    key_list = jax.random.split(jax.random.key(seed), 20)
    return {
        "tokens": scatter_about(key_list[0], (TOKENS, D), 1.0, 6.0, ((0, 32),)),
        "ln1_gain": jnp.clip(1.0 + 0.1 * jax.random.normal(key_list[1], (D,), jnp.float32), 0.5, 1.5),
        "ln1_bias": scatter_about(key_list[2], (D,), 0.3, 1.75, (), jnp.float32),
        "qkv_weight": scatter_about(key_list[3], (D, 3 * D), D ** -0.5, 0.3125),
        "q_bias": scatter_about(key_list[4], (D,), 0.3, 1.75, (), jnp.float32),
        "v_bias": scatter_about(key_list[5], (D,), 0.3, 1.75, (), jnp.float32),
        "bias_table": scatter_about(key_list[6], (TABLE, HEADS), 1.0, 6.0, (), jnp.float32),
        "out_weight": scatter_about(key_list[7], (D, D), (D // 4) ** -0.5, 0.625),
        "out_bias": scatter_about(key_list[8], (D,), 0.3, 1.75, (), jnp.float32),
        "ln2_gain": jnp.clip(1.0 + 0.1 * jax.random.normal(key_list[9], (D,), jnp.float32), 0.5, 1.5),
        "ln2_bias": scatter_about(key_list[10], (D,), 0.3, 1.75, (), jnp.float32),
        "router_weight": scatter_about(key_list[11], (D, EXPERTS), (2 * D) ** -0.5, 0.21875, (), jnp.float32),
        "up_weight": scatter_about(key_list[12], (EXPERTS, D, FF), D ** -0.5, 0.3125, ((0, 4),)),
        "up_bias": scatter_about(key_list[13], (EXPERTS, FF), 0.1, 0.625, ((0, 4),), jnp.float32),
        "down_weight": scatter_about(key_list[14], (EXPERTS, FF, D), (FF // 64) ** -0.5, 1.25, ((0, 4),)),
        "down_bias": scatter_about(key_list[15], (EXPERTS, D), 0.4, 2.5, ((0, 4),), jnp.float32),
        "expert_of": draw_expert_of(jax.random.fold_in(key_list[19], 71), 0),
        "slot_of": draw_slot_of(jax.random.fold_in(key_list[19], 71), 0),
        "grad_output": scatter_about(key_list[18], (TOKENS, D), 1.0, 6.0, ((0, 32),)),
    }


@jax.custom_vjp
def low(v):
    return lax.optimization_barrier(v.astype(jnp.bfloat16)).astype(jnp.float32)

@jax.custom_vjp
def low_back(v):
    return v

def low_keep(v):
    return (low(v), None)

def low_pass(kept, grad):
    return (grad,)

def back_keep(v):
    return (v, None)

def back_low(kept, grad):
    return (low(grad),)
low.defvjp(low_keep, low_pass)
low_back.defvjp(back_keep, back_low)
EPSILON = 1e-05
MASK_NEG = -100.0
HIGHEST = lax.Precision.HIGHEST

def layer_norm(inputs, scaling, offset):
    center = inputs - lax.optimization_barrier(jnp.mean(inputs, axis=-1, keepdims=True))
    spread = lax.optimization_barrier(jnp.mean(center * center, axis=-1, keepdims=True))
    return center * lax.rsqrt(spread + EPSILON) * scaling + offset

def to_windows(grid):
    image_count = grid.shape[0]
    channels = grid.shape[-1]
    per_side = SIDE // WINDOW
    split = grid.reshape(image_count, per_side, WINDOW, per_side, WINDOW, channels)
    return split.transpose(0, 1, 3, 2, 4, 5).reshape(image_count * per_side * per_side, WINDOW * WINDOW, channels)

def from_windows(windows, image_count):
    channels = windows.shape[-1]
    per_side = SIDE // WINDOW
    split = windows.reshape(image_count, per_side, per_side, WINDOW, WINDOW, channels)
    return split.transpose(0, 1, 3, 2, 4, 5).reshape(image_count, SIDE, SIDE, channels)

def shift_in(rows_in, image_count):
    grid = rows_in.reshape(image_count, SIDE, SIDE, rows_in.shape[-1])
    return to_windows(jnp.roll(grid, (-SHIFT, -SHIFT), axis=(1, 2)))

def shift_out(windows, image_count):
    grid = jnp.roll(from_windows(windows, image_count), (SHIFT, SHIFT), axis=(1, 2))
    return grid.reshape(image_count * SIDE * SIDE, windows.shape[-1])

def window_mask(image_count):
    places = jnp.arange(SIDE)
    bands = (places >= SIDE - WINDOW).astype(jnp.int32) + (places >= SIDE - SHIFT).astype(jnp.int32)
    regions = (bands[:, None] * 3 + bands[None, :]).reshape(1, SIDE, SIDE, 1)
    labels = to_windows(regions)[:, :, 0]
    masked = jnp.where(labels[:, :, None] != labels[:, None, :], MASK_NEG, 0.0).astype(jnp.float32)
    return jnp.tile(masked, (image_count, 1, 1))

def position_table():
    cells = jnp.arange(WINDOW * WINDOW)
    rowpos = cells // WINDOW
    colpos = cells % WINDOW
    index_map = (rowpos[:, None] - rowpos[None, :] + WINDOW - 1) * (2 * WINDOW - 1) + (colpos[:, None] - colpos[None, :] + WINDOW - 1)
    return (index_map[:, :, None] == jnp.arange(TABLE)).astype(jnp.float32)

def block_forward(inputs, experts_idx, slots_idx, params):
    ln1_gain, ln1_bias, qkv_weight, q_bias, v_bias, bias_table, out_weight, out_bias, ln2_gain, ln2_bias, router_weight, up_weight, up_bias, down_weight, down_bias = params
    image_count = inputs.shape[0] // (SIDE * SIDE)
    normed = low(layer_norm(inputs, ln1_gain, ln1_bias))
    qkv_offset = jnp.concatenate([q_bias, jnp.zeros_like(q_bias), v_bias])
    projected = jnp.dot(normed, qkv_weight, precision=HIGHEST) + qkv_offset
    projected = low(low_back(projected))
    windows = shift_in(projected, image_count).reshape(-1, WINDOW * WINDOW, 3, HEADS, HEAD)
    queries, keys_win, values_win = (windows[:, :, 0], windows[:, :, 1], windows[:, :, 2])
    scores = jnp.einsum('wphd,wqhd->whpq', queries, keys_win, precision=HIGHEST) * HEAD ** (-0.5)
    relative = jnp.einsum('pqt,th->hpq', position_table(), bias_table, precision=HIGHEST)
    scores = low_back(scores + relative[None] + window_mask(image_count)[:, None])
    weights = low(jax.nn.softmax(scores, axis=-1))
    attended = jnp.einsum('whpq,wqhd->wphd', weights, values_win, precision=HIGHEST)
    attended = low(low_back(attended.reshape(-1, WINDOW * WINDOW, D)))
    mixed_out = low_back(jnp.dot(shift_out(attended, image_count), out_weight, precision=HIGHEST) + out_bias)
    residual = inputs + mixed_out
    normed_two = low(layer_norm(residual, ln2_gain, ln2_bias))
    router_probs = jax.nn.softmax(jnp.dot(normed_two, router_weight, precision=HIGHEST), axis=-1)
    chosen = (experts_idx[:, None] == jnp.arange(EXPERTS)).astype(jnp.float32)
    gate_values = lax.optimization_barrier(jnp.sum(router_probs * chosen, axis=-1))
    places = experts_idx * CAP + slots_idx
    dispatch = ((places[:, None] == jnp.arange(EXPERTS * CAP)) & (slots_idx[:, None] >= 0)).astype(jnp.float32)
    buffers = low_back(jnp.dot(dispatch.T, normed_two, precision=HIGHEST).reshape(EXPERTS, CAP, D))
    hidden_pre = low_back(jnp.einsum('ecd,edf->ecf', buffers, up_weight, precision=HIGHEST) + up_bias[:, None])
    hidden = low(jax.nn.gelu(hidden_pre, approximate=False))
    returned = jnp.einsum('ecf,efd->ecd', hidden, down_weight, precision=HIGHEST) + down_bias[:, None]
    returned = low(low_back(returned)).reshape(EXPERTS * CAP, D)
    combined = jnp.dot(dispatch, returned, precision=HIGHEST)
    return residual + gate_values[:, None] * combined

def reference(tokens, ln1_gain, ln1_bias, qkv_weight, q_bias, v_bias, bias_table, out_weight, out_bias, ln2_gain, ln2_bias, router_weight, up_weight, up_bias, down_weight, down_bias, expert_of, slot_of, grad_output):
    params = tuple((parameter.astype(jnp.float32) for parameter in (ln1_gain, ln1_bias, qkv_weight, q_bias, v_bias, bias_table, out_weight, out_bias, ln2_gain, ln2_bias, router_weight, up_weight, up_bias, down_weight, down_bias)))
    blocks = tokens.shape[0] // TOK_DEV
    inputs = tokens.astype(jnp.float32).reshape(blocks, TOK_DEV, D)
    routes = expert_of.reshape(blocks, TOK_DEV)
    slot_rows = slot_of.reshape(blocks, TOK_DEV)

    def whole(inputs_all, params_all):

        def one_block(carried):
            return block_forward(carried[0], carried[1], carried[2], params_all)
        return lax.map(jax.checkpoint(one_block), (inputs_all, routes, slot_rows))
    outputs, pullback = jax.vjp(whole, inputs, params)
    grad_inputs, grad_params = pullback(grad_output.astype(jnp.float32).reshape(blocks, TOK_DEV, D))
    g_ln1_gain, g_ln1_bias, g_qkv, g_qbias, g_vbias, g_table, g_out, g_outbias, g_ln2_gain, g_ln2_bias, g_router, g_up, g_upbias, g_down, g_downbias = grad_params
    return (outputs.reshape(-1, D).astype(jnp.bfloat16), grad_inputs.reshape(-1, D), g_ln1_gain, g_ln1_bias, g_qkv, g_qbias, g_vbias, g_table, g_out, g_outbias, g_ln2_gain, g_ln2_bias, g_router, g_up, g_upbias, g_down, g_downbias)
```

```python
from functools import partial

import jax
import jax.numpy as jnp
import numpy as np
from jax import lax
from jax.experimental import pallas as pl
from jax.experimental.pallas import tpu as pltpu
from jax.sharding import PartitionSpec as P

D = 384
HEADS = 12
HEAD = 32
FF = 1536
EXPERTS = 8
WINDOW = 7
SIDE = 14
SHIFT = 3
CAP = 245
CELLS = WINDOW * WINDOW
IMAGE = SIDE * SIDE
TABLE = (2 * WINDOW - 1) ** 2

ROWS = 64
SLOTS = 256
FRAME = 4 * ROWS
SPAN = 208
GROUP = 4
GROUPS = HEADS // GROUP
LANES = GROUP * HEAD
WIDE = GROUP * ROWS

EPSILON = 1e-05
MASK_NEG = -100.0
SCALE = HEAD ** (-0.5)
HIGHEST = lax.Precision.HIGHEST
F32 = jnp.float32
BF16 = jnp.bfloat16


def source_cells():
    source = np.full((FRAME, 1), -1000, np.int32)
    for row in range(FRAME):
        window, cell = divmod(row, ROWS)
        if cell < CELLS:
            down = (window // 2) * WINDOW + cell // WINDOW
            across = (window % 2) * WINDOW + cell % WINDOW
            source[row, 0] = ((down + SHIFT) % SIDE) * SIDE + (across + SHIFT) % SIDE
    return source


def window_masks():
    places = np.arange(SIDE)
    bands = (places >= SIDE - WINDOW).astype(np.int32) + (places >= SIDE - SHIFT)
    masks = np.zeros((4, ROWS, ROWS), np.float32)
    for window in range(4):
        rows = bands[(window // 2) * WINDOW : (window // 2 + 1) * WINDOW]
        cols = bands[(window % 2) * WINDOW : (window % 2 + 1) * WINDOW]
        labels = (rows[:, None] * 3 + cols[None, :]).reshape(-1)
        masks[window, :CELLS, :CELLS] = np.where(labels[:, None] != labels[None, :], MASK_NEG, 0.0)
    masks[:, CELLS:, :] = -1e30
    return np.tile(masks, (1, 1, GROUP))


def offset_onehot():
    hot = np.zeros((TABLE, ROWS, ROWS), np.float32)
    for q in range(CELLS):
        for p in range(CELLS):
            entry = (p // WINDOW - q // WINDOW + WINDOW - 1) * (2 * WINDOW - 1)
            entry += p % WINDOW - q % WINDOW + WINDOW - 1
            hot[entry, q, p] = 1.0
    return hot.reshape(TABLE, ROWS * ROWS)


def mm(left, right):
    return jnp.dot(left, right, preferred_element_type=F32)


def mm_nt(left, right):
    return lax.dot_general(left, right, (((1,), (1,)), ((), ())), preferred_element_type=F32)


def mm_tn(left, right):
    return lax.dot_general(left, right, (((0,), (0,)), ((), ())), preferred_element_type=F32)


def permutation(source, offset, width):
    places = lax.broadcasted_iota(jnp.int32, (FRAME, width), 1)
    return jnp.where(source + offset == places, 1.0, 0.0).astype(BF16)


def normalize(values):
    center = values - jnp.mean(values, axis=-1, keepdims=True)
    inverse = lax.rsqrt(jnp.mean(center * center, axis=-1, keepdims=True) + EPSILON)
    return center * inverse, inverse


def normalize_pull(grad, hat, inverse, gain):
    scaled = grad * gain
    first = jnp.mean(scaled, axis=-1, keepdims=True)
    second = jnp.mean(scaled * hat, axis=-1, keepdims=True)
    return (scaled - first - hat * second) * inverse


def spread_heads(block):
    heads = lax.broadcasted_iota(jnp.int32, block.shape, 1) // HEAD
    return jnp.concatenate(
        [jnp.where(heads == h, block, jnp.zeros_like(block)) for h in range(GROUP)], axis=0
    )


def pick_heads(wide):
    heads = lax.broadcasted_iota(jnp.int32, (ROWS, LANES), 1) // HEAD
    picked = wide[:ROWS]
    for h in range(1, GROUP):
        picked = jnp.where(heads == h, wide[h * ROWS : (h + 1) * ROWS], picked)
    return picked


def image_span(image):
    offset = lax.rem(image * (IMAGE % 16), 16)
    return pl.multiple_of(image * IMAGE - offset, 16), offset


def split_three(values):
    high = values.astype(BF16)
    rest = values - high.astype(F32)
    middle = rest.astype(BF16)
    return high, middle, (rest - middle.astype(F32)).astype(BF16)


def forward_kernel(
    tokens_ref, grad_ref, route_ref, source_ref, gain1_ref, bias1_ref, qkv_ref, offset_ref, relative_ref,
    mask_ref, out_weight_ref, out_bias_ref, gain2_ref, bias2_ref, router_ref,
    projected_ref, weights_ref, attended_ref, residual_ref, rows_ref, place_ref, aux_ref,
):
    image = pl.program_id(0)
    start, offset = image_span(image)
    source = source_ref[...]
    order = permutation(source, offset, SPAN)
    inputs = mm(order, tokens_ref[pl.ds(start, SPAN), :])
    upstream = mm(order, grad_ref[pl.ds(start, SPAN), :])

    plain = permutation(source, 0, FRAME)
    route = route_ref[0]
    route_cols = mm_nt(plain, route)
    route_rows = mm_nt(route, plain)
    chosen_col = route_cols[:, 0:1]
    slot_col = route_cols[:, 1:2]
    place_row = jnp.where(
        route_rows[1:2] > 0.5, route_rows[0:1] * SLOTS + route_rows[1:2] - 1.0, -1.0
    )
    place_ref[0] = jnp.broadcast_to(place_row, (8, FRAME)).astype(jnp.int32)
    place_col = jnp.where(slot_col > 0.5, chosen_col * SLOTS + slot_col - 1.0, -1.0)

    hat, _ = normalize(inputs)
    normed = (hat * gain1_ref[...] + bias1_ref[...]).astype(BF16)
    projected_ref[...] = (mm(normed, qkv_ref[...]) + offset_ref[...]).astype(BF16)

    for window in range(4):
        rows = slice(window * ROWS, (window + 1) * ROWS)
        for group in range(GROUPS):
            cols = slice(group * LANES, (group + 1) * LANES)
            wide = slice(group * WIDE, (group + 1) * WIDE)
            queries = projected_ref[rows, group * LANES : (group + 1) * LANES]
            keys = projected_ref[rows, D + group * LANES : D + (group + 1) * LANES]
            values = projected_ref[rows, 2 * D + group * LANES : 2 * D + (group + 1) * LANES]
            scores = mm_nt(keys, spread_heads(queries)) * SCALE
            scores = scores + relative_ref[:, wide] + mask_ref[window]
            powers = jnp.exp(scores - jnp.max(scores, axis=0, keepdims=True))
            weights = (powers / jnp.sum(powers, axis=0, keepdims=True)).astype(BF16)
            place = (window * GROUPS + group) * ROWS
            weights_ref[place : place + ROWS, :] = weights
            attended_ref[rows, cols] = pick_heads(mm_tn(weights, values)).astype(BF16)

    residual = inputs + (mm(attended_ref[...], out_weight_ref[...]) + out_bias_ref[...])
    residual_ref[...] = residual
    hat, _ = normalize(residual)
    normed = (hat * gain2_ref[...] + bias2_ref[...]).astype(BF16)
    logits = sum(mm(normed, part) for part in split_three(router_ref[...]))
    logits = jnp.exp(logits - jnp.max(logits, axis=-1, keepdims=True))
    probs = logits / jnp.sum(logits, axis=-1, keepdims=True)
    experts = lax.broadcasted_iota(jnp.int32, (FRAME, EXPERTS), 1).astype(F32)
    gate = jnp.sum(jnp.where(experts == chosen_col, probs, 0.0), axis=-1, keepdims=True)
    rows_ref[:, :D] = normed
    rows_ref[:, D:] = (gate * upstream).astype(BF16)
    aux_ref[:, 0:EXPERTS] = probs
    aux_ref[:, EXPERTS : EXPERTS + 1] = gate
    aux_ref[:, EXPERTS + 1 : EXPERTS + 2] = place_col
    aux_ref[:, EXPERTS + 2 : EXPERTS + 3] = chosen_col


def dispatch_kernel(place_ref, rows_ref, out_ref):
    expert = pl.program_id(0)
    images = place_ref.shape[0]
    places = jnp.concatenate([place_ref[i, 0:1, :] for i in range(images)], axis=1)
    slots = lax.broadcasted_iota(jnp.int32, (SLOTS, places.shape[1]), 0) + expert * SLOTS
    hot = jnp.where(slots == places, 1.0, 0.0).astype(BF16)
    out_ref[0] = mm(hot, rows_ref[...]).astype(BF16)


TILE = 512


def expert_kernel(
    rows_ref, up_ref, up_bias_ref, down_ref, down_bias_ref,
    back_ref, grad_up_ref, grad_up_bias_ref, grad_down_ref, grad_down_bias_ref,
    up_sum, down_sum, up_bias_sum, down_bias_sum,
):
    member = pl.program_id(1)
    last = pl.num_programs(1) - 1

    @pl.when(member == 0)
    def _():
        up_sum[...] = jnp.zeros_like(up_sum)
        down_sum[...] = jnp.zeros_like(down_sum)
        up_bias_sum[...] = jnp.zeros_like(up_bias_sum)
        down_bias_sum[...] = jnp.zeros_like(down_bias_sum)

    inputs = rows_ref[0, 0, :, :D]
    grads = rows_ref[0, 0, :, D:]
    inputs_t = inputs.T
    grads_t = grads.T
    outs = jnp.zeros((SLOTS, D), F32)
    backs = jnp.zeros((SLOTS, D), F32)
    for tile in range(FF // TILE):
        at = slice(tile * TILE, (tile + 1) * TILE)
        pre = mm(inputs, up_ref[0, :, at]) + up_bias_ref[0, :, at]
        grad_hidden = mm_nt(grads, down_ref[0, at, :])
        share = 0.5 + 0.5 * lax.erf(pre * 0.7071067811865476)
        density = jnp.exp(pre * pre * -0.5) * 0.3989422804014327
        hidden = (pre * share).astype(BF16)
        grad_pre = (grad_hidden * (share + pre * density)).astype(BF16)
        outs += mm(hidden, down_ref[0, at, :])
        backs += mm_nt(grad_pre, up_ref[0, :, at])
        down_sum[:, at] += mm(grads_t, hidden)
        up_sum[:, at] += mm(inputs_t, grad_pre)
        up_bias_sum[:, at] += jnp.sum(grad_pre.astype(F32), axis=0, keepdims=True)
    down_bias_sum[...] += jnp.sum(grads.astype(F32), axis=0, keepdims=True)
    back_ref[0, 0, :, :D] = (outs + down_bias_ref[0]).astype(BF16)
    back_ref[0, 0, :, D:] = backs.astype(BF16)

    @pl.when(member == last)
    def _():
        grad_up_ref[0] = up_sum[...].astype(BF16)
        grad_down_ref[0] = down_sum[...].T.astype(BF16)
        grad_up_bias_ref[0] = up_bias_sum[...]
        grad_down_bias_ref[0] = down_bias_sum[...]


def backward_kernel(
    tokens_ref, grad_ref, source_ref, gain1_ref, bias1_ref, qkv_ref, out_weight_ref, gain2_ref, bias2_ref,
    router_ref, projected_ref, weights_ref, attended_ref, residual_ref, aux_ref, returned_ref,
    output_ref, grad_tokens_ref, grad_qkv_ref, grad_out_ref, totals_ref, grad_router_ref, small_ref,
    grad_projected,
):
    image = pl.program_id(0)

    @pl.when(image == 0)
    def _():
        for ref in (output_ref, grad_tokens_ref, grad_qkv_ref, grad_out_ref, totals_ref, grad_router_ref, small_ref):
            ref[...] = jnp.zeros_like(ref)

    start, offset = image_span(image)
    order = permutation(source_ref[...], offset, SPAN)
    inputs = mm(order, tokens_ref[pl.ds(start, SPAN), :])
    upstream = mm(order, grad_ref[pl.ds(start, SPAN), :])
    residual = residual_ref[...]
    aux = aux_ref[...]
    probs = aux[:, 0:EXPERTS]
    gate = aux[:, EXPERTS : EXPERTS + 1]
    place = aux[:, EXPERTS + 1 : EXPERTS + 2].astype(jnp.int32)
    chosen = aux[:, EXPERTS + 2 : EXPERTS + 3]

    slots = lax.broadcasted_iota(jnp.int32, (FRAME, EXPERTS * SLOTS), 1)
    hot = jnp.where(slots == place, 1.0, 0.0).astype(BF16)
    gathered = mm(hot, returned_ref[...])
    combined = gathered[:, :D]
    output = (residual + gate * combined).astype(BF16)
    output_ref[pl.ds(start, SPAN), :] += mm_tn(order, output).astype(BF16)

    hat2, inverse2 = normalize(residual)
    normed2 = (hat2 * gain2_ref[...] + bias2_ref[...]).astype(BF16)
    gate_grad = jnp.sum(upstream * combined, axis=-1, keepdims=True)
    experts = lax.broadcasted_iota(jnp.int32, (FRAME, EXPERTS), 1).astype(F32)
    grad_logits = gate_grad * gate * (jnp.where(experts == chosen, 1.0, 0.0) - probs)
    logits_high, logits_low, _ = split_three(grad_logits)
    grad_router_ref[...] += mm_tn(logits_high, normed2) + mm_tn(logits_low, normed2)
    router_high, router_low, _ = split_three(router_ref[...])
    grad_normed = (
        gathered[:, D:]
        + mm_nt(logits_high, router_high)
        + mm_nt(logits_low, router_high)
        + mm_nt(logits_high, router_low)
    )
    small_ref[0:1, :D] += jnp.sum(grad_normed * hat2, axis=0, keepdims=True)
    small_ref[1:2, :D] += jnp.sum(grad_normed, axis=0, keepdims=True)
    grad_residual = upstream + normalize_pull(grad_normed, hat2, inverse2, gain2_ref[...])
    mixed = grad_residual.astype(BF16)
    grad_out_ref[...] += mm_tn(attended_ref[...], mixed)
    small_ref[2:3, :D] += jnp.sum(mixed.astype(F32), axis=0, keepdims=True)
    grad_attended = mm_nt(mixed, out_weight_ref[...]).astype(BF16)

    for window in range(4):
        rows = slice(window * ROWS, (window + 1) * ROWS)
        for group in range(GROUPS):
            cols = slice(group * LANES, (group + 1) * LANES)
            wide = slice(group * WIDE, (group + 1) * WIDE)
            key_cols = slice(D + group * LANES, D + (group + 1) * LANES)
            value_cols = slice(2 * D + group * LANES, 2 * D + (group + 1) * LANES)
            keys = projected_ref[rows, key_cols]
            values = projected_ref[rows, value_cols]
            spread_queries = spread_heads(projected_ref[rows, cols])
            spread_grads = spread_heads(grad_attended[rows, cols])
            at = (window * GROUPS + group) * ROWS
            weights = weights_ref[at : at + ROWS, :]
            exact = weights.astype(F32)
            grad_weights = mm_nt(values, spread_grads)
            grad_scores = exact * (grad_weights - jnp.sum(exact * grad_weights, axis=0, keepdims=True))
            grad_scores = grad_scores.astype(BF16)
            totals_ref[:, wide] += grad_scores.astype(F32)
            grad_projected[rows, value_cols] = mm(weights, spread_grads).astype(BF16)
            grad_projected[rows, key_cols] = (mm(grad_scores, spread_queries) * SCALE).astype(BF16)
            grad_projected[rows, cols] = (pick_heads(mm_tn(grad_scores, keys)) * SCALE).astype(BF16)

    grads = grad_projected[...]
    hat1, inverse1 = normalize(inputs)
    normed1 = (hat1 * gain1_ref[...] + bias1_ref[...]).astype(BF16)
    grad_qkv_ref[...] += mm_tn(normed1, grads)
    small_ref[5:6, :] += jnp.sum(grads.astype(F32), axis=0, keepdims=True)
    grad_normed = mm_nt(grads, qkv_ref[...])
    small_ref[3:4, :D] += jnp.sum(grad_normed * hat1, axis=0, keepdims=True)
    small_ref[4:5, :D] += jnp.sum(grad_normed, axis=0, keepdims=True)
    grad_inputs = grad_residual + normalize_pull(grad_normed, hat1, inverse1, gain1_ref[...])
    high, low, _ = split_three(grad_inputs)
    grad_tokens_ref[pl.ds(start, SPAN), :] += mm_tn(order, high) + mm_tn(order, low)


def whole(shape):
    return pl.BlockSpec(shape, lambda *_: (0,) * len(shape))


def per_image(rows, columns):
    return pl.BlockSpec((rows, columns), lambda i: (i, 0))


def shards(
    tokens, ln1_gain, ln1_bias, qkv_weight, q_bias, v_bias, bias_table, out_weight, out_bias, ln2_gain, ln2_bias,
    router_weight, up_weight, up_bias, down_weight, down_bias, expert_of, slot_of, grad_output,
):
    members = lax.axis_size("expert")
    local = up_weight.shape[0]
    count = tokens.shape[0]
    images = count // IMAGE
    framed = images * FRAME
    params = pltpu.CompilerParams(dimension_semantics=("arbitrary",), vmem_limit_bytes=60 * 2**20)

    source = jnp.asarray(source_cells())
    masks = jnp.asarray(window_masks())
    hot = jnp.asarray(offset_onehot())
    relative = jnp.dot(bias_table.T, hot, precision=HIGHEST).reshape(HEADS, ROWS, ROWS)
    relative = relative.transpose(1, 0, 2).reshape(ROWS, HEADS * ROWS)
    offset = jnp.concatenate([q_bias, jnp.zeros_like(q_bias), v_bias])[None]
    route = jnp.stack([expert_of, slot_of + 1]).astype(BF16).reshape(2, images, IMAGE).transpose(1, 0, 2)
    route = jnp.pad(route, ((0, 0), (0, 6), (0, FRAME - IMAGE)))
    row = lambda v: v[None]

    projected, weights, attended, residual, rows, place, aux = pl.pallas_call(
        forward_kernel,
        grid=(images,),
        in_specs=[
            whole((count, D)), whole((count, D)), pl.BlockSpec((1, 8, FRAME), lambda i: (i, 0, 0)),
            whole((FRAME, 1)), whole((1, D)), whole((1, D)), whole((D, 3 * D)), whole((1, 3 * D)),
            whole((ROWS, HEADS * ROWS)), whole((4, ROWS, WIDE)), whole((D, D)), whole((1, D)), whole((1, D)),
            whole((1, D)), whole((D, EXPERTS)),
        ],
        out_specs=[
            per_image(FRAME, 3 * D), per_image(4 * GROUPS * ROWS, WIDE), per_image(FRAME, D), per_image(FRAME, D),
            per_image(FRAME, 2 * D), pl.BlockSpec((1, 8, FRAME), lambda i: (i, 0, 0)), per_image(FRAME, 128),
        ],
        out_shape=[
            jax.ShapeDtypeStruct((framed, 3 * D), BF16),
            jax.ShapeDtypeStruct((images * 4 * GROUPS * ROWS, WIDE), BF16),
            jax.ShapeDtypeStruct((framed, D), BF16),
            jax.ShapeDtypeStruct((framed, D), F32),
            jax.ShapeDtypeStruct((framed, 2 * D), BF16),
            jax.ShapeDtypeStruct((images, 8, FRAME), jnp.int32),
            jax.ShapeDtypeStruct((framed, 128), F32),
        ],
        compiler_params=params,
        name="forward",
    )(
        tokens, grad_output, route, source, row(ln1_gain), row(ln1_bias), qkv_weight, offset, relative, masks,
        out_weight, row(out_bias), row(ln2_gain), row(ln2_bias), router_weight,
    )

    sending = pl.pallas_call(
        dispatch_kernel,
        grid=(EXPERTS,),
        in_specs=[whole((images, 8, FRAME)), whole((framed, 2 * D))],
        out_specs=pl.BlockSpec((1, SLOTS, 2 * D), lambda e: (e, 0, 0)),
        out_shape=jax.ShapeDtypeStruct((EXPERTS, SLOTS, 2 * D), BF16),
        compiler_params=params,
        name="dispatch",
    )(place, rows)

    arrived = lax.all_to_all(
        sending.reshape(members, local, SLOTS, 2 * D), "expert", split_axis=0, concat_axis=0, tiled=True
    )
    per_block = pl.BlockSpec((1, 1, SLOTS, 2 * D), lambda j, m: (m, j, 0, 0))

    def per_expert(*shape):
        return pl.BlockSpec((1, *shape), lambda j, m: (j, 0, 0))

    back, grad_up, grad_up_bias, grad_down, grad_down_bias = pl.pallas_call(
        expert_kernel,
        grid=(local, members),
        in_specs=[per_block, per_expert(D, FF), per_expert(1, FF), per_expert(FF, D), per_expert(1, D)],
        out_specs=[per_block, per_expert(D, FF), per_expert(1, FF), per_expert(FF, D), per_expert(1, D)],
        out_shape=[
            jax.ShapeDtypeStruct((members, local, SLOTS, 2 * D), BF16),
            jax.ShapeDtypeStruct((local, D, FF), BF16),
            jax.ShapeDtypeStruct((local, 1, FF), F32),
            jax.ShapeDtypeStruct((local, FF, D), BF16),
            jax.ShapeDtypeStruct((local, 1, D), F32),
        ],
        scratch_shapes=[
            pltpu.VMEM((D, FF), F32), pltpu.VMEM((D, FF), F32), pltpu.VMEM((1, FF), F32), pltpu.VMEM((1, D), F32),
        ],
        compiler_params=pltpu.CompilerParams(
            dimension_semantics=("arbitrary", "arbitrary"), vmem_limit_bytes=60 * 2**20
        ),
        name="experts",
    )(arrived, up_weight, up_bias[:, None], down_weight, down_bias[:, None])

    returned = lax.all_to_all(back, "expert", split_axis=0, concat_axis=0, tiled=True)
    returned = returned.reshape(EXPERTS * SLOTS, 2 * D)
    grad_up, grad_down = lax.psum((grad_up, grad_down), "dp")

    output, grad_tokens, grad_qkv, grad_out, totals, grad_router, small = pl.pallas_call(
        backward_kernel,
        grid=(images,),
        in_specs=[
            whole((count, D)), whole((count, D)), whole((FRAME, 1)), whole((1, D)), whole((1, D)),
            whole((D, 3 * D)), whole((D, D)), whole((1, D)), whole((1, D)), whole((D, EXPERTS)),
            per_image(FRAME, 3 * D), per_image(4 * GROUPS * ROWS, WIDE), per_image(FRAME, D), per_image(FRAME, D),
            per_image(FRAME, 128), whole((EXPERTS * SLOTS, 2 * D)),
        ],
        out_specs=[
            whole((count, D)), whole((count, D)), whole((D, 3 * D)), whole((D, D)),
            whole((ROWS, HEADS * ROWS)), whole((EXPERTS, D)), whole((8, 3 * D)),
        ],
        out_shape=[
            jax.ShapeDtypeStruct((count, D), BF16),
            jax.ShapeDtypeStruct((count, D), F32),
            jax.ShapeDtypeStruct((D, 3 * D), F32),
            jax.ShapeDtypeStruct((D, D), F32),
            jax.ShapeDtypeStruct((ROWS, HEADS * ROWS), F32),
            jax.ShapeDtypeStruct((EXPERTS, D), F32),
            jax.ShapeDtypeStruct((8, 3 * D), F32),
        ],
        scratch_shapes=[pltpu.VMEM((FRAME, 3 * D), BF16)],
        compiler_params=params,
        name="backward",
    )(
        tokens, grad_output, source, row(ln1_gain), row(ln1_bias), qkv_weight, out_weight, row(ln2_gain),
        row(ln2_bias), router_weight, projected, weights, attended, residual, aux, returned,
    )

    totals = totals.reshape(ROWS, HEADS, ROWS).transpose(1, 0, 2).reshape(HEADS, ROWS * ROWS)
    grad_table = lax.dot_general(totals, hot, (((1,), (1,)), ((), ())), precision=HIGHEST)
    grad_qkv, grad_out = lax.psum((grad_qkv.astype(BF16), grad_out.astype(BF16)), ("dp", "expert"))
    grad_table, grad_router, small = lax.psum((grad_table, grad_router, small), ("dp", "expert"))
    grad_up_bias, grad_down_bias = lax.psum((grad_up_bias, grad_down_bias), "dp")
    return (
        output,
        grad_tokens,
        small[3, :D],
        small[4, :D],
        grad_qkv.astype(F32),
        small[5, :D],
        small[5, 2 * D :],
        grad_table.T,
        grad_out.astype(F32),
        small[2, :D],
        small[0, :D],
        small[1, :D],
        grad_router.T,
        grad_up.astype(F32),
        grad_up_bias[:, 0],
        grad_down.astype(F32),
        grad_down_bias[:, 0],
    )


def solution(mesh):
    tokens = P(("dp", "expert"), None)
    expert = P("expert", None, None)
    expert_bias = P("expert", None)
    routes = P(("dp", "expert"))
    return jax.shard_map(
        shards,
        mesh=mesh,
        in_specs=(
            tokens, P(), P(), P(), P(), P(), P(), P(), P(), P(), P(), P(), expert, expert_bias, expert, expert_bias,
            routes, routes, tokens,
        ),
        out_specs=(
            tokens, tokens, P(), P(), P(), P(), P(), P(), P(), P(), P(), P(), P(), expert, expert_bias, expert,
            expert_bias,
        ),
        check_vma=False,
    )
```

```python
from functools import partial

import jax
import jax.numpy as jnp
import numpy as np
from jax import lax
from jax.experimental import pallas as pl
from jax.experimental.pallas import tpu as pltpu
from jax.sharding import PartitionSpec as P

D = 384
HEADS = 12
HEAD = 32
FF = 1536
EXPERTS = 8
WINDOW = 7
SIDE = 14
SHIFT = 3
CAP = 245
CELLS = WINDOW * WINDOW
IMAGE = SIDE * SIDE
TABLE = (2 * WINDOW - 1) ** 2

ROWS = 64
SLOTS = 256
FRAME = 4 * ROWS
SPAN = 208
GROUP = 4
GROUPS = HEADS // GROUP
LANES = GROUP * HEAD
WIDE = GROUP * ROWS

EPSILON = 1e-05
MASK_NEG = -100.0
SCALE = HEAD ** (-0.5)
HIGHEST = lax.Precision.HIGHEST
F32 = jnp.float32
BF16 = jnp.bfloat16


def source_cells():
    source = np.full((FRAME, 1), -1000, np.int32)
    for row in range(FRAME):
        window, cell = divmod(row, ROWS)
        if cell < CELLS:
            down = (window // 2) * WINDOW + cell // WINDOW
            across = (window % 2) * WINDOW + cell % WINDOW
            source[row, 0] = ((down + SHIFT) % SIDE) * SIDE + (across + SHIFT) % SIDE
    return source


def window_masks():
    places = np.arange(SIDE)
    bands = (places >= SIDE - WINDOW).astype(np.int32) + (places >= SIDE - SHIFT)
    masks = np.zeros((4, ROWS, ROWS), np.float32)
    for window in range(4):
        rows = bands[(window // 2) * WINDOW : (window // 2 + 1) * WINDOW]
        cols = bands[(window % 2) * WINDOW : (window % 2 + 1) * WINDOW]
        labels = (rows[:, None] * 3 + cols[None, :]).reshape(-1)
        masks[window, :CELLS, :CELLS] = np.where(labels[:, None] != labels[None, :], MASK_NEG, 0.0)
    masks[:, CELLS:, :] = -1e30
    return np.tile(masks, (1, 1, GROUP))


def offset_onehot():
    hot = np.zeros((TABLE, ROWS, ROWS), np.float32)
    for q in range(CELLS):
        for p in range(CELLS):
            entry = (p // WINDOW - q // WINDOW + WINDOW - 1) * (2 * WINDOW - 1)
            entry += p % WINDOW - q % WINDOW + WINDOW - 1
            hot[entry, q, p] = 1.0
    return hot.reshape(TABLE, ROWS * ROWS)


def mm(left, right):
    return jnp.dot(left, right, preferred_element_type=F32)


def mm_nt(left, right):
    return lax.dot_general(left, right, (((1,), (1,)), ((), ())), preferred_element_type=F32)


def mm_tn(left, right):
    return lax.dot_general(left, right, (((0,), (0,)), ((), ())), preferred_element_type=F32)


def permutation(source, offset, width):
    places = lax.broadcasted_iota(jnp.int32, (FRAME, width), 1)
    return jnp.where(source + offset == places, 1.0, 0.0).astype(BF16)


def normalize(values):
    center = values - jnp.mean(values, axis=-1, keepdims=True)
    inverse = lax.rsqrt(jnp.mean(center * center, axis=-1, keepdims=True) + EPSILON)
    return center * inverse, inverse


def normalize_pull(grad, hat, inverse, gain):
    scaled = grad * gain
    first = jnp.mean(scaled, axis=-1, keepdims=True)
    second = jnp.mean(scaled * hat, axis=-1, keepdims=True)
    return (scaled - first - hat * second) * inverse


def spread_heads(block):
    heads = lax.broadcasted_iota(jnp.int32, block.shape, 1) // HEAD
    return jnp.concatenate(
        [jnp.where(heads == h, block, jnp.zeros_like(block)) for h in range(GROUP)], axis=0
    )


def pick_heads(wide):
    heads = lax.broadcasted_iota(jnp.int32, (ROWS, LANES), 1) // HEAD
    picked = wide[:ROWS]
    for h in range(1, GROUP):
        picked = jnp.where(heads == h, wide[h * ROWS : (h + 1) * ROWS], picked)
    return picked


def image_span(image):
    offset = lax.rem(image * (IMAGE % 16), 16)
    return pl.multiple_of(image * IMAGE - offset, 16), offset


def split_three(values):
    high = values.astype(BF16)
    rest = values - high.astype(F32)
    middle = rest.astype(BF16)
    return high, middle, (rest - middle.astype(F32)).astype(BF16)


def forward_kernel(
    tokens_ref, grad_ref, route_ref, source_ref, gain1_ref, bias1_ref, qkv_ref, offset_ref, relative_ref,
    mask_ref, out_weight_ref, out_bias_ref, gain2_ref, bias2_ref, router_ref,
    projected_ref, weights_ref, attended_ref, residual_ref, rows_ref, place_ref, aux_ref,
):
    image = pl.program_id(0)
    start, offset = image_span(image)
    source = source_ref[...]
    order = permutation(source, offset, SPAN)
    inputs = mm(order, tokens_ref[pl.ds(start, SPAN), :])
    upstream = mm(order, grad_ref[pl.ds(start, SPAN), :])

    plain = permutation(source, 0, FRAME)
    route = route_ref[0]
    route_cols = mm_nt(plain, route)
    route_rows = mm_nt(route, plain)
    chosen_col = route_cols[:, 0:1]
    slot_col = route_cols[:, 1:2]
    place_row = jnp.where(
        route_rows[1:2] > 0.5, route_rows[0:1] * SLOTS + route_rows[1:2] - 1.0, -1.0
    )
    place_ref[0] = jnp.broadcast_to(place_row, (8, FRAME)).astype(jnp.int32)
    place_col = jnp.where(slot_col > 0.5, chosen_col * SLOTS + slot_col - 1.0, -1.0)

    hat, _ = normalize(inputs)
    normed = (hat * gain1_ref[...] + bias1_ref[...]).astype(BF16)
    projected_ref[...] = (mm(normed, qkv_ref[...]) + offset_ref[...]).astype(BF16)

    for window in range(4):
        rows = slice(window * ROWS, (window + 1) * ROWS)
        for group in range(GROUPS):
            cols = slice(group * LANES, (group + 1) * LANES)
            wide = slice(group * WIDE, (group + 1) * WIDE)
            queries = projected_ref[rows, group * LANES : (group + 1) * LANES]
            keys = projected_ref[rows, D + group * LANES : D + (group + 1) * LANES]
            values = projected_ref[rows, 2 * D + group * LANES : 2 * D + (group + 1) * LANES]
            scores = mm_nt(keys, spread_heads(queries)) * SCALE
            scores = scores + relative_ref[:, wide] + mask_ref[window]
            powers = jnp.exp(scores - jnp.max(scores, axis=0, keepdims=True))
            weights = (powers / jnp.sum(powers, axis=0, keepdims=True)).astype(BF16)
            place = (window * GROUPS + group) * ROWS
            weights_ref[place : place + ROWS, :] = weights
            attended_ref[rows, cols] = pick_heads(mm_tn(weights, values)).astype(BF16)

    residual = inputs + (mm(attended_ref[...], out_weight_ref[...]) + out_bias_ref[...])
    residual_ref[...] = residual
    hat, _ = normalize(residual)
    normed = (hat * gain2_ref[...] + bias2_ref[...]).astype(BF16)
    logits = sum(mm(normed, part) for part in split_three(router_ref[...]))
    logits = jnp.exp(logits - jnp.max(logits, axis=-1, keepdims=True))
    probs = logits / jnp.sum(logits, axis=-1, keepdims=True)
    experts = lax.broadcasted_iota(jnp.int32, (FRAME, EXPERTS), 1).astype(F32)
    gate = jnp.sum(jnp.where(experts == chosen_col, probs, 0.0), axis=-1, keepdims=True)
    rows_ref[:, :D] = normed
    rows_ref[:, D:] = (gate * upstream).astype(BF16)
    aux_ref[:, 0:EXPERTS] = probs
    aux_ref[:, EXPERTS : EXPERTS + 1] = gate
    aux_ref[:, EXPERTS + 1 : EXPERTS + 2] = place_col
    aux_ref[:, EXPERTS + 2 : EXPERTS + 3] = chosen_col


def dispatch_kernel(place_ref, rows_ref, out_ref):
    expert = pl.program_id(0)
    images = place_ref.shape[0]
    places = jnp.concatenate([place_ref[i, 0:1, :] for i in range(images)], axis=1)
    slots = lax.broadcasted_iota(jnp.int32, (SLOTS, places.shape[1]), 0) + expert * SLOTS
    hot = jnp.where(slots == places, 1.0, 0.0).astype(BF16)
    out_ref[0] = mm(hot, rows_ref[...]).astype(BF16)


TILE = 512


def expert_kernel(
    rows_ref, up_ref, up_bias_ref, down_ref, down_bias_ref,
    back_ref, chunks_ref, biases_ref, up_sum, down_sum, up_bias_sum, down_bias_sum,
):
    member = pl.program_id(1)
    last = pl.num_programs(1) - 1

    @pl.when(member == 0)
    def _():
        up_sum[...] = jnp.zeros_like(up_sum)
        down_sum[...] = jnp.zeros_like(down_sum)
        up_bias_sum[...] = jnp.zeros_like(up_bias_sum)
        down_bias_sum[...] = jnp.zeros_like(down_bias_sum)

    inputs = rows_ref[0, 0, :, :D]
    grads = rows_ref[0, 0, :, D:]
    inputs_t = inputs.T
    grads_t = grads.T
    outs = jnp.zeros((SLOTS, D), F32)
    backs = jnp.zeros((SLOTS, D), F32)
    for tile in range(FF // TILE):
        at = slice(tile * TILE, (tile + 1) * TILE)
        pre = mm(inputs, up_ref[0, :, at]) + up_bias_ref[0, :, at]
        grad_hidden = mm_nt(grads, down_ref[0, at, :])
        share = 0.5 + 0.5 * lax.erf(pre * 0.7071067811865476)
        density = jnp.exp(pre * pre * -0.5) * 0.3989422804014327
        hidden = (pre * share).astype(BF16)
        grad_pre = (grad_hidden * (share + pre * density)).astype(BF16)
        outs += mm(hidden, down_ref[0, at, :])
        backs += mm_nt(grad_pre, up_ref[0, :, at])
        down_sum[:, at] += mm(grads_t, hidden)
        up_sum[:, at] += mm(inputs_t, grad_pre)
        up_bias_sum[:, at] += jnp.sum(grad_pre.astype(F32), axis=0, keepdims=True)
    down_bias_sum[...] += jnp.sum(grads.astype(F32), axis=0, keepdims=True)
    back_ref[0, 0, :, :D] = (outs + down_bias_ref[0]).astype(BF16)
    back_ref[0, 0, :, D:] = backs.astype(BF16)

    @pl.when(member == last)
    def _():
        for tile in range(FF // D):
            at = slice(tile * D, (tile + 1) * D)
            chunks_ref[0, at, :] = up_sum[:, at].astype(BF16)
            chunks_ref[1, at, :] = down_sum[:, at].T.astype(BF16)
            biases_ref[tile : tile + 1, :] = up_bias_sum[:, at]
        biases_ref[FF // D : FF // D + 1, :] = down_bias_sum[...]
        biases_ref[FF // D + 1 :, :] = jnp.zeros((7 - FF // D, D), F32)


def backward_kernel(
    tokens_ref, grad_ref, source_ref, gain1_ref, bias1_ref, qkv_ref, out_weight_ref, gain2_ref, bias2_ref,
    router_ref, projected_ref, weights_ref, attended_ref, residual_ref, aux_ref, returned_ref,
    output_ref, grad_tokens_ref, shared_ref, totals_ref, small_ref, grad_projected, grad_qkv, grad_out,
):
    image = pl.program_id(0)

    @pl.when(image == 0)
    def _():
        for ref in (output_ref, grad_tokens_ref, grad_qkv, grad_out, totals_ref, small_ref):
            ref[...] = jnp.zeros_like(ref)

    start, offset = image_span(image)
    order = permutation(source_ref[...], offset, SPAN)
    inputs = mm(order, tokens_ref[pl.ds(start, SPAN), :])
    upstream = mm(order, grad_ref[pl.ds(start, SPAN), :])
    residual = residual_ref[...]
    aux = aux_ref[...]
    probs = aux[:, 0:EXPERTS]
    gate = aux[:, EXPERTS : EXPERTS + 1]
    place = aux[:, EXPERTS + 1 : EXPERTS + 2].astype(jnp.int32)
    chosen = aux[:, EXPERTS + 2 : EXPERTS + 3]

    slots = lax.broadcasted_iota(jnp.int32, (FRAME, EXPERTS * SLOTS), 1)
    hot = jnp.where(slots == place, 1.0, 0.0).astype(BF16)
    gathered = mm(hot, returned_ref[...])
    combined = gathered[:, :D]
    output = (residual + gate * combined).astype(BF16)
    output_ref[pl.ds(start, SPAN), :] += mm_tn(order, output).astype(BF16)

    hat2, inverse2 = normalize(residual)
    normed2 = (hat2 * gain2_ref[...] + bias2_ref[...]).astype(BF16)
    gate_grad = jnp.sum(upstream * combined, axis=-1, keepdims=True)
    experts = lax.broadcasted_iota(jnp.int32, (FRAME, EXPERTS), 1).astype(F32)
    grad_logits = gate_grad * gate * (jnp.where(experts == chosen, 1.0, 0.0) - probs)
    logits_high, logits_low, _ = split_three(grad_logits)
    small_ref[8:16, :] += mm_tn(logits_high, normed2) + mm_tn(logits_low, normed2)
    router_high, router_low, _ = split_three(router_ref[...])
    grad_normed = (
        gathered[:, D:]
        + mm_nt(logits_high, router_high)
        + mm_nt(logits_low, router_high)
        + mm_nt(logits_high, router_low)
    )
    small_ref[0:1, :] += jnp.sum(grad_normed * hat2, axis=0, keepdims=True)
    small_ref[1:2, :] += jnp.sum(grad_normed, axis=0, keepdims=True)
    grad_residual = upstream + normalize_pull(grad_normed, hat2, inverse2, gain2_ref[...])
    mixed = grad_residual.astype(BF16)
    grad_out[...] += mm_tn(attended_ref[...], mixed)
    small_ref[2:3, :] += jnp.sum(mixed.astype(F32), axis=0, keepdims=True)
    grad_attended = mm_nt(mixed, out_weight_ref[...]).astype(BF16)

    for window in range(4):
        rows = slice(window * ROWS, (window + 1) * ROWS)
        for group in range(GROUPS):
            cols = slice(group * LANES, (group + 1) * LANES)
            wide = slice(group * WIDE, (group + 1) * WIDE)
            key_cols = slice(D + group * LANES, D + (group + 1) * LANES)
            value_cols = slice(2 * D + group * LANES, 2 * D + (group + 1) * LANES)
            keys = projected_ref[rows, key_cols]
            values = projected_ref[rows, value_cols]
            spread_queries = spread_heads(projected_ref[rows, cols])
            spread_grads = spread_heads(grad_attended[rows, cols])
            at = (window * GROUPS + group) * ROWS
            weights = weights_ref[at : at + ROWS, :]
            exact = weights.astype(F32)
            grad_weights = mm_nt(values, spread_grads)
            grad_scores = exact * (grad_weights - jnp.sum(exact * grad_weights, axis=0, keepdims=True))
            grad_scores = grad_scores.astype(BF16)
            totals_ref[:, wide] += grad_scores.astype(F32)
            grad_projected[rows, value_cols] = mm(weights, spread_grads).astype(BF16)
            grad_projected[rows, key_cols] = (mm(grad_scores, spread_queries) * SCALE).astype(BF16)
            grad_projected[rows, cols] = (pick_heads(mm_tn(grad_scores, keys)) * SCALE).astype(BF16)

    grads = grad_projected[...]
    hat1, inverse1 = normalize(inputs)
    normed1 = (hat1 * gain1_ref[...] + bias1_ref[...]).astype(BF16)
    grad_qkv[...] += mm_tn(normed1, grads)
    column_sums = jnp.sum(grads.astype(F32), axis=0, keepdims=True)
    for third in range(3):
        small_ref[5 + third : 6 + third, :] += column_sums[:, third * D : (third + 1) * D]
    grad_normed = mm_nt(grads, qkv_ref[...])
    small_ref[3:4, :] += jnp.sum(grad_normed * hat1, axis=0, keepdims=True)
    small_ref[4:5, :] += jnp.sum(grad_normed, axis=0, keepdims=True)
    grad_inputs = grad_residual + normalize_pull(grad_normed, hat1, inverse1, gain1_ref[...])
    high, low, _ = split_three(grad_inputs)
    grad_tokens_ref[pl.ds(start, SPAN), :] += mm_tn(order, high) + mm_tn(order, low)

    @pl.when(image == pl.num_programs(0) - 1)
    def _():
        for third in range(3):
            at = slice(third * D, (third + 1) * D)
            shared_ref[at, :] = grad_qkv[:, at].astype(BF16)
        shared_ref[3 * D :, :] = grad_out[...].astype(BF16)


CHUNK = 4 * D
STEP = 48
MESH = pl.DeviceIdType.MESH


def add_rows(left, left_at, right, right_at, out, out_at, count):
    def body(i, carry):
        here = i * STEP
        total = left[pl.ds(pl.multiple_of(left_at + here, 16), STEP), :].astype(F32)
        total = total + right[pl.ds(pl.multiple_of(right_at + here, 16), STEP), :].astype(F32)
        out[pl.ds(pl.multiple_of(out_at + here, 16), STEP), :] = total.astype(out.dtype)
        return carry

    lax.fori_loop(0, count // STEP, body, 0)


def partner(axis, stride):
    index = lax.axis_index(axis)
    bit = lax.rem(lax.div(index, stride), 2)
    return bit, {axis: index + stride - 2 * stride * bit}


class Halving:
    def __init__(self, source, out, work, landing, sends, recvs, bits):
        self.source, self.out, self.work, self.landing = source, out, work, landing
        self.sends, self.recvs, self.bits = sends, recvs, bits
        self.sizes = []
        size = CHUNK
        for _ in bits:
            halved = size % 32 == 0 and (size // 2) % STEP == 0
            size = size // 2 if halved else size
            self.sizes.append((size, halved))
        self.spreads = [k for k in reversed(range(len(bits))) if self.sizes[k][1]]
        self.steps = len(bits) + len(self.spreads)

    @staticmethod
    def landing_rows(count):
        rows, size = 0, CHUNK
        for _ in range(count):
            halved = size % 32 == 0 and (size // 2) % STEP == 0
            size = size // 2 if halved else size
            rows += size
        return rows

    def start(self, step):
        count = len(self.bits)
        if step == 0:
            self.at, self.start_row, self.land = 0, 0, 0
            self.held = []
        if step < count:
            size, halved = self.sizes[step]
            bit, device = partner(*self.bits[step])
            mine = self.source if step == 0 else self.work
            if halved:
                give, self.keep = self.at + (1 - bit) * size, self.at + bit * size
                self.start_row = self.start_row + bit * size
            else:
                give = self.keep = self.at
            self.held.append((self.start_row, size))
            copy = pltpu.make_async_remote_copy(
                src_ref=mine.at[pl.ds(pl.multiple_of(give, 16), size)],
                dst_ref=self.landing.at[pl.ds(self.land, size)],
                send_sem=self.sends.at[step], recv_sem=self.recvs.at[step], device_id=device, device_id_type=MESH,
            )
        else:
            stage = self.spreads[step - count]
            _, device = partner(*self.bits[stage])
            start, size = self.held[stage]
            rows = pl.ds(pl.multiple_of(start, 16), size)
            copy = pltpu.make_async_remote_copy(
                src_ref=self.out.at[rows], dst_ref=self.out.at[rows],
                send_sem=self.sends.at[step], recv_sem=self.recvs.at[step], device_id=device, device_id_type=MESH,
            )
        copy.start()
        self.copy = copy

    def finish(self, step):
        self.copy.wait()
        count = len(self.bits)
        if step >= count:
            return
        size, halved = self.sizes[step]
        mine = self.source if step == 0 else self.work
        if step == count - 1:
            add_rows(mine, self.keep, self.landing, self.land, self.out, self.start_row, size)
        elif step == 0:
            add_rows(mine, self.keep, self.landing, self.land, self.work, 0, size)
            self.at = 0
        else:
            add_rows(mine, self.keep, self.landing, self.land, self.work, self.keep, size)
            self.at = self.keep
        self.land += size


class Doubling:
    def __init__(self, source, out, landing, sends, recvs, bits):
        self.source, self.out, self.landing = source, out, landing
        self.sends, self.recvs, self.bits = sends, recvs, bits
        self.steps = len(bits)

    def start(self, step):
        if step == 0:
            self.out[...] = self.source[...]
        _, device = partner(*self.bits[step])
        self.copy = pltpu.make_async_remote_copy(
            src_ref=self.out, dst_ref=self.landing.at[step],
            send_sem=self.sends.at[step], recv_sem=self.recvs.at[step], device_id=device, device_id_type=MESH,
        )
        self.copy.start()

    def finish(self, step):
        self.copy.wait()
        self.out[...] = self.out[...] + self.landing[step]


def strides(size):
    return [2**k for k in range(size.bit_length() - 1)]


def copy_bits(copies):
    low = len(strides(copies)) // 2
    all_bits = [("dp", s) for s in strides(copies)]
    return all_bits, all_bits[low : low + 1] + all_bits[:low] + all_bits[low + 1 :]


def greet(bits):
    barrier = pltpu.get_barrier_semaphore()
    for bit in bits:
        pl.semaphore_signal(barrier, inc=1, device_id=partner(*bit)[1], device_id_type=MESH)
    pl.semaphore_wait(barrier, len(bits))


def reduce_kernel(
    copies, members, chunks_ref, biases_ref, shared_ref, small_ref,
    chunks_out, biases_out, shared_out, small_out,
    work, shared_work, landing, shared_landing, bias_landing, small_landing,
    chunk_sends, chunk_recvs, shared_sends, shared_recvs, bias_sends, bias_recvs, small_sends, small_recvs,
):
    first, second = copy_bits(copies)
    member_bits = [("expert", s) for s in strides(members)]
    everyone = member_bits + first
    greet(everyone)
    streams = [
        Doubling(small_ref, small_out, small_landing, small_sends, small_recvs, everyone),
        Halving(shared_ref, shared_out, shared_work, shared_landing, shared_sends, shared_recvs, everyone),
        Doubling(biases_ref, biases_out, bias_landing, bias_sends, bias_recvs, first),
    ]
    for c in range(chunks_ref.shape[0]):
        streams.append(
            Halving(
                chunks_ref.at[c], chunks_out.at[c], work.at[c], landing.at[c], chunk_sends.at[c], chunk_recvs.at[c],
                second if c % 4 == 3 else first,
            )
        )
    run(streams)


def run(streams):
    at = [0] * len(streams)
    for stream in streams:
        stream.start(0)
    while any(a < s.steps for a, s in zip(at, streams)):
        for i, stream in enumerate(streams):
            if at[i] < stream.steps:
                stream.finish(at[i])
                at[i] += 1
                if at[i] < stream.steps:
                    stream.start(at[i])


def whole(shape):
    return pl.BlockSpec(shape, lambda *_: (0,) * len(shape))


def per_image(rows, columns):
    return pl.BlockSpec((rows, columns), lambda i: (i, 0))


def shards(
    tokens, ln1_gain, ln1_bias, qkv_weight, q_bias, v_bias, bias_table, out_weight, out_bias, ln2_gain, ln2_bias,
    router_weight, up_weight, up_bias, down_weight, down_bias, expert_of, slot_of, grad_output,
):
    members = lax.axis_size("expert")
    local = up_weight.shape[0]
    count = tokens.shape[0]
    images = count // IMAGE
    framed = images * FRAME
    params = pltpu.CompilerParams(dimension_semantics=("arbitrary",), vmem_limit_bytes=60 * 2**20)

    source = jnp.asarray(source_cells())
    masks = jnp.asarray(window_masks())
    hot = jnp.asarray(offset_onehot())
    relative = jnp.dot(bias_table.T, hot, precision=HIGHEST).reshape(HEADS, ROWS, ROWS)
    relative = relative.transpose(1, 0, 2).reshape(ROWS, HEADS * ROWS)
    offset = jnp.concatenate([q_bias, jnp.zeros_like(q_bias), v_bias])[None]
    route = jnp.stack([expert_of, slot_of + 1]).astype(BF16).reshape(2, images, IMAGE).transpose(1, 0, 2)
    route = jnp.pad(route, ((0, 0), (0, 6), (0, FRAME - IMAGE)))
    row = lambda v: v[None]

    projected, weights, attended, residual, rows, place, aux = pl.pallas_call(
        forward_kernel,
        grid=(images,),
        in_specs=[
            whole((count, D)), whole((count, D)), pl.BlockSpec((1, 8, FRAME), lambda i: (i, 0, 0)),
            whole((FRAME, 1)), whole((1, D)), whole((1, D)), whole((D, 3 * D)), whole((1, 3 * D)),
            whole((ROWS, HEADS * ROWS)), whole((4, ROWS, WIDE)), whole((D, D)), whole((1, D)), whole((1, D)),
            whole((1, D)), whole((D, EXPERTS)),
        ],
        out_specs=[
            per_image(FRAME, 3 * D), per_image(4 * GROUPS * ROWS, WIDE), per_image(FRAME, D), per_image(FRAME, D),
            per_image(FRAME, 2 * D), pl.BlockSpec((1, 8, FRAME), lambda i: (i, 0, 0)), per_image(FRAME, 128),
        ],
        out_shape=[
            jax.ShapeDtypeStruct((framed, 3 * D), BF16),
            jax.ShapeDtypeStruct((images * 4 * GROUPS * ROWS, WIDE), BF16),
            jax.ShapeDtypeStruct((framed, D), BF16),
            jax.ShapeDtypeStruct((framed, D), F32),
            jax.ShapeDtypeStruct((framed, 2 * D), BF16),
            jax.ShapeDtypeStruct((images, 8, FRAME), jnp.int32),
            jax.ShapeDtypeStruct((framed, 128), F32),
        ],
        compiler_params=params,
        name="forward",
    )(
        tokens, grad_output, route, source, row(ln1_gain), row(ln1_bias), qkv_weight, offset, relative, masks,
        out_weight, row(out_bias), row(ln2_gain), row(ln2_bias), router_weight,
    )

    sending = pl.pallas_call(
        dispatch_kernel,
        grid=(EXPERTS,),
        in_specs=[whole((images, 8, FRAME)), whole((framed, 2 * D))],
        out_specs=pl.BlockSpec((1, SLOTS, 2 * D), lambda e: (e, 0, 0)),
        out_shape=jax.ShapeDtypeStruct((EXPERTS, SLOTS, 2 * D), BF16),
        compiler_params=params,
        name="dispatch",
    )(place, rows)

    arrived = lax.all_to_all(
        sending.reshape(members, local, SLOTS, 2 * D), "expert", split_axis=0, concat_axis=0, tiled=True
    )
    per_block = pl.BlockSpec((1, 1, SLOTS, 2 * D), lambda j, m: (m, j, 0, 0))

    def per_expert(*shape):
        return pl.BlockSpec((1, *shape), lambda j, m: (j, 0, 0))

    back, chunks, biases = pl.pallas_call(
        expert_kernel,
        grid=(local, members),
        in_specs=[per_block, per_expert(D, FF), per_expert(1, FF), per_expert(FF, D), per_expert(1, D)],
        out_specs=[
            per_block,
            pl.BlockSpec((2, CHUNK, D), lambda j, m: (j, 0, 0)),
            pl.BlockSpec((8, D), lambda j, m: (j, 0)),
        ],
        out_shape=[
            jax.ShapeDtypeStruct((members, local, SLOTS, 2 * D), BF16),
            jax.ShapeDtypeStruct((2 * local, CHUNK, D), BF16),
            jax.ShapeDtypeStruct((8 * local, D), F32),
        ],
        scratch_shapes=[
            pltpu.VMEM((D, FF), F32), pltpu.VMEM((D, FF), F32), pltpu.VMEM((1, FF), F32), pltpu.VMEM((1, D), F32),
        ],
        compiler_params=pltpu.CompilerParams(
            dimension_semantics=("arbitrary", "arbitrary"), vmem_limit_bytes=60 * 2**20
        ),
        name="experts",
    )(arrived, up_weight, up_bias[:, None], down_weight, down_bias[:, None])

    returned = lax.all_to_all(back, "expert", split_axis=0, concat_axis=0, tiled=True)
    returned = returned.reshape(EXPERTS * SLOTS, 2 * D)

    output, grad_tokens, shared, totals, small = pl.pallas_call(
        backward_kernel,
        grid=(images,),
        in_specs=[
            whole((count, D)), whole((count, D)), whole((FRAME, 1)), whole((1, D)), whole((1, D)),
            whole((D, 3 * D)), whole((D, D)), whole((1, D)), whole((1, D)), whole((D, EXPERTS)),
            per_image(FRAME, 3 * D), per_image(4 * GROUPS * ROWS, WIDE), per_image(FRAME, D), per_image(FRAME, D),
            per_image(FRAME, 128), whole((EXPERTS * SLOTS, 2 * D)),
        ],
        out_specs=[
            whole((count, D)), whole((count, D)), whole((CHUNK, D)), whole((ROWS, HEADS * ROWS)), whole((16, D)),
        ],
        out_shape=[
            jax.ShapeDtypeStruct((count, D), BF16),
            jax.ShapeDtypeStruct((count, D), F32),
            jax.ShapeDtypeStruct((CHUNK, D), BF16),
            jax.ShapeDtypeStruct((ROWS, HEADS * ROWS), F32),
            jax.ShapeDtypeStruct((16, D), F32),
        ],
        scratch_shapes=[pltpu.VMEM((FRAME, 3 * D), BF16), pltpu.VMEM((D, 3 * D), F32), pltpu.VMEM((D, D), F32)],
        compiler_params=params,
        name="backward",
    )(
        tokens, grad_output, source, row(ln1_gain), row(ln1_bias), qkv_weight, out_weight, row(ln2_gain),
        row(ln2_bias), router_weight, projected, weights, attended, residual, aux, returned,
    )

    totals = totals.reshape(ROWS, HEADS, ROWS).transpose(1, 0, 2).reshape(HEADS, ROWS * ROWS)
    grad_table = lax.dot_general(totals, hot, (((1,), (1,)), ((), ())), precision=HIGHEST)
    small = jnp.concatenate([small, jnp.pad(grad_table, ((0, 16 - HEADS), (0, D - TABLE)))])

    copies = lax.axis_size("dp")
    depth = len(strides(copies))
    total = depth + len(strides(members))
    rows_in = Halving.landing_rows
    vmem = pl.BlockSpec(memory_space=pltpu.VMEM)
    dma = pltpu.SemaphoreType.DMA
    chunks, biases, shared, small = pl.pallas_call(
        partial(reduce_kernel, copies, members),
        in_specs=[vmem] * 4,
        out_specs=[vmem] * 4,
        out_shape=[jax.ShapeDtypeStruct(a.shape, a.dtype) for a in (chunks, biases, shared, small)],
        scratch_shapes=[
            pltpu.VMEM((2 * local, CHUNK // 2, D), BF16),
            pltpu.VMEM((CHUNK // 2, D), BF16),
            pltpu.VMEM((2 * local, rows_in(depth), D), BF16),
            pltpu.VMEM((rows_in(total), D), BF16),
            pltpu.VMEM((depth, *biases.shape), F32),
            pltpu.VMEM((total, *small.shape), F32),
            dma((2 * local, 2 * depth)), dma((2 * local, 2 * depth)), dma((2 * total,)), dma((2 * total,)),
            dma((depth,)), dma((depth,)), dma((total,)), dma((total,)),
        ],
        compiler_params=pltpu.CompilerParams(
            collective_id=1, has_side_effects=True, vmem_limit_bytes=60 * 2**20
        ),
        name="reduce",
    )(chunks, biases, shared, small)

    def tiles(chunk):
        return chunk.reshape(-1, D, D).transpose(1, 0, 2).reshape(D, -1)

    chunks = chunks.reshape(local, 2, CHUNK, D).astype(F32)
    biases = biases.reshape(local, 8, D)
    grad_up = chunks[:, 0].reshape(local, FF // D, D, D).transpose(0, 2, 1, 3).reshape(local, D, FF)
    shared = shared.astype(F32)
    return (
        output,
        grad_tokens,
        small[3],
        small[4],
        tiles(shared[: 3 * D]),
        small[5],
        small[7],
        small[16 : 16 + HEADS, :TABLE].T,
        shared[3 * D :],
        small[2],
        small[0],
        small[1],
        small[8:16].T,
        grad_up,
        biases[:, : FF // D].reshape(local, FF),
        chunks[:, 1],
        biases[:, FF // D],
    )


def solution(mesh):
    tokens = P(("dp", "expert"), None)
    expert = P("expert", None, None)
    expert_bias = P("expert", None)
    routes = P(("dp", "expert"))
    return jax.shard_map(
        shards,
        mesh=mesh,
        in_specs=(
            tokens, P(), P(), P(), P(), P(), P(), P(), P(), P(), P(), P(), expert, expert_bias, expert, expert_bias,
            routes, routes, tokens,
        ),
        out_specs=(
            tokens, tokens, P(), P(), P(), P(), P(), P(), P(), P(), P(), P(), P(), expert, expert_bias, expert,
            expert_bias,
        ),
        check_vma=False,
    )
```

```python
from functools import partial

import jax
import jax.numpy as jnp
import numpy as np
from jax import lax
from jax.experimental import pallas as pl
from jax.experimental.pallas import tpu as pltpu
from jax.sharding import PartitionSpec as P

D = 384
HEADS = 12
HEAD = 32
FF = 1536
EXPERTS = 8
WINDOW = 7
SIDE = 14
SHIFT = 3
CAP = 245
CELLS = WINDOW * WINDOW
IMAGE = SIDE * SIDE
TABLE = (2 * WINDOW - 1) ** 2

ROWS = 64
SLOTS = 256
FRAME = 4 * ROWS
SPAN = 208
GROUP = 4
GROUPS = HEADS // GROUP
LANES = GROUP * HEAD
WIDE = GROUP * ROWS

EPSILON = 1e-05
MASK_NEG = -100.0
SCALE = HEAD ** (-0.5)
HIGHEST = lax.Precision.HIGHEST
F32 = jnp.float32
BF16 = jnp.bfloat16


def source_cells():
    source = np.full((FRAME, 1), -1000, np.int32)
    for row in range(FRAME):
        window, cell = divmod(row, ROWS)
        if cell < CELLS:
            down = (window // 2) * WINDOW + cell // WINDOW
            across = (window % 2) * WINDOW + cell % WINDOW
            source[row, 0] = ((down + SHIFT) % SIDE) * SIDE + (across + SHIFT) % SIDE
    return source


def window_masks():
    places = np.arange(SIDE)
    bands = (places >= SIDE - WINDOW).astype(np.int32) + (places >= SIDE - SHIFT)
    masks = np.zeros((4, ROWS, ROWS), np.float32)
    for window in range(4):
        rows = bands[(window // 2) * WINDOW : (window // 2 + 1) * WINDOW]
        cols = bands[(window % 2) * WINDOW : (window % 2 + 1) * WINDOW]
        labels = (rows[:, None] * 3 + cols[None, :]).reshape(-1)
        masks[window, :CELLS, :CELLS] = np.where(labels[:, None] != labels[None, :], MASK_NEG, 0.0)
    masks[:, CELLS:, :] = -1e30
    return np.tile(masks, (1, 1, GROUP))


def offset_onehot():
    hot = np.zeros((TABLE, ROWS, ROWS), np.float32)
    for q in range(CELLS):
        for p in range(CELLS):
            entry = (p // WINDOW - q // WINDOW + WINDOW - 1) * (2 * WINDOW - 1)
            entry += p % WINDOW - q % WINDOW + WINDOW - 1
            hot[entry, q, p] = 1.0
    return hot.reshape(TABLE, ROWS * ROWS)


def mm(left, right):
    return jnp.dot(left, right, preferred_element_type=F32)


def mm_nt(left, right):
    return lax.dot_general(left, right, (((1,), (1,)), ((), ())), preferred_element_type=F32)


def mm_tn(left, right):
    return lax.dot_general(left, right, (((0,), (0,)), ((), ())), preferred_element_type=F32)


def permutation(source, offset, width):
    places = lax.broadcasted_iota(jnp.int32, (FRAME, width), 1)
    return jnp.where(source + offset == places, 1.0, 0.0).astype(BF16)


def normalize(values):
    center = values - jnp.mean(values, axis=-1, keepdims=True)
    inverse = lax.rsqrt(jnp.mean(center * center, axis=-1, keepdims=True) + EPSILON)
    return center * inverse, inverse


def normalize_pull(grad, hat, inverse, gain):
    scaled = grad * gain
    first = jnp.mean(scaled, axis=-1, keepdims=True)
    second = jnp.mean(scaled * hat, axis=-1, keepdims=True)
    return (scaled - first - hat * second) * inverse


def spread_heads(block):
    heads = lax.broadcasted_iota(jnp.int32, block.shape, 1) // HEAD
    return jnp.concatenate(
        [jnp.where(heads == h, block, jnp.zeros_like(block)) for h in range(GROUP)], axis=0
    )


def pick_heads(wide):
    heads = lax.broadcasted_iota(jnp.int32, (ROWS, LANES), 1) // HEAD
    picked = wide[:ROWS]
    for h in range(1, GROUP):
        picked = jnp.where(heads == h, wide[h * ROWS : (h + 1) * ROWS], picked)
    return picked


def image_span(image):
    offset = lax.rem(image * (IMAGE % 16), 16)
    return pl.multiple_of(image * IMAGE - offset, 16), offset


def split_three(values):
    high = values.astype(BF16)
    rest = values - high.astype(F32)
    middle = rest.astype(BF16)
    return high, middle, (rest - middle.astype(F32)).astype(BF16)


VECTORS = ("ln1_gain", "ln1_bias", "q_bias", "k_bias", "v_bias", "out_bias", "ln2_gain", "ln2_bias")


def vector(ref, name):
    row = VECTORS.index(name)
    return ref[row : row + 1, :]


def forward_kernel(
    tokens_ref, grad_ref, route_ref, source_ref, vectors_ref, qkv_ref, relative_ref, mask_ref, out_weight_ref, router_ref,
    projected_ref, weights_ref, attended_ref, residual_ref, rows_ref, place_ref, aux_ref,
):
    image = pl.program_id(0)
    start, offset = image_span(image)
    source = source_ref[...]
    order = permutation(source, offset, SPAN)
    inputs = mm(order, tokens_ref[pl.ds(start, SPAN), :])
    upstream = mm(order, grad_ref[pl.ds(start, SPAN), :])

    plain = permutation(source, 0, FRAME)
    route = route_ref[0]
    route_cols = mm_nt(plain, route)
    route_rows = mm_nt(route, plain)
    chosen_col = route_cols[:, 0:1]
    slot_col = route_cols[:, 1:2]
    place_row = jnp.where(
        route_rows[1:2] > 0.5, route_rows[0:1] * SLOTS + route_rows[1:2] - 1.0, -1.0
    )
    place_ref[0] = jnp.broadcast_to(place_row, (8, FRAME)).astype(jnp.int32)
    place_col = jnp.where(slot_col > 0.5, chosen_col * SLOTS + slot_col - 1.0, -1.0)

    hat, _ = normalize(inputs)
    normed = (hat * vector(vectors_ref, "ln1_gain") + vector(vectors_ref, "ln1_bias")).astype(BF16)
    for third, name in enumerate(("q_bias", "k_bias", "v_bias")):
        at = slice(third * D, (third + 1) * D)
        projected_ref[:, at] = (mm(normed, qkv_ref[:, at]) + vector(vectors_ref, name)).astype(BF16)

    for window in range(4):
        rows = slice(window * ROWS, (window + 1) * ROWS)
        for group in range(GROUPS):
            cols = slice(group * LANES, (group + 1) * LANES)
            wide = slice(group * WIDE, (group + 1) * WIDE)
            queries = projected_ref[rows, group * LANES : (group + 1) * LANES]
            keys = projected_ref[rows, D + group * LANES : D + (group + 1) * LANES]
            values = projected_ref[rows, 2 * D + group * LANES : 2 * D + (group + 1) * LANES]
            scores = mm_nt(keys, spread_heads(queries)) * SCALE
            scores = scores + relative_ref[:, wide] + mask_ref[window]
            powers = jnp.exp(scores - jnp.max(scores, axis=0, keepdims=True))
            weights = (powers / jnp.sum(powers, axis=0, keepdims=True)).astype(BF16)
            place = (window * GROUPS + group) * ROWS
            weights_ref[place : place + ROWS, :] = weights
            attended_ref[rows, cols] = pick_heads(mm_tn(weights, values)).astype(BF16)

    residual = inputs + (mm(attended_ref[...], out_weight_ref[...]) + vector(vectors_ref, "out_bias"))
    residual_ref[...] = residual
    hat, _ = normalize(residual)
    normed = (hat * vector(vectors_ref, "ln2_gain") + vector(vectors_ref, "ln2_bias")).astype(BF16)
    logits = sum(mm_nt(normed, part) for part in split_three(router_ref[...]))
    logits = jnp.exp(logits - jnp.max(logits, axis=-1, keepdims=True))
    probs = logits / jnp.sum(logits, axis=-1, keepdims=True)
    experts = lax.broadcasted_iota(jnp.int32, (FRAME, EXPERTS), 1).astype(F32)
    gate = jnp.sum(jnp.where(experts == chosen_col, probs, 0.0), axis=-1, keepdims=True)
    rows_ref[:, :D] = normed
    rows_ref[:, D:] = (gate * upstream).astype(BF16)
    aux_ref[:, 0:EXPERTS] = probs
    aux_ref[:, EXPERTS : EXPERTS + 1] = gate
    aux_ref[:, EXPERTS + 1 : EXPERTS + 2] = place_col
    aux_ref[:, EXPERTS + 2 : EXPERTS + 3] = chosen_col


def backward_kernel(
    copies, members, tokens_ref, grad_ref, source_ref, vectors_ref, qkv_ref, out_weight_ref, router_ref, hot_ref,
    projected_ref, weights_ref, attended_ref, residual_ref, aux_ref, returned_ref, shards_ref,
    output_ref, grad_tokens_ref, chunks_ref, shared_ref, small_ref,
    grad_projected, grad_qkv, grad_out, totals, flat, shared, small, work, landing, shard, small_landing,
    chunks, shared_sum, small_sum,
    chunk_sends, chunk_recvs, scatter_sends, scatter_recvs, gather_sends, gather_recvs, small_sends, small_recvs, writes,
):
    image = pl.program_id(0)
    images = IMAGES
    everyone = [("expert", s) for s in strides(members)] + copy_bits(copies)[0]
    gathers = [
        Gather(shards_ref.at[c], chunks.at[c], CHUNK, chunk_sends.at[c], chunk_recvs.at[c], bits)
        for c, bits in enumerate(chunk_bits(copies, shards_ref.shape[0]))
    ]

    @pl.when(image == 0)
    def _():
        greet([partner(*bit)[1] for bit in everyone])
        for ref in (output_ref, grad_tokens_ref, grad_qkv, grad_out, totals, small):
            ref[...] = jnp.zeros_like(ref)

    def pieces(boundary):
        due = []
        for c, gather in enumerate(gathers):
            step = boundary - c
            if 0 < step < gather.steps:
                due.append(partial(gather.finish, step - 1))
            if 0 <= step < gather.steps:
                due.append(partial(gather.start, step))
        return due

    for boundary in range(images):
        if due := pieces(boundary):

            @pl.when(image == boundary)
            def _(due=due):
                for piece in due:
                    piece()

    start, offset = image_span(image)
    order = permutation(source_ref[...], offset, SPAN)
    inputs = mm(order, tokens_ref[pl.ds(start, SPAN), :])
    upstream = mm(order, grad_ref[pl.ds(start, SPAN), :])
    residual = residual_ref[...]
    aux = aux_ref[...]
    probs = aux[:, 0:EXPERTS]
    gate = aux[:, EXPERTS : EXPERTS + 1]
    place = aux[:, EXPERTS + 1 : EXPERTS + 2].astype(jnp.int32)
    chosen = aux[:, EXPERTS + 2 : EXPERTS + 3]

    slots = lax.broadcasted_iota(jnp.int32, (FRAME, EXPERTS * SLOTS), 1)
    hot = jnp.where(slots == place, 1.0, 0.0).astype(BF16)
    gathered = mm(hot, returned_ref[...])
    combined = gathered[:, :D]
    output = (residual + gate * combined).astype(BF16)
    output_ref[pl.ds(start, SPAN), :] += mm_tn(order, output).astype(BF16)

    hat2, inverse2 = normalize(residual)
    normed2 = (hat2 * vector(vectors_ref, "ln2_gain") + vector(vectors_ref, "ln2_bias")).astype(BF16)
    gate_grad = jnp.sum(upstream * combined, axis=-1, keepdims=True)
    experts = lax.broadcasted_iota(jnp.int32, (FRAME, EXPERTS), 1).astype(F32)
    grad_logits = gate_grad * gate * (jnp.where(experts == chosen, 1.0, 0.0) - probs)
    logits_high, logits_low, _ = split_three(grad_logits)
    small[8:16, :] += mm_tn(logits_high, normed2) + mm_tn(logits_low, normed2)
    router_high, router_low, _ = split_three(router_ref[...])
    grad_normed = (
        gathered[:, D:]
        + mm(logits_high, router_high)
        + mm(logits_low, router_high)
        + mm(logits_high, router_low)
    )
    small[0:1, :] += jnp.sum(grad_normed * hat2, axis=0, keepdims=True)
    small[1:2, :] += jnp.sum(grad_normed, axis=0, keepdims=True)
    grad_residual = upstream + normalize_pull(grad_normed, hat2, inverse2, vector(vectors_ref, "ln2_gain"))
    mixed = grad_residual.astype(BF16)
    grad_out[...] += mm_tn(attended_ref[...], mixed)
    small[2:3, :] += jnp.sum(mixed.astype(F32), axis=0, keepdims=True)
    grad_attended = mm_nt(mixed, out_weight_ref[...]).astype(BF16)

    for window in range(4):
        rows = slice(window * ROWS, (window + 1) * ROWS)
        for group in range(GROUPS):
            cols = slice(group * LANES, (group + 1) * LANES)
            wide = slice(group * WIDE, (group + 1) * WIDE)
            key_cols = slice(D + group * LANES, D + (group + 1) * LANES)
            value_cols = slice(2 * D + group * LANES, 2 * D + (group + 1) * LANES)
            keys = projected_ref[rows, key_cols]
            values = projected_ref[rows, value_cols]
            spread_queries = spread_heads(projected_ref[rows, cols])
            spread_grads = spread_heads(grad_attended[rows, cols])
            at = (window * GROUPS + group) * ROWS
            weights = weights_ref[at : at + ROWS, :]
            exact = weights.astype(F32)
            grad_weights = mm_nt(values, spread_grads)
            grad_scores = exact * (grad_weights - jnp.sum(exact * grad_weights, axis=0, keepdims=True))
            grad_scores = grad_scores.astype(BF16)
            totals[:, wide] += grad_scores.astype(F32)
            grad_projected[rows, value_cols] = mm(weights, spread_grads).astype(BF16)
            grad_projected[rows, key_cols] = (mm(grad_scores, spread_queries) * SCALE).astype(BF16)
            grad_projected[rows, cols] = (pick_heads(mm_tn(grad_scores, keys)) * SCALE).astype(BF16)

    grads = grad_projected[...]
    hat1, inverse1 = normalize(inputs)
    normed1 = (hat1 * vector(vectors_ref, "ln1_gain") + vector(vectors_ref, "ln1_bias")).astype(BF16)
    grad_qkv[...] += mm_tn(normed1, grads)
    column_sums = jnp.sum(grads.astype(F32), axis=0, keepdims=True)
    for third in range(3):
        small[5 + third : 6 + third, :] += column_sums[:, third * D : (third + 1) * D]
    grad_normed = mm_nt(grads, qkv_ref[...])
    small[3:4, :] += jnp.sum(grad_normed * hat1, axis=0, keepdims=True)
    small[4:5, :] += jnp.sum(grad_normed, axis=0, keepdims=True)
    grad_inputs = grad_residual + normalize_pull(grad_normed, hat1, inverse1, vector(vectors_ref, "ln1_gain"))
    high, low, _ = split_three(grad_inputs)
    grad_tokens_ref[pl.ds(start, SPAN), :] += mm_tn(order, high) + mm_tn(order, low)

    @pl.when(image == images - 1)
    def _():
        for third in range(3):
            at = slice(third * D, (third + 1) * D)
            shared[at, :] = grad_qkv[:, at].astype(BF16)
        shared[3 * D :, :] = grad_out[...].astype(BF16)
        flat[...] = jnp.zeros_like(flat)
        for q in range(CELLS):
            for h in range(HEADS):
                flat[h : h + 1, q * ROWS : (q + 1) * ROWS] = totals[q : q + 1, h * ROWS : (h + 1) * ROWS]
        small[16:32, :] = jnp.zeros((16, D), F32)
        table = sum(mm_nt(part, hot_ref[...]) for part in split_three(flat[...]))
        small[16:32, : table.shape[1]] = table

        for gather in gathers:
            for step in range(min(gather.steps, max(0, images - gathers.index(gather))), gather.steps):
                gather.finish(step - 1)
                gather.start(step)
        streams = [Doubling(small, small_sum, small_landing, small_sends, small_recvs, everyone)]
        rest = everyone[1:]
        for part in range(PARTS):
            turn = part * len(rest) // PARTS
            bits = everyone[:1] + rest[turn:] + rest[:turn]
            rows = pl.ds(part * PART, PART)
            scatter = Scatter(
                shared.at[rows], shard.at[part], PART, work.at[part], landing.at[part],
                scatter_sends.at[part], scatter_recvs.at[part], bits,
            )
            gather = Gather(
                shard.at[part], shared_sum.at[rows], PART, gather_sends.at[part], gather_recvs.at[part], bits
            )
            streams.append(Chain(scatter, gather))
        run(streams)
        small_ref[...] = small_sum[...]
        copies_out = [pltpu.make_async_copy(shared_sum, shared_ref, writes.at[len(gathers)])]
        copies_out[0].start()
        for c, gather in enumerate(gathers):
            gather.finish(gather.steps - 1)
            copies_out.append(pltpu.make_async_copy(chunks.at[c], chunks_ref.at[c], writes.at[c]))
            copies_out[-1].start()
        for copy in copies_out:
            copy.wait()


IMAGES = 8
CHUNK = 4 * D
PARTS = 3
PART = CHUNK // PARTS
STEP = 16
MESH = pl.DeviceIdType.MESH


def add_rows(left, left_at, right, right_at, out, out_at, count):
    step = next(s for s in (64, 48, 32, 16) if count % s == 0)

    def body(i, carry):
        here = i * step
        total = left[pl.ds(pl.multiple_of(left_at + here, 16), step), :].astype(F32)
        total = total + right[pl.ds(pl.multiple_of(right_at + here, 16), step), :].astype(F32)
        out[pl.ds(pl.multiple_of(out_at + here, 16), step), :] = total.astype(out.dtype)
        return carry

    lax.fori_loop(0, count // step, body, 0)


def partner(axis, stride):
    index = lax.axis_index(axis)
    bit = lax.rem(lax.div(index, stride), 2)
    return bit, {axis: index + stride - 2 * stride * bit}


def halvings(rows, count):
    sizes = []
    for _ in range(count):
        halved = rows % 32 == 0
        rows = rows // 2 if halved else rows
        sizes.append((rows, halved))
    return sizes


def landing_rows(rows, count):
    return sum(size for size, _ in halvings(rows, count))


def exchange(src, dst, sends, recvs, step, device):
    return pltpu.make_async_remote_copy(
        src_ref=src, dst_ref=dst, send_sem=sends.at[step], recv_sem=recvs.at[step], device_id=device, device_id_type=MESH
    )


def rows_at(ref, start, size):
    return ref.at[pl.ds(pl.multiple_of(start, 16), size)]


class Scatter:
    def __init__(self, source, out, rows, work, landing, sends, recvs, bits):
        self.source, self.out, self.work, self.landing = source, out, work, landing
        self.sends, self.recvs, self.bits = sends, recvs, bits
        self.steps = len(bits)
        self.plan = []
        at = land = 0
        for bit, (size, halved) in zip(bits, halvings(rows, len(bits))):
            b, device = partner(*bit)
            give, keep = (at + (1 - b) * size, at + b * size) if halved else (at, at)
            self.plan.append((give, keep, land, size, device))
            at = 0 if not self.plan[1:] else keep
            land += size

    def copy(self, step):
        give, _, land, size, device = self.plan[step]
        mine = self.work if step else self.source
        return exchange(
            rows_at(mine, give, size), self.landing.at[pl.ds(land, size)], self.sends, self.recvs, step, device
        )

    def start(self, step):
        self.copy(step).start()

    def finish(self, step):
        self.copy(step).wait()
        _, keep, land, size, _ = self.plan[step]
        mine = self.work if step else self.source
        if step == self.steps - 1:
            add_rows(mine, keep, self.landing, land, self.out, 0, size)
        else:
            add_rows(mine, keep, self.landing, land, self.work, keep if step else 0, size)


class Gather:
    def __init__(self, share, out, rows, sends, recvs, bits):
        self.share, self.out, self.sends, self.recvs = share, out, sends, recvs
        self.plan = []
        start = 0
        for bit, (size, halved) in zip(bits, halvings(rows, len(bits))):
            b, device = partner(*bit)
            start = start + b * size if halved else start
            if halved:
                self.plan.insert(0, (start, size, device))
        self.steps = len(self.plan)

    def copy(self, step):
        start, size, device = self.plan[step]
        return exchange(
            rows_at(self.out, start, size), rows_at(self.out, start, size), self.sends, self.recvs, step, device
        )

    def start(self, step):
        if step == 0:
            start, size, _ = self.plan[0]
            self.out[pl.ds(pl.multiple_of(start, 16), size), :] = self.share[...]
        self.copy(step).start()

    def finish(self, step):
        self.copy(step).wait()


class Chain:
    def __init__(self, first, second):
        self.first, self.second, self.steps = first, second, first.steps + second.steps

    def of(self, step):
        return (self.first, step) if step < self.first.steps else (self.second, step - self.first.steps)

    def start(self, step):
        stream, step = self.of(step)
        stream.start(step)

    def finish(self, step):
        stream, step = self.of(step)
        stream.finish(step)


class Doubling:
    def __init__(self, source, out, landing, sends, recvs, bits):
        self.source, self.out, self.landing = source, out, landing
        self.sends, self.recvs, self.bits = sends, recvs, bits
        self.steps = len(bits)

    def copy(self, step):
        device = partner(*self.bits[step])[1]
        return exchange(self.out, self.landing.at[step], self.sends, self.recvs, step, device)

    def start(self, step):
        if step == 0:
            self.out[...] = self.source[...]
        self.copy(step).start()

    def finish(self, step):
        self.copy(step).wait()
        self.out[...] = self.out[...] + self.landing[step]


def run(streams, begun=()):
    at = [0] * len(streams)
    for stream in streams:
        if stream not in begun:
            stream.start(0)
    while any(a < s.steps for a, s in zip(at, streams)):
        for i, stream in enumerate(streams):
            if at[i] < stream.steps:
                stream.finish(at[i])
                at[i] += 1
                if at[i] < stream.steps:
                    stream.start(at[i])


def strides(size):
    return [2**k for k in range(size.bit_length() - 1)]


def copy_bits(copies):
    low = len(strides(copies)) // 2
    all_bits = [("dp", s) for s in strides(copies)]
    return all_bits, all_bits[low : low + 1] + all_bits[:low] + all_bits[low + 1 :]


def chunk_bits(copies, count):
    first, second = copy_bits(copies)
    return [second if c % 4 == 1 else first for c in range(count)]


def greet(devices):
    barrier = pltpu.get_barrier_semaphore()
    for device in devices:
        pl.semaphore_signal(barrier, inc=1, device_id=device, device_id_type=MESH)
    pl.semaphore_wait(barrier, len(devices))


def member_at(members, hop, sign):
    index = lax.axis_index("expert")
    chips = members // 2
    chip = lax.rem(lax.div(index, 2) + sign * (hop // 2) + chips, chips)
    return chip * 2 + lax.rem(lax.rem(index, 2) + hop % 2, 2)


TILE = 512


def experts_kernel(
    copies, members, local, place_ref, rows_ref, up_ref, up_bias_ref, down_ref, down_bias_ref,
    returned_ref, shards_ref, biases_ref,
    outbox, inbox, results, up_sum, down_sum, up_bias_sum, down_bias_sum, chunks, biases, work, landing, bias_landing,
    out_sends, out_recvs, back_sends, back_recvs, chunk_sends, chunk_recvs, bias_sends, bias_recvs,
):
    me = lax.axis_index("expert")
    bits = chunk_bits(copies, 2 * local)
    greet(
        [{"expert": member_at(members, hop, 1)} for hop in range(1, members)]
        + [partner(*bit)[1] for bit in copy_bits(copies)[0]]
    )
    places = jnp.concatenate([place_ref[i, 0:1, :] for i in range(place_ref.shape[0])], axis=1)

    def out_copy(hop, j):
        return pltpu.make_async_remote_copy(
            src_ref=outbox.at[j, hop], dst_ref=inbox.at[j, hop],
            send_sem=out_sends.at[j, hop], recv_sem=out_recvs.at[j, hop],
            device_id={"expert": member_at(members, hop, 1)}, device_id_type=MESH,
        )

    def back_copy(hop, j):
        return pltpu.make_async_remote_copy(
            src_ref=results.at[j, hop], dst_ref=returned_ref.at[me, j],
            send_sem=back_sends.at[j, hop], recv_sem=back_recvs.at[j, hop],
            device_id={"expert": member_at(members, hop, -1)}, device_id_type=MESH,
        )

    def dispatch(hop, j):
        expert = member_at(members, hop, 1) * local + j
        slots = lax.broadcasted_iota(jnp.int32, (SLOTS, places.shape[1]), 0) + expert * SLOTS
        hot = jnp.where(slots == places, 1.0, 0.0).astype(BF16)
        return mm(hot, rows_ref[...]).astype(BF16)

    order = [(hop, j) for j in range(local) for hop in range(members - 1, 1, -1)]
    order += [(hop, j) for j in range(local) for hop in (1, 0)]
    for hop, j in order:
        if hop:
            outbox[j, hop] = dispatch(hop, j)
            out_copy(hop, j).start()
        else:
            inbox[j, 0] = dispatch(0, j)

    up_sum[...] = jnp.zeros_like(up_sum)
    down_sum[...] = jnp.zeros_like(down_sum)
    up_bias_sum[...] = jnp.zeros_like(up_bias_sum)
    down_bias_sum[...] = jnp.zeros_like(down_bias_sum)

    def compute(pair, j):
        hops = (2 * pair, 2 * pair + 1)
        for hop in hops:
            if hop:
                out_copy(hop, j).wait_recv()
        inputs = inbox[j, 2 * pair : 2 * pair + 2, :, :D].reshape(2 * SLOTS, D)
        grads = inbox[j, 2 * pair : 2 * pair + 2, :, D:].reshape(2 * SLOTS, D)
        inputs_t = inputs.T
        grads_t = grads.T
        outs = jnp.zeros((2 * SLOTS, D), F32)
        backs = jnp.zeros((2 * SLOTS, D), F32)
        for tile in range(FF // TILE):
            at = slice(tile * TILE, (tile + 1) * TILE)
            pre = mm(inputs, up_ref[j, :, at]) + up_bias_ref[j : j + 1, at]
            grad_hidden = mm_nt(grads, down_ref[j, at, :])
            share = 0.5 + 0.5 * lax.erf(pre * 0.7071067811865476)
            density = jnp.exp(pre * pre * -0.5) * 0.3989422804014327
            hidden = (pre * share).astype(BF16)
            grad_pre = (grad_hidden * (share + pre * density)).astype(BF16)
            outs += mm(hidden, down_ref[j, at, :])
            backs += mm_nt(grad_pre, up_ref[j, :, at])
            down_sum[j, :, at] += mm(grads_t, hidden)
            up_sum[j, :, at] += mm(inputs_t, grad_pre)
            up_bias_sum[j : j + 1, at] += jnp.sum(grad_pre.astype(F32), axis=0, keepdims=True)
        down_bias_sum[j : j + 1, :] += jnp.sum(grads.astype(F32), axis=0, keepdims=True)
        results[j, 2 * pair : 2 * pair + 2, :, :D] = (
            (outs + down_bias_ref[j : j + 1, :]).astype(BF16).reshape(2, SLOTS, D)
        )
        results[j, 2 * pair : 2 * pair + 2, :, D:] = backs.astype(BF16).reshape(2, SLOTS, D)
        for hop in hops:
            if hop:
                back_copy(hop, j).start()
            else:
                returned_ref[me, j] = results[j, 0]

    def seal(j):
        for tile in range(FF // D):
            at = slice(tile * D, (tile + 1) * D)
            chunks[2 * j, at, :] = up_sum[j, :, at].astype(BF16)
            chunks[2 * j + 1, at, :] = down_sum[j, :, at].T.astype(BF16)
            biases[8 * j + tile : 8 * j + tile + 1, :] = up_bias_sum[j : j + 1, at]
        biases[8 * j + 4 : 8 * j + 5, :] = down_bias_sum[j : j + 1, :]
        biases[8 * j + 5 : 8 * j + 8, :] = jnp.zeros((3, D), F32)

    streams = [
        Scatter(
            chunks.at[c], shards_ref.at[c], CHUNK, work.at[c], landing.at[c], chunk_sends.at[c], chunk_recvs.at[c],
            bits[c],
        )
        for c in range(2 * local)
    ]
    for pair in range(members // 2):
        for j in range(local):
            compute(pair, j)
            if pair == members // 2 - 1:
                seal(j)
                for stream in streams[2 * j : 2 * j + 2]:
                    stream.start(0)
    small = Doubling(biases, biases_ref, bias_landing, bias_sends, bias_recvs, copy_bits(copies)[0])
    run([*streams, small], begun=streams)
    for j in range(local):
        for hop in range(1, members):
            out_copy(hop, j).wait_send()
            back_copy(hop, j).wait()


def finish_kernel(
    up_tile_ref, down_tile_ref, biases_ref, shared_ref, small_ref,
    up_ref, down_ref, up_bias_ref, down_bias_ref, qkv_ref, out_ref, router_ref, table_ref, *vector_refs,
):
    up_ref[0] = up_tile_ref[0].astype(F32)
    down_ref[0] = down_tile_ref[0].astype(F32)

    @pl.when((pl.program_id(0) == 0) & (pl.program_id(1) == 0))
    def _():
        for j in range(up_bias_ref.shape[0]):
            for tile in range(FF // D):
                row = 8 * j + tile
                up_bias_ref[j : j + 1, tile * D : (tile + 1) * D] = biases_ref[row : row + 1, :]
            down_bias_ref[j : j + 1, :] = biases_ref[8 * j + 4 : 8 * j + 5, :]
        for third in range(3):
            at = slice(third * D, (third + 1) * D)
            qkv_ref[:, at] = shared_ref[at, :].astype(F32)
        out_ref[...] = shared_ref[3 * D :, :].astype(F32)
        router_ref[...] = small_ref[8:16, :]
        table_ref[...] = small_ref[16 : 16 + HEADS, :TABLE]
        for ref, row in zip(vector_refs, (3, 4, 5, 7, 2, 0, 1)):
            ref[...] = small_ref[row, :]


def whole(shape):
    return pl.BlockSpec(shape, lambda *_: (0,) * len(shape))


def per_image(rows, columns):
    return pl.BlockSpec((rows, columns), lambda i: (i, 0))


def shards(
    tokens, ln1_gain, ln1_bias, qkv_weight, q_bias, v_bias, bias_table, out_weight, out_bias, ln2_gain, ln2_bias,
    router_weight, up_weight, up_bias, down_weight, down_bias, expert_of, slot_of, grad_output,
):
    members = lax.axis_size("expert")
    local = up_weight.shape[0]
    count = tokens.shape[0]
    images = count // IMAGE
    framed = images * FRAME
    params = pltpu.CompilerParams(dimension_semantics=("arbitrary",), vmem_limit_bytes=60 * 2**20)

    source = jnp.asarray(source_cells())
    masks = jnp.asarray(window_masks())
    hot = jnp.asarray(offset_onehot())
    relative = jnp.dot(bias_table.T, hot, precision=HIGHEST).reshape(HEADS, ROWS, ROWS)
    relative = relative.transpose(1, 0, 2).reshape(ROWS, HEADS * ROWS)
    route = jnp.stack([expert_of, slot_of + 1]).astype(BF16).reshape(2, images, IMAGE).transpose(1, 0, 2)
    route = jnp.pad(route, ((0, 0), (0, 6), (0, FRAME - IMAGE)))
    vectors = jnp.stack(
        [ln1_gain, ln1_bias, q_bias, jnp.zeros_like(q_bias), v_bias, out_bias, ln2_gain, ln2_bias]
    )
    router = router_weight.T
    vmem = pl.BlockSpec(memory_space=pltpu.VMEM)
    dma = pltpu.SemaphoreType.DMA

    projected, weights, attended, residual, rows, place, aux = pl.pallas_call(
        forward_kernel,
        grid=(images,),
        in_specs=[
            whole((count, D)), whole((count, D)), pl.BlockSpec((1, 8, FRAME), lambda i: (i, 0, 0)),
            whole((FRAME, 1)), whole((8, D)), whole((D, 3 * D)), whole((ROWS, HEADS * ROWS)),
            whole((4, ROWS, WIDE)), whole((D, D)), whole((EXPERTS, D)),
        ],
        out_specs=[
            per_image(FRAME, 3 * D), per_image(4 * GROUPS * ROWS, WIDE), per_image(FRAME, D), per_image(FRAME, D),
            per_image(FRAME, 2 * D), pl.BlockSpec((1, 8, FRAME), lambda i: (i, 0, 0)), per_image(FRAME, 128),
        ],
        out_shape=[
            jax.ShapeDtypeStruct((framed, 3 * D), BF16),
            jax.ShapeDtypeStruct((images * 4 * GROUPS * ROWS, WIDE), BF16),
            jax.ShapeDtypeStruct((framed, D), BF16),
            jax.ShapeDtypeStruct((framed, D), F32),
            jax.ShapeDtypeStruct((framed, 2 * D), BF16),
            jax.ShapeDtypeStruct((images, 8, FRAME), jnp.int32),
            jax.ShapeDtypeStruct((framed, 128), F32),
        ],
        compiler_params=params,
        name="forward",
    )(tokens, grad_output, route, source, vectors, qkv_weight, relative, masks, out_weight, router)

    copies = lax.axis_size("dp")
    depth = len(strides(copies))
    total = depth + len(strides(members))
    pieces = 2 * local
    share = halvings(CHUNK, depth)[-1][0]
    returned, shares, biases = pl.pallas_call(
        partial(experts_kernel, copies, members, local),
        in_specs=[vmem] * 6,
        out_specs=[vmem] * 3,
        out_shape=[
            jax.ShapeDtypeStruct((members, local, SLOTS, 2 * D), BF16),
            jax.ShapeDtypeStruct((pieces, share, D), BF16),
            jax.ShapeDtypeStruct((8 * local, D), F32),
        ],
        scratch_shapes=[
            pltpu.VMEM((local, members, SLOTS, 2 * D), BF16),
            pltpu.VMEM((local, members, SLOTS, 2 * D), BF16),
            pltpu.VMEM((local, members, SLOTS, 2 * D), BF16),
            pltpu.VMEM((local, D, FF), F32),
            pltpu.VMEM((local, D, FF), F32),
            pltpu.VMEM((local, FF), F32),
            pltpu.VMEM((local, D), F32),
            pltpu.VMEM((pieces, CHUNK, D), BF16),
            pltpu.VMEM((8 * local, D), F32),
            pltpu.VMEM((pieces, CHUNK // 2, D), BF16),
            pltpu.VMEM((pieces, landing_rows(CHUNK, depth), D), BF16),
            pltpu.VMEM((depth, 8 * local, D), F32),
            dma((local, members)), dma((local, members)), dma((local, members)), dma((local, members)),
            dma((pieces, depth)), dma((pieces, depth)), dma((depth,)), dma((depth,)),
        ],
        compiler_params=pltpu.CompilerParams(
            collective_id=1, has_side_effects=True, vmem_limit_bytes=60 * 2**20
        ),
        name="experts",
    )(place, rows, up_weight, up_bias, down_weight, down_bias)
    returned = returned.reshape(EXPERTS * SLOTS, 2 * D)

    output, grad_tokens, chunks, shared, small = pl.pallas_call(
        partial(backward_kernel, copies, members),
        grid=(images,),
        in_specs=[
            whole((count, D)), whole((count, D)), whole((FRAME, 1)), whole((8, D)), whole((D, 3 * D)), whole((D, D)),
            whole((EXPERTS, D)), whole((TABLE, ROWS * ROWS)),
            per_image(FRAME, 3 * D), per_image(4 * GROUPS * ROWS, WIDE), per_image(FRAME, D), per_image(FRAME, D),
            per_image(FRAME, 128), whole((EXPERTS * SLOTS, 2 * D)), whole((pieces, share, D)),
        ],
        out_specs=[
            whole((count, D)), whole((count, D)), pl.BlockSpec(memory_space=pl.ANY),
            pl.BlockSpec(memory_space=pl.ANY), whole((32, D)),
        ],
        out_shape=[
            jax.ShapeDtypeStruct((count, D), BF16),
            jax.ShapeDtypeStruct((count, D), F32),
            jax.ShapeDtypeStruct((pieces, CHUNK, D), BF16),
            jax.ShapeDtypeStruct((CHUNK, D), BF16),
            jax.ShapeDtypeStruct((32, D), F32),
        ],
        scratch_shapes=[
            pltpu.VMEM((FRAME, 3 * D), BF16), pltpu.VMEM((D, 3 * D), F32), pltpu.VMEM((D, D), F32),
            pltpu.VMEM((ROWS, HEADS * ROWS), F32),
            pltpu.VMEM((16, ROWS * ROWS), F32),
            pltpu.VMEM((CHUNK, D), BF16),
            pltpu.VMEM((32, D), F32),
            pltpu.VMEM((PARTS, PART // 2, D), BF16),
            pltpu.VMEM((PARTS, landing_rows(PART, total), D), BF16),
            pltpu.VMEM((PARTS, halvings(PART, total)[-1][0], D), BF16),
            pltpu.VMEM((total, 32, D), F32),
            pltpu.VMEM((pieces, CHUNK, D), BF16),
            pltpu.VMEM((CHUNK, D), BF16),
            pltpu.VMEM((32, D), F32),
            dma((pieces, depth)), dma((pieces, depth)), dma((PARTS, total)), dma((PARTS, total)),
            dma((PARTS, total)), dma((PARTS, total)), dma((total,)), dma((total,)), dma((pieces + 1,)),
        ],
        compiler_params=pltpu.CompilerParams(
            dimension_semantics=("arbitrary",), collective_id=2, has_side_effects=True, vmem_limit_bytes=60 * 2**20
        ),
        name="backward",
    )(
        tokens, grad_output, source, vectors, qkv_weight, out_weight, router, hot.astype(BF16), projected, weights,
        attended, residual, aux, returned, shares,
    )

    results = pl.pallas_call(
        finish_kernel,
        grid=(local, FF // D),
        in_specs=[
            pl.BlockSpec((1, D, D), lambda j, t: (2 * j, t, 0)), pl.BlockSpec((1, D, D), lambda j, t: (2 * j + 1, t, 0)),
            whole((8 * local, D)), whole((CHUNK, D)), whole((32, D)),
        ],
        out_specs=[
            pl.BlockSpec((1, D, D), lambda j, t: (j, 0, t)), pl.BlockSpec((1, D, D), lambda j, t: (j, t, 0)),
            whole((local, FF)), whole((local, D)), whole((D, 3 * D)), whole((D, D)), whole((EXPERTS, D)),
            whole((HEADS, TABLE)), *[whole((D,))] * 7,
        ],
        out_shape=[
            jax.ShapeDtypeStruct(shape, F32)
            for shape in (
                (local, D, FF), (local, FF, D), (local, FF), (local, D), (D, 3 * D), (D, D), (EXPERTS, D),
                (HEADS, TABLE), *[(D,)] * 7,
            )
        ],
        compiler_params=pltpu.CompilerParams(
            dimension_semantics=("arbitrary", "arbitrary"), vmem_limit_bytes=60 * 2**20
        ),
        name="finish",
    )(chunks, chunks, biases, shared, small)
    grad_up, grad_down, grad_up_bias, grad_down_bias, grad_qkv, grad_out, grad_router, grad_table = results[:8]
    grad_gain1, grad_bias1, grad_q, grad_v, grad_out_bias, grad_gain2, grad_bias2 = results[8:]
    return (
        output, grad_tokens, grad_gain1, grad_bias1, grad_qkv, grad_q, grad_v, grad_table.T, grad_out, grad_out_bias,
        grad_gain2, grad_bias2, grad_router.T, grad_up, grad_up_bias, grad_down, grad_down_bias,
    )


def solution(mesh):
    tokens = P(("dp", "expert"), None)
    expert = P("expert", None, None)
    expert_bias = P("expert", None)
    routes = P(("dp", "expert"))
    return jax.shard_map(
        shards,
        mesh=mesh,
        in_specs=(
            tokens, P(), P(), P(), P(), P(), P(), P(), P(), P(), P(), P(), expert, expert_bias, expert, expert_bias,
            routes, routes, tokens,
        ),
        out_specs=(
            tokens, tokens, P(), P(), P(), P(), P(), P(), P(), P(), P(), P(), P(), expert, expert_bias, expert,
            expert_bias,
        ),
        check_vma=False,
    )
```

```python
from functools import partial

import jax
import jax.numpy as jnp
import numpy as np
from jax import lax
from jax.experimental import pallas as pl
from jax.experimental.pallas import tpu as pltpu
from jax.sharding import PartitionSpec as P

D = 384
HEADS = 12
HEAD = 32
FF = 1536
EXPERTS = 8
WINDOW = 7
SIDE = 14
SHIFT = 3
CAP = 245
CELLS = WINDOW * WINDOW
IMAGE = SIDE * SIDE
TABLE = (2 * WINDOW - 1) ** 2

ROWS = 64
SLOTS = 256
FRAME = 4 * ROWS
SPAN = 208
GROUP = 4
GROUPS = HEADS // GROUP
LANES = GROUP * HEAD
WIDE = GROUP * ROWS

EPSILON = 1e-05
MASK_NEG = -100.0
SCALE = HEAD ** (-0.5)
HIGHEST = lax.Precision.HIGHEST
F32 = jnp.float32
BF16 = jnp.bfloat16


def source_cells():
    source = np.full((FRAME, 1), -1000, np.int32)
    for row in range(FRAME):
        window, cell = divmod(row, ROWS)
        if cell < CELLS:
            down = (window // 2) * WINDOW + cell // WINDOW
            across = (window % 2) * WINDOW + cell % WINDOW
            source[row, 0] = ((down + SHIFT) % SIDE) * SIDE + (across + SHIFT) % SIDE
    return source


def window_masks():
    places = np.arange(SIDE)
    bands = (places >= SIDE - WINDOW).astype(np.int32) + (places >= SIDE - SHIFT)
    masks = np.zeros((4, ROWS, ROWS), np.float32)
    for window in range(4):
        rows = bands[(window // 2) * WINDOW : (window // 2 + 1) * WINDOW]
        cols = bands[(window % 2) * WINDOW : (window % 2 + 1) * WINDOW]
        labels = (rows[:, None] * 3 + cols[None, :]).reshape(-1)
        masks[window, :CELLS, :CELLS] = np.where(labels[:, None] != labels[None, :], MASK_NEG, 0.0)
    masks[:, CELLS:, :] = -1e30
    return np.tile(masks, (1, 1, GROUP))


def offset_onehot():
    hot = np.zeros((TABLE, ROWS, ROWS), np.float32)
    for q in range(CELLS):
        for p in range(CELLS):
            entry = (p // WINDOW - q // WINDOW + WINDOW - 1) * (2 * WINDOW - 1)
            entry += p % WINDOW - q % WINDOW + WINDOW - 1
            hot[entry, q, p] = 1.0
    return hot.reshape(TABLE, ROWS * ROWS)


def mm(left, right):
    return jnp.dot(left, right, preferred_element_type=F32)


def mm_nt(left, right):
    return lax.dot_general(left, right, (((1,), (1,)), ((), ())), preferred_element_type=F32)


def mm_tn(left, right):
    return lax.dot_general(left, right, (((0,), (0,)), ((), ())), preferred_element_type=F32)


def permutation(source, offset, width):
    places = lax.broadcasted_iota(jnp.int32, (FRAME, width), 1)
    return jnp.where(source + offset == places, 1.0, 0.0).astype(BF16)


def normalize(values):
    center = values - jnp.mean(values, axis=-1, keepdims=True)
    inverse = lax.rsqrt(jnp.mean(center * center, axis=-1, keepdims=True) + EPSILON)
    return center * inverse, inverse


def normalize_pull(grad, hat, inverse, gain):
    scaled = grad * gain
    first = jnp.mean(scaled, axis=-1, keepdims=True)
    second = jnp.mean(scaled * hat, axis=-1, keepdims=True)
    return (scaled - first - hat * second) * inverse


def spread_heads(block):
    heads = lax.broadcasted_iota(jnp.int32, block.shape, 1) // HEAD
    return jnp.concatenate(
        [jnp.where(heads == h, block, jnp.zeros_like(block)) for h in range(GROUP)], axis=0
    )


def pick_heads(wide):
    heads = lax.broadcasted_iota(jnp.int32, (ROWS, LANES), 1) // HEAD
    picked = wide[:ROWS]
    for h in range(1, GROUP):
        picked = jnp.where(heads == h, wide[h * ROWS : (h + 1) * ROWS], picked)
    return picked


def image_span(image):
    offset = lax.rem(image * (IMAGE % 16), 16)
    return pl.multiple_of(image * IMAGE - offset, 16), offset


def split_three(values):
    high = values.astype(BF16)
    rest = values - high.astype(F32)
    middle = rest.astype(BF16)
    return high, middle, (rest - middle.astype(F32)).astype(BF16)


VECTORS = ("ln1_gain", "ln1_bias", "q_bias", "k_bias", "v_bias", "out_bias", "ln2_gain", "ln2_bias")


def vector(ref, name):
    row = VECTORS.index(name)
    return ref[row : row + 1, :]


PAIR = 2
SPREAD = PAIR * FRAME


def orders(step, source):
    found = []
    for k in range(PAIR):
        start, offset = image_span(step * PAIR + k)
        found.append((pl.ds(start, SPAN), permutation(source, offset, SPAN)))
    return found


def arranged(ref, order):
    return jnp.concatenate([mm(hot, ref[rows, :]) for rows, hot in order], axis=0)


def windows_of_step():
    return [(w % 4, slice(w * ROWS, (w + 1) * ROWS)) for w in range(4 * PAIR)]


def group_cols(third, group):
    return slice(third * D + group * LANES, third * D + (group + 1) * LANES)


def forward_kernel(
    tokens_ref, grad_ref, route_ref, source_ref, vectors_ref, qkv_ref, relative_ref, mask_ref, out_weight_ref, router_ref,
    projected_ref, weights_ref, attended_ref, residual_ref, rows_ref, place_ref, aux_ref,
):
    source = source_ref[...]
    order = orders(pl.program_id(0), source)
    inputs = arranged(tokens_ref, order)

    hat, _ = normalize(inputs)
    normed = (hat * vector(vectors_ref, "ln1_gain") + vector(vectors_ref, "ln1_bias")).astype(BF16)
    for third, name in enumerate(("q_bias", "k_bias", "v_bias")):
        at = slice(third * D, (third + 1) * D)
        projected_ref[:, at] = (mm(normed, qkv_ref[:, at]) + vector(vectors_ref, name)).astype(BF16)

    for index, (window, rows) in enumerate(windows_of_step()):
        scores = []
        for group in range(GROUPS):
            queries = projected_ref[rows, group_cols(0, group)]
            scores.append(mm_nt(projected_ref[rows, group_cols(1, group)], spread_heads(queries)))
        for group in range(GROUPS):
            wide = slice(group * WIDE, (group + 1) * WIDE)
            full = scores[group] * SCALE + (relative_ref[:, wide] + mask_ref[window])
            powers = jnp.exp(full - jnp.max(full, axis=0, keepdims=True))
            weights = (powers * (1.0 / jnp.sum(powers, axis=0, keepdims=True))).astype(BF16)
            place = (index * GROUPS + group) * ROWS
            weights_ref[place : place + ROWS, :] = weights
            mixed = mm_tn(weights, projected_ref[rows, group_cols(2, group)])
            attended_ref[rows, group_cols(0, group)] = pick_heads(mixed).astype(BF16)

    plain = permutation(source, 0, FRAME)
    chosen_cols, place_cols = [], []
    for k in range(PAIR):
        route = route_ref[k]
        cols = mm_nt(plain, route)
        rows = mm_nt(route, plain)
        place_row = jnp.where(rows[1:2] > 0.5, rows[0:1] * SLOTS + rows[1:2] - 1.0, -1.0)
        place_ref[k] = jnp.broadcast_to(place_row, (8, FRAME)).astype(jnp.int32)
        chosen_cols.append(cols[:, 0:1])
        place_cols.append(jnp.where(cols[:, 1:2] > 0.5, cols[:, 0:1] * SLOTS + cols[:, 1:2] - 1.0, -1.0))
    chosen = jnp.concatenate(chosen_cols, axis=0)

    residual = inputs + (mm(attended_ref[...], out_weight_ref[...]) + vector(vectors_ref, "out_bias"))
    residual_ref[...] = residual
    hat, _ = normalize(residual)
    normed = (hat * vector(vectors_ref, "ln2_gain") + vector(vectors_ref, "ln2_bias")).astype(BF16)
    logits = sum(mm_nt(normed, part) for part in split_three(router_ref[...]))
    logits = jnp.exp(logits - jnp.max(logits, axis=-1, keepdims=True))
    probs = logits / jnp.sum(logits, axis=-1, keepdims=True)
    experts = lax.broadcasted_iota(jnp.int32, (SPREAD, EXPERTS), 1).astype(F32)
    gate = jnp.sum(jnp.where(experts == chosen, probs, 0.0), axis=-1, keepdims=True)
    rows_ref[:, :D] = normed
    rows_ref[:, D:] = (gate * arranged(grad_ref, order)).astype(BF16)
    aux_ref[:, 0:EXPERTS] = probs
    aux_ref[:, EXPERTS : EXPERTS + 1] = gate
    aux_ref[:, EXPERTS + 1 : EXPERTS + 2] = jnp.concatenate(place_cols, axis=0)
    aux_ref[:, EXPERTS + 2 : EXPERTS + 3] = chosen


def backward_kernel(
    copies, members, local, tokens_ref, grad_ref, source_ref, vectors_ref, qkv_ref, out_weight_ref, router_ref, hot_ref,
    projected_ref, weights_ref, attended_ref, residual_ref, aux_ref, returned_ref, held_ref,
    output_ref, grad_tokens_ref, chunks_ref, shared_ref, small_ref,
    grad_projected, grad_attended, grad_residual, grad_qkv, grad_out, totals, flat, shared, small,
    work, landing, shard, small_landing, held, late_landing, shares, chunks, shared_sum, small_sum,
    chunk_sends, chunk_recvs, scatter_sends, scatter_recvs, gather_sends, gather_recvs, small_sends, small_recvs, writes,
):
    step = pl.program_id(0)
    steps = IMAGES // PAIR
    everyone = [("expert", s) for s in strides(members)] + copy_bits(copies)[0]
    gathers = []
    share = shares.shape[1]
    for c, bits in enumerate(chunk_bits(copies, 2 * local)):
        depth = len(bits)
        if c < 2 * (local - 1):
            semaphores = chunk_sends.at[c], chunk_recvs.at[c]
            gathers.append(Gather(held.at[c], chunks.at[c], CHUNK, *semaphores, bits, skip=1))
        else:
            last = chunk_sends.at[c, pl.ds(depth, 1)], chunk_recvs.at[c, pl.ds(depth, 1)]
            scatter = Scatter(held.at[c], shares.at[c], 2 * share, None, late_landing.at[c], *last, bits[-1:])
            semaphores = chunk_sends.at[c], chunk_recvs.at[c]
            gathers.append(Chain(scatter, Gather(shares.at[c], chunks.at[c], CHUNK, *semaphores, bits)))
    plan = {}
    for c, gather in enumerate(gathers):
        for stage, place in enumerate(PLACES.get(gather.steps, ())):
            plan.setdefault(place, []).append((c, stage))
    planned = [pair for pairs in plan.values() for pair in pairs]

    def advance(c, stage):
        if stage:
            gathers[c].finish(stage - 1)
        gathers[c].start(stage)

    def exchange_at(phase):
        for s in range(steps):
            if due := plan.get(s * PHASES + phase):

                @pl.when(step == s)
                def _(due=due):
                    for c, stage in due:
                        advance(c, stage)

    @pl.when(step == 0)
    def _():
        greet([partner(*bit)[1] for bit in everyone])
        for ref in (output_ref, grad_tokens_ref, grad_qkv, grad_out, totals, small):
            ref[...] = jnp.zeros_like(ref)
        held[...] = held_ref[...]

    exchange_at(0)
    order = orders(step, source_ref[...])
    upstream = arranged(grad_ref, order)
    residual = residual_ref[...]
    aux = aux_ref[...]
    probs = aux[:, 0:EXPERTS]
    gate = aux[:, EXPERTS : EXPERTS + 1]
    place = aux[:, EXPERTS + 1 : EXPERTS + 2].astype(jnp.int32)
    chosen = aux[:, EXPERTS + 2 : EXPERTS + 3]

    slots = lax.broadcasted_iota(jnp.int32, (SPREAD, EXPERTS * SLOTS), 1)
    hot = jnp.where(slots == place, 1.0, 0.0).astype(BF16)
    gathered = mm(hot, returned_ref[...])
    combined = gathered[:, :D]
    output = (residual + gate * combined).astype(BF16)
    for k, (rows, hot) in enumerate(order):
        output_ref[rows, :] += mm_tn(hot, output[k * FRAME : (k + 1) * FRAME]).astype(BF16)

    hat2, inverse2 = normalize(residual)
    normed2 = (hat2 * vector(vectors_ref, "ln2_gain") + vector(vectors_ref, "ln2_bias")).astype(BF16)
    gate_grad = jnp.sum(upstream * combined, axis=-1, keepdims=True)
    experts = lax.broadcasted_iota(jnp.int32, (SPREAD, EXPERTS), 1).astype(F32)
    grad_logits = gate_grad * gate * (jnp.where(experts == chosen, 1.0, 0.0) - probs)
    logits_high, logits_low, _ = split_three(grad_logits)
    small[8:16, :] += mm_tn(logits_high, normed2) + mm_tn(logits_low, normed2)
    router_high, router_low, _ = split_three(router_ref[...])
    grad_normed = (
        gathered[:, D:] + mm(logits_high, router_high) + mm(logits_low, router_high) + mm(logits_high, router_low)
    )
    small[0:1, :] += jnp.sum(grad_normed * hat2, axis=0, keepdims=True)
    small[1:2, :] += jnp.sum(grad_normed, axis=0, keepdims=True)
    grad_mixed = upstream + normalize_pull(grad_normed, hat2, inverse2, vector(vectors_ref, "ln2_gain"))
    grad_residual[...] = grad_mixed
    grad_mixed = grad_mixed.astype(BF16)
    grad_out[...] += mm_tn(attended_ref[...], grad_mixed)
    small[2:3, :] += jnp.sum(grad_mixed.astype(F32), axis=0, keepdims=True)
    grad_attended[...] = mm_nt(grad_mixed, out_weight_ref[...]).astype(BF16)

    exchange_at(1)
    for index, (_, rows) in enumerate(windows_of_step()):
        if index == 2 * PAIR:
            exchange_at(2)
        spread_grads = [spread_heads(grad_attended[rows, group_cols(0, g)]) for g in range(GROUPS)]
        grad_weights = [
            mm_nt(projected_ref[rows, group_cols(2, g)], spread_grads[g]) for g in range(GROUPS)
        ]
        for g in range(GROUPS):
            at = (index * GROUPS + g) * ROWS
            weights = weights_ref[at : at + ROWS, :]
            exact = weights.astype(F32)
            scores = exact * (grad_weights[g] - jnp.sum(exact * grad_weights[g], axis=0, keepdims=True))
            scores = scores.astype(BF16)
            totals[:, g * WIDE : (g + 1) * WIDE] += scores.astype(F32)
            grad_projected[rows, group_cols(2, g)] = mm(weights, spread_grads[g]).astype(BF16)
            grad_keys = mm(scores, spread_heads(projected_ref[rows, group_cols(0, g)]))
            grad_projected[rows, group_cols(1, g)] = (grad_keys * SCALE).astype(BF16)
            grad_queries = pick_heads(mm_tn(scores, projected_ref[rows, group_cols(1, g)]))
            grad_projected[rows, group_cols(0, g)] = (grad_queries * SCALE).astype(BF16)

    exchange_at(3)
    grads = grad_projected[...]
    order = orders(step, source_ref[...])
    hat1, inverse1 = normalize(arranged(tokens_ref, order))
    normed1 = (hat1 * vector(vectors_ref, "ln1_gain") + vector(vectors_ref, "ln1_bias")).astype(BF16)
    grad_qkv[...] += mm_tn(normed1, grads)
    column_sums = jnp.sum(grads.astype(F32), axis=0, keepdims=True)
    for third in range(3):
        small[5 + third : 6 + third, :] += column_sums[:, third * D : (third + 1) * D]
    grad_normed = mm_nt(grads, qkv_ref[...])
    small[3:4, :] += jnp.sum(grad_normed * hat1, axis=0, keepdims=True)
    small[4:5, :] += jnp.sum(grad_normed, axis=0, keepdims=True)
    grad_inputs = grad_residual[...] + normalize_pull(grad_normed, hat1, inverse1, vector(vectors_ref, "ln1_gain"))
    high, low, _ = split_three(grad_inputs)
    for k, (rows, hot) in enumerate(order):
        of_image = slice(k * FRAME, (k + 1) * FRAME)
        grad_tokens_ref[rows, :] += mm_tn(hot, high[of_image]) + mm_tn(hot, low[of_image])

    @pl.when(step == steps - 1)
    def _():
        for third in range(3):
            at = slice(third * D, (third + 1) * D)
            shared[at, :] = grad_qkv[:, at].astype(BF16)
        shared[3 * D :, :] = grad_out[...].astype(BF16)
        flat[...] = jnp.zeros_like(flat)
        for q in range(CELLS):
            for h in range(HEADS):
                flat[h : h + 1, q * ROWS : (q + 1) * ROWS] = totals[q : q + 1, h * ROWS : (h + 1) * ROWS]
        table = sum(mm_nt(part, hot_ref[...]) for part in split_three(flat[...]))
        small[16:32, : table.shape[1]] = table

        for c, gather in enumerate(gathers):
            for stage in range(gather.steps):
                if (c, stage) not in planned:
                    advance(c, stage)
        streams = [Doubling(small, small_sum, small_landing, small_sends, small_recvs, everyone)]
        rest = everyone[1:]
        for part in range(PARTS):
            turn = part * len(rest) // PARTS
            bits = everyone[:1] + rest[turn:] + rest[:turn]
            rows = pl.ds(part * PART, PART)
            scatter = Scatter(
                shared.at[rows], shard.at[part], PART, work.at[part], landing.at[part],
                scatter_sends.at[part], scatter_recvs.at[part], bits,
            )
            gather = Gather(
                shard.at[part], shared_sum.at[rows], PART, gather_sends.at[part], gather_recvs.at[part], bits
            )
            streams.append(Chain(scatter, gather))
        run(streams)
        small_ref[...] = small_sum[...]
        copies_out = [pltpu.make_async_copy(shared_sum, shared_ref, writes.at[len(gathers)])]
        copies_out[0].start()
        for c, gather in enumerate(gathers):
            gather.finish(gather.steps - 1)
            copies_out.append(pltpu.make_async_copy(chunks.at[c], chunks_ref.at[c], writes.at[c]))
            copies_out[-1].start()
        for copy in copies_out:
            copy.wait()


PHASES = 4


PLACES = {2: (0, 3), 4: (0, 5, 10, 13), 6: (0, 5, 8, 10, 12, 14)}


IMAGES = 8
CHUNK = 4 * D
PARTS = 3
PART = CHUNK // PARTS
STEP = 16
MESH = pl.DeviceIdType.MESH


def add_rows(left, left_at, right, right_at, out, out_at, count):
    step = next(s for s in (64, 48, 32, 16) if count % s == 0)

    def body(i, carry):
        here = i * step
        total = left[pl.ds(pl.multiple_of(left_at + here, 16), step), :].astype(F32)
        total = total + right[pl.ds(pl.multiple_of(right_at + here, 16), step), :].astype(F32)
        out[pl.ds(pl.multiple_of(out_at + here, 16), step), :] = total.astype(out.dtype)
        return carry

    lax.fori_loop(0, count // step, body, 0)


def partner(axis, stride):
    index = lax.axis_index(axis)
    bit = lax.rem(lax.div(index, stride), 2)
    return bit, {axis: index + stride - 2 * stride * bit}


def halvings(rows, count):
    sizes = []
    for _ in range(count):
        halved = rows % 32 == 0
        rows = rows // 2 if halved else rows
        sizes.append((rows, halved))
    return sizes


def landing_rows(rows, count):
    return sum(size for size, _ in halvings(rows, count))


def exchange(src, dst, sends, recvs, step, device):
    return pltpu.make_async_remote_copy(
        src_ref=src, dst_ref=dst, send_sem=sends.at[step], recv_sem=recvs.at[step], device_id=device, device_id_type=MESH
    )


def rows_at(ref, start, size):
    return ref.at[pl.ds(pl.multiple_of(start, 16), size)]


class Scatter:
    def __init__(self, source, out, rows, work, landing, sends, recvs, bits):
        self.source, self.out, self.work, self.landing = source, out, work, landing
        self.sends, self.recvs, self.bits = sends, recvs, bits
        self.steps = len(bits)
        self.plan = []
        at = land = 0
        for bit, (size, halved) in zip(bits, halvings(rows, len(bits))):
            b, device = partner(*bit)
            give, keep = (at + (1 - b) * size, at + b * size) if halved else (at, at)
            self.plan.append((give, keep, land, size, device))
            at = 0 if not self.plan[1:] else keep
            land += size

    def copy(self, step):
        give, _, land, size, device = self.plan[step]
        mine = self.work if step else self.source
        return exchange(
            rows_at(mine, give, size), self.landing.at[pl.ds(land, size)], self.sends, self.recvs, step, device
        )

    def start(self, step):
        self.copy(step).start()

    def finish(self, step):
        self.copy(step).wait()
        _, keep, land, size, _ = self.plan[step]
        mine = self.work if step else self.source
        if step == self.steps - 1:
            add_rows(mine, keep, self.landing, land, self.out, 0, size)
        else:
            add_rows(mine, keep, self.landing, land, self.work, keep if step else 0, size)


class Gather:
    def __init__(self, share, out, rows, sends, recvs, bits, skip=0):
        self.share, self.out, self.sends, self.recvs = share, out, sends, recvs
        self.plan = []
        start = 0
        for bit, (size, halved) in zip(bits, halvings(rows, len(bits))):
            b, device = partner(*bit)
            start = start + b * size if halved else start
            if halved:
                self.plan.insert(0, (start, size, device))
        self.plan = self.plan[skip:]
        self.steps = len(self.plan)

    def copy(self, step):
        start, size, device = self.plan[step]
        return exchange(
            rows_at(self.out, start, size), rows_at(self.out, start, size), self.sends, self.recvs, step, device
        )

    def start(self, step):
        if step == 0:
            start, size, _ = self.plan[0]
            self.out[pl.ds(pl.multiple_of(start, 16), size), :] = self.share[...]
        self.copy(step).start()

    def finish(self, step):
        self.copy(step).wait()


class Chain:
    def __init__(self, first, second):
        self.first, self.second, self.steps = first, second, first.steps + second.steps

    def of(self, step):
        return (self.first, step) if step < self.first.steps else (self.second, step - self.first.steps)

    def start(self, step):
        stream, step = self.of(step)
        stream.start(step)

    def finish(self, step):
        stream, step = self.of(step)
        stream.finish(step)


class Doubling:
    def __init__(self, source, out, landing, sends, recvs, bits):
        self.source, self.out, self.landing = source, out, landing
        self.sends, self.recvs, self.bits = sends, recvs, bits
        self.steps = len(bits)

    def copy(self, step):
        device = partner(*self.bits[step])[1]
        return exchange(self.out, self.landing.at[step], self.sends, self.recvs, step, device)

    def start(self, step):
        if step == 0:
            self.out[...] = self.source[...]
        self.copy(step).start()

    def finish(self, step):
        self.copy(step).wait()
        self.out[...] = self.out[...] + self.landing[step]


def run(streams, begun=(), order=()):
    at = dict.fromkeys(streams, 0)
    for stream in streams:
        if stream not in begun:
            stream.start(0)

    def advance(stream):
        if at[stream] < stream.steps:
            stream.finish(at[stream])
            at[stream] += 1
            if at[stream] < stream.steps:
                stream.start(at[stream])

    for stream in order:
        advance(stream)
    while any(at[s] < s.steps for s in streams):
        for stream in streams:
            advance(stream)


def strides(size):
    return [2**k for k in range(size.bit_length() - 1)]


def copy_bits(copies):
    low = len(strides(copies)) // 2
    all_bits = [("dp", s) for s in strides(copies)]
    return all_bits, all_bits[low : low + 1] + all_bits[:low] + all_bits[low + 1 :]


def chunk_bits(copies, count):
    first, second = copy_bits(copies)
    return [second if c % 2 else first for c in range(count)]


def greet(devices):
    barrier = pltpu.get_barrier_semaphore()
    for device in devices:
        pl.semaphore_signal(barrier, inc=1, device_id=device, device_id_type=MESH)
    pl.semaphore_wait(barrier, len(devices))


def member_at(members, hop, sign):
    index = lax.axis_index("expert")
    chips = members // 2
    chip = lax.rem(lax.div(index, 2) + sign * (hop // 2) + chips, chips)
    return chip * 2 + lax.rem(lax.rem(index, 2) + hop % 2, 2)


TILE = 512


def experts_kernel(
    copies, members, local, place_ref, rows_ref, up_ref, up_bias_ref, down_ref, down_bias_ref,
    returned_ref, held_ref, biases_ref,
    outbox, inbox, results, up_sum, down_sum, up_bias_sum, down_bias_sum, chunks, biases, work, landing, shares,
    bias_landing,
    out_sends, out_recvs, back_sends, back_recvs, chunk_sends, chunk_recvs, bias_sends, bias_recvs,
):
    me = lax.axis_index("expert")
    bits = chunk_bits(copies, 2 * local)
    greet(
        [{"expert": member_at(members, hop, 1)} for hop in range(1, members)]
        + [partner(*bit)[1] for bit in copy_bits(copies)[0]]
    )
    places = jnp.concatenate([place_ref[i, 0:1, :] for i in range(place_ref.shape[0])], axis=1)

    def out_copy(hop, j):
        return pltpu.make_async_remote_copy(
            src_ref=outbox.at[j, hop], dst_ref=inbox.at[j, hop],
            send_sem=out_sends.at[j, hop], recv_sem=out_recvs.at[j, hop],
            device_id={"expert": member_at(members, hop, 1)}, device_id_type=MESH,
        )

    def back_copy(hop, j):
        return pltpu.make_async_remote_copy(
            src_ref=results.at[j, hop], dst_ref=returned_ref.at[me, j],
            send_sem=back_sends.at[j, hop], recv_sem=back_recvs.at[j, hop],
            device_id={"expert": member_at(members, hop, -1)}, device_id_type=MESH,
        )

    def dispatch(hop, j):
        expert = member_at(members, hop, 1) * local + j
        slots = lax.broadcasted_iota(jnp.int32, (SLOTS, places.shape[1]), 0) + expert * SLOTS
        hot = jnp.where(slots == places, 1.0, 0.0).astype(BF16)
        return mm(hot, rows_ref[...]).astype(BF16)

    order = [(hop, j) for j in range(local) for hop in range(members - 1, 1, -1)]
    order += [(hop, j) for j in range(local) for hop in (1, 0)]
    for hop, j in order:
        if hop:
            outbox[j, hop] = dispatch(hop, j)
            out_copy(hop, j).start()
        else:
            inbox[j, 0] = dispatch(0, j)

    up_sum[...] = jnp.zeros_like(up_sum)
    down_sum[...] = jnp.zeros_like(down_sum)
    up_bias_sum[...] = jnp.zeros_like(up_bias_sum)
    down_bias_sum[...] = jnp.zeros_like(down_bias_sum)

    def compute(pair, j):
        hops = (2 * pair, 2 * pair + 1)
        for hop in hops:
            if hop:
                out_copy(hop, j).wait_recv()
        inputs = inbox[j, 2 * pair : 2 * pair + 2, :, :D].reshape(2 * SLOTS, D)
        grads = inbox[j, 2 * pair : 2 * pair + 2, :, D:].reshape(2 * SLOTS, D)
        inputs_t = inputs.T
        grads_t = grads.T
        outs = jnp.zeros((2 * SLOTS, D), F32)
        backs = jnp.zeros((2 * SLOTS, D), F32)
        for tile in range(FF // TILE):
            at = slice(tile * TILE, (tile + 1) * TILE)
            pre = mm(inputs, up_ref[j, :, at]) + up_bias_ref[j : j + 1, at]
            grad_hidden = mm_nt(grads, down_ref[j, at, :])
            share = 0.5 + 0.5 * lax.erf(pre * 0.7071067811865476)
            density = jnp.exp(pre * pre * -0.5) * 0.3989422804014327
            hidden = (pre * share).astype(BF16)
            grad_pre = (grad_hidden * (share + pre * density)).astype(BF16)
            outs += mm(hidden, down_ref[j, at, :])
            backs += mm_nt(grad_pre, up_ref[j, :, at])
            down_sum[j, :, at] += mm(grads_t, hidden)
            up_sum[j, :, at] += mm(inputs_t, grad_pre)
            up_bias_sum[j : j + 1, at] += jnp.sum(grad_pre.astype(F32), axis=0, keepdims=True)
        down_bias_sum[j : j + 1, :] += jnp.sum(grads.astype(F32), axis=0, keepdims=True)
        results[j, 2 * pair : 2 * pair + 2, :, :D] = (
            (outs + down_bias_ref[j : j + 1, :]).astype(BF16).reshape(2, SLOTS, D)
        )
        results[j, 2 * pair : 2 * pair + 2, :, D:] = backs.astype(BF16).reshape(2, SLOTS, D)
        for hop in hops:
            if hop:
                back_copy(hop, j).start()
            else:
                returned_ref[me, j] = results[j, 0]

    def seal(j):
        for tile in range(FF // D):
            at = slice(tile * D, (tile + 1) * D)
            chunks[2 * j, at, :] = up_sum[j, :, at].astype(BF16)
            chunks[2 * j + 1, at, :] = down_sum[j, :, at].T.astype(BF16)
            biases[8 * j + tile : 8 * j + tile + 1, :] = up_bias_sum[j : j + 1, at]
        biases[8 * j + 4 : 8 * j + 5, :] = down_bias_sum[j : j + 1, :]
        biases[8 * j + 5 : 8 * j + 8, :] = jnp.zeros((3, D), F32)

    streams = []
    for c in range(2 * local):
        early = c < 2 * (local - 1)
        parts = chunks.at[c], shares.at[c] if early else held_ref.at[c], CHUNK, work.at[c], landing.at[c]
        semaphores = chunk_sends.at[c], chunk_recvs.at[c]
        if early:
            depth, share = len(bits[c]), shares.shape[1]
            semaphores_back = chunk_sends.at[c, pl.ds(depth, 1)], chunk_recvs.at[c, pl.ds(depth, 1)]
            back = Gather(shares.at[c], held_ref.at[c], 2 * share, *semaphores_back, bits[c][-1:])
            streams.append(Chain(Scatter(*parts, *semaphores, bits[c]), back))
        else:
            streams.append(Scatter(*parts, *semaphores, bits[c][:-1]))
    for pair in range(members // 2):
        for j in range(local):
            compute(pair, j)
            if pair == members // 2 - 1:
                seal(j)
                for stream in streams[2 * j : 2 * j + 2]:
                    stream.start(0)
    small = Doubling(biases, biases_ref, bias_landing, bias_sends, bias_recvs, copy_bits(copies)[0])
    early, late = streams[: 2 * (local - 1)], [*streams[2 * (local - 1) :], small]
    run([*early, *late], begun=streams, order=early + early + late + early + late + early)
    for j in range(local):
        for hop in range(1, members):
            out_copy(hop, j).wait_send()
            back_copy(hop, j).wait()


def finish_kernel(
    up_tile_ref, down_tile_ref, biases_ref, shared_ref, small_ref,
    up_ref, down_ref, up_bias_ref, down_bias_ref, qkv_ref, out_ref, router_ref, table_ref, *vector_refs,
):
    up_ref[0] = up_tile_ref[0].astype(F32)
    down_ref[0] = down_tile_ref[0].astype(F32)

    @pl.when((pl.program_id(0) == 0) & (pl.program_id(1) == 0))
    def _():
        for j in range(up_bias_ref.shape[0]):
            for tile in range(FF // D):
                row = 8 * j + tile
                up_bias_ref[j : j + 1, tile * D : (tile + 1) * D] = biases_ref[row : row + 1, :]
            down_bias_ref[j : j + 1, :] = biases_ref[8 * j + 4 : 8 * j + 5, :]
        for third in range(3):
            at = slice(third * D, (third + 1) * D)
            qkv_ref[:, at] = shared_ref[at, :].astype(F32)
        out_ref[...] = shared_ref[3 * D :, :].astype(F32)
        router_ref[...] = small_ref[8:16, :]
        table_ref[...] = small_ref[16 : 16 + HEADS, :TABLE]
        for ref, row in zip(vector_refs, (3, 4, 5, 7, 2, 0, 1)):
            ref[...] = small_ref[row, :]


def whole(shape):
    return pl.BlockSpec(shape, lambda *_: (0,) * len(shape))


def per_step(rows, columns):
    return pl.BlockSpec((rows, columns), lambda i: (i, 0))


def shards(
    tokens, ln1_gain, ln1_bias, qkv_weight, q_bias, v_bias, bias_table, out_weight, out_bias, ln2_gain, ln2_bias,
    router_weight, up_weight, up_bias, down_weight, down_bias, expert_of, slot_of, grad_output,
):
    members = lax.axis_size("expert")
    local = up_weight.shape[0]
    count = tokens.shape[0]
    images = count // IMAGE
    framed = images * FRAME
    params = pltpu.CompilerParams(dimension_semantics=("arbitrary",), vmem_limit_bytes=60 * 2**20)

    source = jnp.asarray(source_cells())
    masks = jnp.asarray(window_masks())
    hot = jnp.asarray(offset_onehot())
    relative = jnp.dot(bias_table.T, hot, precision=HIGHEST).reshape(HEADS, ROWS, ROWS)
    relative = relative.transpose(1, 0, 2).reshape(ROWS, HEADS * ROWS)
    route = jnp.stack([expert_of, slot_of + 1]).astype(BF16).reshape(2, images, IMAGE).transpose(1, 0, 2)
    route = jnp.pad(route, ((0, 0), (0, 6), (0, FRAME - IMAGE)))
    vectors = jnp.stack(
        [ln1_gain, ln1_bias, q_bias, jnp.zeros_like(q_bias), v_bias, out_bias, ln2_gain, ln2_bias]
    )
    router = router_weight.T
    vmem = pl.BlockSpec(memory_space=pltpu.VMEM)
    dma = pltpu.SemaphoreType.DMA

    projected, weights, attended, residual, rows, place, aux = pl.pallas_call(
        forward_kernel,
        grid=(images // PAIR,),
        in_specs=[
            whole((count, D)), whole((count, D)), pl.BlockSpec((PAIR, 8, FRAME), lambda i: (i, 0, 0)),
            whole((FRAME, 1)), whole((8, D)), whole((D, 3 * D)), whole((ROWS, HEADS * ROWS)),
            whole((4, ROWS, WIDE)), whole((D, D)), whole((EXPERTS, D)),
        ],
        out_specs=[
            per_step(SPREAD, 3 * D), per_step(4 * PAIR * GROUPS * ROWS, WIDE), per_step(SPREAD, D), per_step(SPREAD, D),
            per_step(SPREAD, 2 * D), pl.BlockSpec((PAIR, 8, FRAME), lambda i: (i, 0, 0)), per_step(SPREAD, 128),
        ],
        out_shape=[
            jax.ShapeDtypeStruct((framed, 3 * D), BF16),
            jax.ShapeDtypeStruct((images * 4 * GROUPS * ROWS, WIDE), BF16),
            jax.ShapeDtypeStruct((framed, D), BF16),
            jax.ShapeDtypeStruct((framed, D), F32),
            jax.ShapeDtypeStruct((framed, 2 * D), BF16),
            jax.ShapeDtypeStruct((images, 8, FRAME), jnp.int32),
            jax.ShapeDtypeStruct((framed, 128), F32),
        ],
        compiler_params=params,
        name="forward",
    )(tokens, grad_output, route, source, vectors, qkv_weight, relative, masks, out_weight, router)

    copies = lax.axis_size("dp")
    depth = len(strides(copies))
    total = depth + len(strides(members))
    pieces = 2 * local
    share = halvings(CHUNK, depth)[-1][0]
    returned, held, biases = pl.pallas_call(
        partial(experts_kernel, copies, members, local),
        in_specs=[vmem] * 6,
        out_specs=[vmem] * 3,
        out_shape=[
            jax.ShapeDtypeStruct((members, local, SLOTS, 2 * D), BF16),
            jax.ShapeDtypeStruct((pieces, 2 * share, D), BF16),
            jax.ShapeDtypeStruct((8 * local, D), F32),
        ],
        scratch_shapes=[
            pltpu.VMEM((local, members, SLOTS, 2 * D), BF16),
            pltpu.VMEM((local, members, SLOTS, 2 * D), BF16),
            pltpu.VMEM((local, members, SLOTS, 2 * D), BF16),
            pltpu.VMEM((local, D, FF), F32),
            pltpu.VMEM((local, D, FF), F32),
            pltpu.VMEM((local, FF), F32),
            pltpu.VMEM((local, D), F32),
            pltpu.VMEM((pieces, CHUNK, D), BF16),
            pltpu.VMEM((8 * local, D), F32),
            pltpu.VMEM((pieces, CHUNK // 2, D), BF16),
            pltpu.VMEM((pieces, landing_rows(CHUNK, depth), D), BF16),
            pltpu.VMEM((pieces, share, D), BF16),
            pltpu.VMEM((depth, 8 * local, D), F32),
            dma((local, members)), dma((local, members)), dma((local, members)), dma((local, members)),
            dma((pieces, depth + 1)), dma((pieces, depth + 1)), dma((depth,)), dma((depth,)),
        ],
        compiler_params=pltpu.CompilerParams(
            collective_id=1, has_side_effects=True, vmem_limit_bytes=60 * 2**20
        ),
        name="experts",
    )(place, rows, up_weight, up_bias, down_weight, down_bias)
    returned = returned.reshape(EXPERTS * SLOTS, 2 * D)

    output, grad_tokens, chunks, shared, small = pl.pallas_call(
        partial(backward_kernel, copies, members, local),
        grid=(images // PAIR,),
        in_specs=[
            whole((count, D)), whole((count, D)), whole((FRAME, 1)), whole((8, D)), whole((D, 3 * D)), whole((D, D)),
            whole((EXPERTS, D)), whole((TABLE, ROWS * ROWS)),
            per_step(SPREAD, 3 * D), per_step(4 * PAIR * GROUPS * ROWS, WIDE), per_step(SPREAD, D), per_step(SPREAD, D),
            per_step(SPREAD, 128), whole((EXPERTS * SLOTS, 2 * D)), whole((pieces, 2 * share, D)),
        ],
        out_specs=[
            whole((count, D)), whole((count, D)), pl.BlockSpec(memory_space=pl.ANY),
            pl.BlockSpec(memory_space=pl.ANY), whole((32, D)),
        ],
        out_shape=[
            jax.ShapeDtypeStruct((count, D), BF16),
            jax.ShapeDtypeStruct((count, D), F32),
            jax.ShapeDtypeStruct((pieces, CHUNK, D), BF16),
            jax.ShapeDtypeStruct((CHUNK, D), BF16),
            jax.ShapeDtypeStruct((32, D), F32),
        ],
        scratch_shapes=[
            pltpu.VMEM((SPREAD, 3 * D), BF16), pltpu.VMEM((SPREAD, D), BF16), pltpu.VMEM((SPREAD, D), F32),
            pltpu.VMEM((D, 3 * D), F32), pltpu.VMEM((D, D), F32),
            pltpu.VMEM((ROWS, HEADS * ROWS), F32),
            pltpu.VMEM((16, ROWS * ROWS), F32),
            pltpu.VMEM((CHUNK, D), BF16),
            pltpu.VMEM((32, D), F32),
            pltpu.VMEM((PARTS, PART // 2, D), BF16),
            pltpu.VMEM((PARTS, landing_rows(PART, total), D), BF16),
            pltpu.VMEM((PARTS, halvings(PART, total)[-1][0], D), BF16),
            pltpu.VMEM((total, 32, D), F32),
            pltpu.VMEM((pieces, 2 * share, D), BF16),
            pltpu.VMEM((pieces, share, D), BF16),
            pltpu.VMEM((pieces, share, D), BF16),
            pltpu.VMEM((pieces, CHUNK, D), BF16),
            pltpu.VMEM((CHUNK, D), BF16),
            pltpu.VMEM((32, D), F32),
            dma((pieces, depth + 1)), dma((pieces, depth + 1)), dma((PARTS, total)), dma((PARTS, total)),
            dma((PARTS, total)), dma((PARTS, total)), dma((total,)), dma((total,)), dma((pieces + 1,)),
        ],
        compiler_params=pltpu.CompilerParams(
            dimension_semantics=("arbitrary",), collective_id=2, has_side_effects=True, vmem_limit_bytes=60 * 2**20
        ),
        name="backward",
    )(
        tokens, grad_output, source, vectors, qkv_weight, out_weight, router, hot.astype(BF16), projected, weights,
        attended, residual, aux, returned, held,
    )

    results = pl.pallas_call(
        finish_kernel,
        grid=(local, FF // D),
        in_specs=[
            pl.BlockSpec((1, D, D), lambda j, t: (2 * j, t, 0)), pl.BlockSpec((1, D, D), lambda j, t: (2 * j + 1, t, 0)),
            whole((8 * local, D)), whole((CHUNK, D)), whole((32, D)),
        ],
        out_specs=[
            pl.BlockSpec((1, D, D), lambda j, t: (j, 0, t)), pl.BlockSpec((1, D, D), lambda j, t: (j, t, 0)),
            whole((local, FF)), whole((local, D)), whole((D, 3 * D)), whole((D, D)), whole((EXPERTS, D)),
            whole((HEADS, TABLE)), *[whole((D,))] * 7,
        ],
        out_shape=[
            jax.ShapeDtypeStruct(shape, F32)
            for shape in (
                (local, D, FF), (local, FF, D), (local, FF), (local, D), (D, 3 * D), (D, D), (EXPERTS, D),
                (HEADS, TABLE), *[(D,)] * 7,
            )
        ],
        compiler_params=pltpu.CompilerParams(
            dimension_semantics=("arbitrary", "arbitrary"), vmem_limit_bytes=60 * 2**20
        ),
        name="finish",
    )(chunks, chunks, biases, shared, small)
    grad_up, grad_down, grad_up_bias, grad_down_bias, grad_qkv, grad_out, grad_router, grad_table = results[:8]
    grad_gain1, grad_bias1, grad_q, grad_v, grad_out_bias, grad_gain2, grad_bias2 = results[8:]
    return (
        output, grad_tokens, grad_gain1, grad_bias1, grad_qkv, grad_q, grad_v, grad_table.T, grad_out, grad_out_bias,
        grad_gain2, grad_bias2, grad_router.T, grad_up, grad_up_bias, grad_down, grad_down_bias,
    )


def solution(mesh):
    tokens = P(("dp", "expert"), None)
    expert = P("expert", None, None)
    expert_bias = P("expert", None)
    routes = P(("dp", "expert"))
    return jax.shard_map(
        shards,
        mesh=mesh,
        in_specs=(
            tokens, P(), P(), P(), P(), P(), P(), P(), P(), P(), P(), P(), expert, expert_bias, expert, expert_bias,
            routes, routes, tokens,
        ),
        out_specs=(
            tokens, tokens, P(), P(), P(), P(), P(), P(), P(), P(), P(), P(), P(), expert, expert_bias, expert,
            expert_bias,
        ),
        check_vma=False,
    )
```

```python
from functools import partial

import jax
import jax.numpy as jnp
import numpy as np
from jax import lax
from jax.experimental import pallas as pl
from jax.experimental.pallas import tpu as pltpu
from jax.sharding import PartitionSpec as P

D = 384
HEADS = 12
HEAD = 32
FF = 1536
EXPERTS = 8
WINDOW = 7
SIDE = 14
SHIFT = 3
CAP = 245
CELLS = WINDOW * WINDOW
IMAGE = SIDE * SIDE
TABLE = (2 * WINDOW - 1) ** 2

ROWS = 64
SLOTS = 256
FRAME = 4 * ROWS
SPAN = 208
GROUP = 4
GROUPS = HEADS // GROUP
LANES = GROUP * HEAD
WIDE = GROUP * ROWS

EPSILON = 1e-05
MASK_NEG = -100.0
SCALE = HEAD ** (-0.5)
HIGHEST = lax.Precision.HIGHEST
F32 = jnp.float32
BF16 = jnp.bfloat16


def source_cells():
    source = np.full((FRAME, 1), -1000, np.int32)
    for row in range(FRAME):
        window, cell = divmod(row, ROWS)
        if cell < CELLS:
            down = (window // 2) * WINDOW + cell // WINDOW
            across = (window % 2) * WINDOW + cell % WINDOW
            source[row, 0] = ((down + SHIFT) % SIDE) * SIDE + (across + SHIFT) % SIDE
    return source


def window_masks():
    places = np.arange(SIDE)
    bands = (places >= SIDE - WINDOW).astype(np.int32) + (places >= SIDE - SHIFT)
    masks = np.zeros((4, ROWS, ROWS), np.float32)
    for window in range(4):
        rows = bands[(window // 2) * WINDOW : (window // 2 + 1) * WINDOW]
        cols = bands[(window % 2) * WINDOW : (window % 2 + 1) * WINDOW]
        labels = (rows[:, None] * 3 + cols[None, :]).reshape(-1)
        masks[window, :CELLS, :CELLS] = np.where(labels[:, None] != labels[None, :], MASK_NEG, 0.0)
    masks[:, CELLS:, :] = -1e30
    return np.tile(masks, (1, 1, GROUP))


def offset_onehot():
    hot = np.zeros((TABLE, ROWS, ROWS), np.float32)
    for q in range(CELLS):
        for p in range(CELLS):
            entry = (p // WINDOW - q // WINDOW + WINDOW - 1) * (2 * WINDOW - 1)
            entry += p % WINDOW - q % WINDOW + WINDOW - 1
            hot[entry, q, p] = 1.0
    return hot.reshape(TABLE, ROWS * ROWS)


def mm(left, right):
    return jnp.dot(left, right, preferred_element_type=F32)


def mm_nt(left, right):
    return lax.dot_general(left, right, (((1,), (1,)), ((), ())), preferred_element_type=F32)


def mm_tn(left, right):
    return lax.dot_general(left, right, (((0,), (0,)), ((), ())), preferred_element_type=F32)


def permutation(source, offset, width):
    places = lax.broadcasted_iota(jnp.int32, (FRAME, width), 1)
    return jnp.where(source + offset == places, 1.0, 0.0).astype(BF16)


def normalize(values):
    center = values - jnp.mean(values, axis=-1, keepdims=True)
    inverse = lax.rsqrt(jnp.mean(center * center, axis=-1, keepdims=True) + EPSILON)
    return center * inverse, inverse


def normalize_pull(grad, hat, inverse, gain):
    scaled = grad * gain
    first = jnp.mean(scaled, axis=-1, keepdims=True)
    second = jnp.mean(scaled * hat, axis=-1, keepdims=True)
    return (scaled - first - hat * second) * inverse


def spread_heads(block):
    heads = lax.broadcasted_iota(jnp.int32, block.shape, 1) // HEAD
    return jnp.concatenate(
        [jnp.where(heads == h, block, jnp.zeros_like(block)) for h in range(GROUP)], axis=0
    )


def pick_heads(wide):
    heads = lax.broadcasted_iota(jnp.int32, (ROWS, LANES), 1) // HEAD
    picked = wide[:ROWS]
    for h in range(1, GROUP):
        picked = jnp.where(heads == h, wide[h * ROWS : (h + 1) * ROWS], picked)
    return picked


def image_span(image):
    offset = lax.rem(image * (IMAGE % 16), 16)
    return pl.multiple_of(image * IMAGE - offset, 16), offset


def split_three(values):
    high = values.astype(BF16)
    rest = values - high.astype(F32)
    middle = rest.astype(BF16)
    return high, middle, (rest - middle.astype(F32)).astype(BF16)


VECTORS = ("ln1_gain", "ln1_bias", "q_bias", "v_bias", "out_bias", "ln2_gain", "ln2_bias")


def vector(refs, name):
    return refs[name][...][None, :]


def with_vectors(kernel, at):
    def wrapped(*refs):
        after = at + len(VECTORS)
        return kernel(*refs[:at], dict(zip(VECTORS, refs[at:after])), *refs[after:])

    return wrapped


PAIR = 2
SPREAD = PAIR * FRAME


def orders(step, source):
    found = []
    for k in range(PAIR):
        start, offset = image_span(step * PAIR + k)
        found.append((pl.ds(start, SPAN), permutation(source, offset, SPAN)))
    return found


def arranged(ref, order):
    return jnp.concatenate([mm(hot, ref[rows, :]) for rows, hot in order], axis=0)


def windows_of_step():
    return [(w % 4, slice(w * ROWS, (w + 1) * ROWS)) for w in range(4 * PAIR)]


def group_cols(third, group):
    return slice(third * D + group * LANES, third * D + (group + 1) * LANES)


def forward_kernel(
    tokens_ref, grad_ref, route_ref, source_ref, vectors_ref, qkv_ref, table_ref, hot_ref, mask_ref, out_weight_ref, router_ref,
    projected_ref, weights_ref, attended_ref, residual_ref, rows_ref, place_ref, aux_ref,
    relative, hot_copy, grad_copy, fetches,
):
    fetched = [
        pltpu.make_async_copy(hot_ref, hot_copy, fetches.at[0]), pltpu.make_async_copy(grad_ref, grad_copy, fetches.at[1])
    ]

    @pl.when(pl.program_id(0) == 0)
    def _():
        for copy in fetched:
            copy.start()

    source = source_ref[...]
    order = orders(pl.program_id(0), source)
    inputs = arranged(tokens_ref, order)

    hat, _ = normalize(inputs)
    normed = (hat * vector(vectors_ref, "ln1_gain") + vector(vectors_ref, "ln1_bias")).astype(BF16)
    for third, name in enumerate(("q_bias", "k_bias", "v_bias")):
        at = slice(third * D, (third + 1) * D)
        part = mm(normed, qkv_ref[:, at])
        if name in VECTORS:
            part = part + vector(vectors_ref, name)
        projected_ref[:, at] = part.astype(BF16)

    @pl.when(pl.program_id(0) == 0)
    def _():
        relative[...] = jnp.zeros_like(relative)
        for copy in fetched:
            copy.wait()
        flat = sum(mm(part, hot_copy[...]) for part in split_three(table_ref[...]))
        for q in range(CELLS):
            for h in range(HEADS):
                relative[q : q + 1, h * ROWS : (h + 1) * ROWS] = flat[h : h + 1, q * ROWS : (q + 1) * ROWS]

    for index, (window, rows) in enumerate(windows_of_step()):
        scores = []
        for group in range(GROUPS):
            queries = projected_ref[rows, group_cols(0, group)]
            scores.append(mm_nt(projected_ref[rows, group_cols(1, group)], spread_heads(queries)))
        for group in range(GROUPS):
            wide = slice(group * WIDE, (group + 1) * WIDE)
            full = scores[group] * SCALE + (relative[:, wide] + mask_ref[window])
            powers = jnp.exp(full - jnp.max(full, axis=0, keepdims=True))
            weights = (powers * (1.0 / jnp.sum(powers, axis=0, keepdims=True))).astype(BF16)
            place = (index * GROUPS + group) * ROWS
            weights_ref[place : place + ROWS, :] = weights
            mixed = mm_tn(weights, projected_ref[rows, group_cols(2, group)])
            attended_ref[rows, group_cols(0, group)] = pick_heads(mixed).astype(BF16)

    plain = permutation(source, 0, FRAME)
    chosen_cols, place_cols = [], []
    for k in range(PAIR):
        route = route_ref[k]
        cols = mm_nt(plain, route)
        rows = mm_nt(route, plain)
        place_row = jnp.where(rows[1:2] > 0.5, rows[0:1] * SLOTS + rows[1:2] - 1.0, -1.0)
        place_ref[k] = jnp.broadcast_to(place_row, (8, FRAME)).astype(jnp.int32)
        chosen_cols.append(cols[:, 0:1])
        place_cols.append(jnp.where(cols[:, 1:2] > 0.5, cols[:, 0:1] * SLOTS + cols[:, 1:2] - 1.0, -1.0))
    chosen = jnp.concatenate(chosen_cols, axis=0)

    residual = inputs + (mm(attended_ref[...], out_weight_ref[...]) + vector(vectors_ref, "out_bias"))
    residual_ref[...] = residual
    hat, _ = normalize(residual)
    normed = (hat * vector(vectors_ref, "ln2_gain") + vector(vectors_ref, "ln2_bias")).astype(BF16)
    logits = sum(mm_nt(normed, part) for part in split_three(router_ref[...]))
    logits = jnp.exp(logits - jnp.max(logits, axis=-1, keepdims=True))
    probs = logits / jnp.sum(logits, axis=-1, keepdims=True)
    experts = lax.broadcasted_iota(jnp.int32, (SPREAD, EXPERTS), 1).astype(F32)
    gate = jnp.sum(jnp.where(experts == chosen, probs, 0.0), axis=-1, keepdims=True)
    rows_ref[:, :D] = normed
    rows_ref[:, D:] = (gate * arranged(grad_copy, order)).astype(BF16)
    aux_ref[:, 0:EXPERTS] = probs
    aux_ref[:, EXPERTS : EXPERTS + 1] = gate
    aux_ref[:, EXPERTS + 1 : EXPERTS + 2] = jnp.concatenate(place_cols, axis=0)
    aux_ref[:, EXPERTS + 2 : EXPERTS + 3] = chosen


def backward_kernel(
    copies, members, local, tokens_ref, grad_ref, source_ref, vectors_ref, qkv_ref, out_weight_ref, router_ref, hot_ref,
    projected_ref, weights_ref, attended_ref, residual_ref, aux_ref, returned_ref, held_ref,
    output_ref, grad_tokens_ref, chunks_ref, shared_ref, small_ref,
    grad_projected, grad_attended, grad_residual, outputs, grad_qkv, grad_out, totals, flat, shared, small,
    work, landing, shard, small_landing, held, late_landing, shares, chunks, shared_sum, small_sum,
    tokens, hot_table, output_sum, grad_tokens, fetches,
    chunk_sends, chunk_recvs, scatter_sends, scatter_recvs, gather_sends, gather_recvs, small_sends, small_recvs, part_sends, part_recvs,
    writes,
):
    step = pl.program_id(0)
    steps = IMAGES // PAIR
    everyone = [("expert", s) for s in strides(members)] + copy_bits(copies)[0]
    gathers, late = [], []
    share = shares.shape[1]
    for c, bits in enumerate(chunk_bits(copies, 2 * local)):
        depth = len(bits)
        if c < 2 * (local - 1):
            semaphores = chunk_sends.at[c], chunk_recvs.at[c]
            gathers.append(Gather(held.at[c], chunks.at[c], CHUNK, *semaphores, bits, skip=1))
        else:
            last = chunk_sends.at[c, pl.ds(depth, 1)], chunk_recvs.at[c, pl.ds(depth, 1)]
            scatter = Scatter(held.at[c], shares.at[c], 2 * share, None, late_landing.at[c], *last, bits[-1:])
            semaphores = chunk_sends.at[c], chunk_recvs.at[c]
            gathers.append(Chain(scatter, Gather(shares.at[c], chunks.at[c], CHUNK, *semaphores, bits)))
            late.append(c)
    small_stream = Doubling(small, small_sum, small_landing, small_sends, small_recvs, everyone)
    shared_streams = []
    rest = everyone[1:]
    for part in range(PARTS):
        turn = part * len(rest) // PARTS
        bits = everyone[:1] + rest[turn:] + rest[:turn]
        rows = pl.ds(part * PART, PART)
        scatter = Scatter(
            shared.at[rows], shard.at[part], PART, work.at[part], landing.at[part],
            scatter_sends.at[part], scatter_recvs.at[part], bits,
        )
        gather = Gather(shard.at[part], shared_sum.at[rows], PART, gather_sends.at[part], gather_recvs.at[part], bits)
        shared_streams.append(Chain(scatter, gather))
    runner = Runner()
    plan = {}
    for c, gather in enumerate(gathers):
        for stage, place in enumerate(PLACES.get(gather.steps, ())):
            plan.setdefault(place, []).append((c, stage))
    planned = [pair for pairs in plan.values() for pair in pairs]

    def advance(c, stage):
        if stage:
            gathers[c].finish(stage - 1)
        gathers[c].start(stage)

    def last_part(c, part):
        return gathers[c].second.last_part(part, part_sends.at[c], part_recvs.at[c])

    def exchange_at(phase):
        for s in range(steps):
            if due := plan.get(s * PHASES + phase):

                @pl.when(step == s)
                def _(due=due):
                    for c, stage in due:
                        advance(c, stage)

    fetched = [
        pltpu.make_async_copy(source, target, fetches.at[i])
        for i, (source, target) in enumerate(((held_ref, held), (tokens_ref, tokens), (hot_ref, hot_table)))
    ]

    @pl.when(step == 0)
    def _():
        greet([partner(*bit)[1] for bit in everyone])
        for copy in fetched:
            copy.start()
        for ref in (output_sum, grad_tokens, grad_qkv, grad_out, totals, small):
            ref[...] = jnp.zeros_like(ref)
        fetched[0].wait()

    exchange_at(0)
    order = orders(step, source_ref[...])
    upstream = arranged(grad_ref, order)
    residual = residual_ref[...]
    aux = aux_ref[...]
    probs = aux[:, 0:EXPERTS]
    gate = aux[:, EXPERTS : EXPERTS + 1]
    place = aux[:, EXPERTS + 1 : EXPERTS + 2].astype(jnp.int32)
    chosen = aux[:, EXPERTS + 2 : EXPERTS + 3]

    slots = lax.broadcasted_iota(jnp.int32, (SPREAD, EXPERTS * SLOTS), 1)
    hot = jnp.where(slots == place, 1.0, 0.0).astype(BF16)
    gathered = mm(hot, returned_ref[...])
    combined = gathered[:, :D]
    output = (residual + gate * combined).astype(BF16)
    of_step = pl.ds(pl.multiple_of(step * SPREAD, SPREAD), SPREAD)
    outputs[of_step, :] = output

    hat2, inverse2 = normalize(residual)
    normed2 = (hat2 * vector(vectors_ref, "ln2_gain") + vector(vectors_ref, "ln2_bias")).astype(BF16)
    gate_grad = jnp.sum(upstream * combined, axis=-1, keepdims=True)
    experts = lax.broadcasted_iota(jnp.int32, (SPREAD, EXPERTS), 1).astype(F32)
    grad_logits = gate_grad * gate * (jnp.where(experts == chosen, 1.0, 0.0) - probs)
    logits_high, logits_low, _ = split_three(grad_logits)
    small[8:16, :] += mm_tn(logits_high, normed2) + mm_tn(logits_low, normed2)
    router_high, router_low, _ = split_three(router_ref[...])
    grad_normed = (
        gathered[:, D:] + mm(logits_high, router_high) + mm(logits_low, router_high) + mm(logits_high, router_low)
    )
    small[0:1, :] += jnp.sum(grad_normed * hat2, axis=0, keepdims=True)
    small[1:2, :] += jnp.sum(grad_normed, axis=0, keepdims=True)
    grad_mixed = upstream + normalize_pull(grad_normed, hat2, inverse2, vector(vectors_ref, "ln2_gain"))
    grad_residual[of_step, :] = grad_mixed
    grad_mixed = grad_mixed.astype(BF16)
    grad_out[...] += mm_tn(attended_ref[...], grad_mixed)
    small[2:3, :] += jnp.sum(grad_mixed.astype(F32), axis=0, keepdims=True)
    grad_attended[...] = mm_nt(grad_mixed, out_weight_ref[...]).astype(BF16)

    exchange_at(1)
    for index, (_, rows) in enumerate(windows_of_step()):
        if index == 2 * PAIR:
            exchange_at(2)
        out_rows = pl.ds(pl.multiple_of(step * SPREAD + index * ROWS, ROWS), ROWS)
        spread_grads = [spread_heads(grad_attended[rows, group_cols(0, g)]) for g in range(GROUPS)]
        grad_weights = [
            mm_nt(projected_ref[rows, group_cols(2, g)], spread_grads[g]) for g in range(GROUPS)
        ]
        for g in range(GROUPS):
            at = (index * GROUPS + g) * ROWS
            weights = weights_ref[at : at + ROWS, :]
            exact = weights.astype(F32)
            scores = exact * (grad_weights[g] - jnp.sum(exact * grad_weights[g], axis=0, keepdims=True))
            scores = scores.astype(BF16)
            totals[:, g * WIDE : (g + 1) * WIDE] += scores.astype(F32)
            grad_projected[out_rows, group_cols(2, g)] = mm(weights, spread_grads[g]).astype(BF16)
            grad_keys = mm(scores, spread_heads(projected_ref[rows, group_cols(0, g)]))
            grad_projected[out_rows, group_cols(1, g)] = (grad_keys * SCALE).astype(BF16)
            grad_queries = pick_heads(mm_tn(scores, projected_ref[rows, group_cols(1, g)]))
            grad_projected[out_rows, group_cols(0, g)] = (grad_queries * SCALE).astype(BF16)

    exchange_at(3)

    @pl.when(step == 0)
    def _():
        for copy in fetched[1:]:
            copy.wait()

    grads = grad_projected[of_step, :]
    hat1, _ = normalize(arranged(tokens, order))
    normed1 = (hat1 * vector(vectors_ref, "ln1_gain") + vector(vectors_ref, "ln1_bias")).astype(BF16)
    grad_qkv[...] += mm_tn(normed1, grads)
    column_sums = jnp.sum(grads.astype(F32), axis=0, keepdims=True)
    for third in range(3):
        small[5 + third : 6 + third, :] += column_sums[:, third * D : (third + 1) * D]

    def first_norm_back(step):
        of_step = slice(step * SPREAD, (step + 1) * SPREAD)
        order = orders(step, source_ref[...])
        hat, inverse = normalize(arranged(tokens, order))
        grad_normed = mm_nt(grad_projected[of_step, :], qkv_ref[...])
        small[3:4, :] += jnp.sum(grad_normed * hat, axis=0, keepdims=True)
        small[4:5, :] += jnp.sum(grad_normed, axis=0, keepdims=True)
        pulled = normalize_pull(grad_normed, hat, inverse, vector(vectors_ref, "ln1_gain"))
        high, low, _ = split_three(grad_residual[of_step, :] + pulled)
        for k, (rows, hot) in enumerate(order):
            of_image = slice(k * FRAME, (k + 1) * FRAME)
            grad_tokens[rows, :] += mm_tn(hot, high[of_image]) + mm_tn(hot, low[of_image])
            output_sum[rows, :] += mm_tn(hot, outputs[of_step, :][of_image]).astype(BF16)

    @pl.when(step == steps - 1)
    def _():
        for third in range(3):
            at = slice(third * D, (third + 1) * D)
            shared[at, :] = grad_qkv[:, at].astype(BF16)
        shared[3 * D :, :] = grad_out[...].astype(BF16)
        runner.advance(*shared_streams)
        for c, gather in enumerate(gathers):
            for stage in range(gather.steps - (c in late)):
                if (c, stage) not in planned:
                    advance(c, stage)
        for c in late:
            gathers[c].finish(gathers[c].steps - 2)
        for done in range(max(steps, LAST_PARTS)):
            if done < LAST_PARTS:
                for c in late:
                    last_part(c, done).start()
            if done < steps:
                first_norm_back(done)
            runner.advance(*shared_streams)
        copies_out = [
            pltpu.make_async_copy(output_sum, output_ref, writes.at[len(gathers) + 1]),
            pltpu.make_async_copy(grad_tokens, grad_tokens_ref, writes.at[len(gathers) + 2]),
        ]
        for c, gather in enumerate(gathers):
            if c not in late:
                gather.finish(gather.steps - 1)
                copies_out.append(pltpu.make_async_copy(chunks.at[c], chunks_ref.at[c], writes.at[c]))
        for copy in copies_out:
            copy.start()
        flat[...] = jnp.zeros_like(flat)
        for q in range(CELLS):
            for h in range(HEADS):
                flat[h : h + 1, q * ROWS : (q + 1) * ROWS] = totals[q : q + 1, h * ROWS : (h + 1) * ROWS]
        table = sum(mm_nt(part, hot_table[...]) for part in split_three(flat[...]))
        small[16:32, : table.shape[1]] = table
        runner.advance(small_stream, *shared_streams)
        runner.complete(*shared_streams, small_stream)
        small_ref[...] = small_sum[...]
        ends = [pltpu.make_async_copy(shared_sum, shared_ref, writes.at[len(gathers)])]
        for c in late:
            for part in range(LAST_PARTS):
                last_part(c, part).wait()
            ends.append(pltpu.make_async_copy(chunks.at[c], chunks_ref.at[c], writes.at[c]))
        for copy in ends:
            copy.start()
        copies_out += ends
        for copy in copies_out:
            copy.wait()


PHASES = 4


PLACES = {2: (0, 7), 4: (0, 8, 14), 6: (0, 5, 8, 10, 12)}


IMAGES = 8
CHUNK = 4 * D
PARTS = 3
PART = CHUNK // PARTS
LAST_PARTS = 4
MESH = pl.DeviceIdType.MESH


def add_rows(left, left_at, right, right_at, out, out_at, count):
    step = next(s for s in (64, 48, 32, 16) if count % s == 0)

    def body(i, carry):
        here = i * step
        total = left[pl.ds(pl.multiple_of(left_at + here, 16), step), :].astype(F32)
        total = total + right[pl.ds(pl.multiple_of(right_at + here, 16), step), :].astype(F32)
        out[pl.ds(pl.multiple_of(out_at + here, 16), step), :] = total.astype(out.dtype)
        return carry

    lax.fori_loop(0, count // step, body, 0)


def partner(axis, stride):
    index = lax.axis_index(axis)
    bit = lax.rem(lax.div(index, stride), 2)
    return bit, {axis: index + stride - 2 * stride * bit}


def halvings(rows, count):
    sizes = []
    for _ in range(count):
        halved = rows % 32 == 0
        rows = rows // 2 if halved else rows
        sizes.append((rows, halved))
    return sizes


def landing_rows(rows, count):
    return sum(size for size, _ in halvings(rows, count))


def exchange(src, dst, sends, recvs, step, device):
    return pltpu.make_async_remote_copy(
        src_ref=src, dst_ref=dst, send_sem=sends.at[step], recv_sem=recvs.at[step], device_id=device, device_id_type=MESH
    )


def rows_at(ref, start, size):
    return ref.at[pl.ds(pl.multiple_of(start, 16), size)]


class Scatter:
    def __init__(self, source, out, rows, work, landing, sends, recvs, bits):
        self.source, self.out, self.work, self.landing = source, out, work, landing
        self.sends, self.recvs, self.bits = sends, recvs, bits
        self.steps = len(bits)
        self.plan = []
        at = land = 0
        for bit, (size, halved) in zip(bits, halvings(rows, len(bits))):
            b, device = partner(*bit)
            give, keep = (at + (1 - b) * size, at + b * size) if halved else (at, at)
            self.plan.append((give, keep, land, size, device))
            at = 0 if not self.plan[1:] else keep
            land += size

    def copy(self, step):
        give, _, land, size, device = self.plan[step]
        mine = self.work if step else self.source
        return exchange(
            rows_at(mine, give, size), self.landing.at[pl.ds(land, size)], self.sends, self.recvs, step, device
        )

    def add(self, step, start, size):
        _, keep, land, _, _ = self.plan[step]
        mine = self.work if step else self.source
        if step == self.steps - 1:
            out, out_at = self.out, 0
        else:
            out, out_at = self.work, keep if step else 0
        add_rows(mine, keep + start, self.landing, land + start, out, out_at + start, size)

    def halves(self, step):
        give, keep, _, size, _ = self.plan[step + 1]
        base = self.plan[step][1] if step else 0
        return size, give - base, keep - base

    def splits(self, step):
        return 0 <= step < self.steps - 1 and 2 * self.plan[step + 1][3] == self.plan[step][3]

    def start(self, step):
        self.copy(step).start()
        if self.splits(step - 1):
            size, _, stays = self.halves(step - 1)
            self.add(step - 1, stays, size)

    def finish(self, step):
        self.copy(step).wait()
        if self.splits(step):
            size, goes, _ = self.halves(step)
            self.add(step, goes, size)
        else:
            self.add(step, 0, self.plan[step][3])


class Gather:
    def __init__(self, share, out, rows, sends, recvs, bits, skip=0):
        self.share, self.out, self.sends, self.recvs = share, out, sends, recvs
        self.plan = []
        start = 0
        for bit, (size, halved) in zip(bits, halvings(rows, len(bits))):
            b, device = partner(*bit)
            start = start + b * size if halved else start
            if halved:
                self.plan.insert(0, (start, size, device))
        self.plan = self.plan[skip:]
        self.steps = len(self.plan)

    def copy(self, step):
        start, size, device = self.plan[step]
        return exchange(
            rows_at(self.out, start, size), rows_at(self.out, start, size), self.sends, self.recvs, step, device
        )

    def last_part(self, part, sends, recvs):
        start, size, device = self.plan[-1]
        size = size // LAST_PARTS
        rows = rows_at(self.out, start + part * size, size)
        return exchange(rows, rows, sends, recvs, part, device)

    def start(self, step):
        if step == 0:
            start, size, _ = self.plan[0]
            self.out[pl.ds(pl.multiple_of(start, 16), size), :] = self.share[...]
        self.copy(step).start()

    def finish(self, step):
        self.copy(step).wait()


class Chain:
    def __init__(self, first, second):
        self.first, self.second, self.steps = first, second, first.steps + second.steps

    def of(self, step):
        return (self.first, step) if step < self.first.steps else (self.second, step - self.first.steps)

    def start(self, step):
        stream, step = self.of(step)
        stream.start(step)

    def finish(self, step):
        stream, step = self.of(step)
        stream.finish(step)


class Doubling:
    def __init__(self, source, out, landing, sends, recvs, bits):
        self.source, self.out, self.landing = source, out, landing
        self.sends, self.recvs, self.bits = sends, recvs, bits
        self.steps = len(bits)

    def copy(self, step):
        device = partner(*self.bits[step])[1]
        return exchange(self.out, self.landing.at[step], self.sends, self.recvs, step, device)

    def start(self, step):
        if step == 0:
            self.out[...] = self.source[...]
        self.copy(step).start()

    def finish(self, step):
        self.copy(step).wait()
        self.out[...] = self.out[...] + self.landing[step]


class Runner:
    def __init__(self):
        self.at = {}

    def advance(self, *streams):
        for stream in streams:
            step = self.at.get(stream, -1)
            if step < stream.steps:
                if step >= 0:
                    stream.finish(step)
                self.at[stream] = step = step + 1
                if step < stream.steps:
                    stream.start(step)

    def complete(self, *streams):
        while any(self.at.get(s, -1) < s.steps for s in streams):
            self.advance(*streams)


def strides(size):
    return [2**k for k in range(size.bit_length() - 1)]


def copy_bits(copies):
    low = len(strides(copies)) // 2
    all_bits = [("dp", s) for s in strides(copies)]
    return all_bits, all_bits[low : low + 1] + all_bits[:low] + all_bits[low + 1 :]


def chunk_bits(copies, count):
    first, second = copy_bits(copies)
    return [second if c % 2 else first for c in range(count)]


def greet(devices):
    barrier = pltpu.get_barrier_semaphore()
    for device in devices:
        pl.semaphore_signal(barrier, inc=1, device_id=device, device_id_type=MESH)
    pl.semaphore_wait(barrier, len(devices))


def member_at(members, hop, sign):
    index = lax.axis_index("expert")
    chips = members // 2
    chip = lax.rem(lax.div(index, 2) + sign * (hop // 2) + chips, chips)
    return chip * 2 + lax.rem(lax.rem(index, 2) + hop % 2, 2)


TILE = 512


def experts_kernel(
    copies, members, local, place_ref, rows_ref, up_ref, up_bias_ref, down_ref, down_bias_ref,
    returned_ref, held_ref, biases_ref,
    up, down, outbox, inbox, results, up_sum, down_sum, up_bias_sum, down_bias_sum, chunks, biases, work, landing, shares,
    bias_landing,
    out_sends, out_recvs, back_sends, back_recvs, chunk_sends, chunk_recvs, bias_sends, bias_recvs, fetches,
):
    me = lax.axis_index("expert")
    fetched = [
        pltpu.make_async_copy(up_ref, up, fetches.at[0]), pltpu.make_async_copy(down_ref, down, fetches.at[1])
    ]
    for copy in fetched:
        copy.start()
    bits = chunk_bits(copies, 2 * local)
    greet(
        [{"expert": member_at(members, hop, 1)} for hop in range(1, members)]
        + [partner(*bit)[1] for bit in copy_bits(copies)[0]]
    )
    places = jnp.concatenate([place_ref[i, 0:1, :] for i in range(place_ref.shape[0])], axis=1)

    def out_copy(hop, j):
        return pltpu.make_async_remote_copy(
            src_ref=outbox.at[j, hop], dst_ref=inbox.at[j, hop],
            send_sem=out_sends.at[j, hop], recv_sem=out_recvs.at[j, hop],
            device_id={"expert": member_at(members, hop, 1)}, device_id_type=MESH,
        )

    def back_copy(hop, j):
        return pltpu.make_async_remote_copy(
            src_ref=results.at[j, hop], dst_ref=returned_ref.at[me, j],
            send_sem=back_sends.at[j, hop], recv_sem=back_recvs.at[j, hop],
            device_id={"expert": member_at(members, hop, -1)}, device_id_type=MESH,
        )

    def dispatch(hop, j):
        expert = member_at(members, hop, 1) * local + j
        slots = lax.broadcasted_iota(jnp.int32, (SLOTS, places.shape[1]), 0) + expert * SLOTS
        hot = jnp.where(slots == places, 1.0, 0.0).astype(BF16)
        return mm(hot, rows_ref[...]).astype(BF16)

    order = [(hop, j) for j in range(local) for hop in range(members - 1, 1, -1)]
    order += [(hop, j) for j in range(local) for hop in (1, 0)]
    for hop, j in order:
        if hop:
            outbox[j, hop] = dispatch(hop, j)
            if hop == 1 or j == 0:
                out_copy(hop, j).start()
        else:
            inbox[j, 0] = dispatch(0, j)

    for copy in fetched:
        copy.wait()
    up_sum[...] = jnp.zeros_like(up_sum)
    down_sum[...] = jnp.zeros_like(down_sum)
    up_bias_sum[...] = jnp.zeros_like(up_bias_sum)
    down_bias_sum[...] = jnp.zeros_like(down_bias_sum)

    def compute(pair, j):
        hops = (2 * pair, 2 * pair + 1)
        for hop in hops:
            if hop:
                out_copy(hop, j).wait_recv()
        inputs = inbox[j, 2 * pair : 2 * pair + 2, :, :D].reshape(2 * SLOTS, D)
        grads = inbox[j, 2 * pair : 2 * pair + 2, :, D:].reshape(2 * SLOTS, D)
        inputs_t = inputs.T
        grads_t = grads.T
        outs = jnp.zeros((2 * SLOTS, D), F32)
        backs = jnp.zeros((2 * SLOTS, D), F32)
        for tile in range(FF // TILE):
            at = slice(tile * TILE, (tile + 1) * TILE)
            pre = mm(inputs, up[j, :, at]) + up_bias_ref[j : j + 1, at]
            grad_hidden = mm_nt(grads, down[j, at, :])
            share = 0.5 + 0.5 * lax.erf(pre * 0.7071067811865476)
            density = jnp.exp(pre * pre * -0.5) * 0.3989422804014327
            hidden = (pre * share).astype(BF16)
            grad_pre = (grad_hidden * (share + pre * density)).astype(BF16)
            outs += mm(hidden, down[j, at, :])
            backs += mm_nt(grad_pre, up[j, :, at])
            down_sum[j, :, at] += mm(grads_t, hidden)
            up_sum[j, :, at] += mm(inputs_t, grad_pre)
            up_bias_sum[j : j + 1, at] += jnp.sum(grad_pre.astype(F32), axis=0, keepdims=True)
        down_bias_sum[j : j + 1, :] += jnp.sum(grads.astype(F32), axis=0, keepdims=True)
        results[j, 2 * pair : 2 * pair + 2, :, :D] = (
            (outs + down_bias_ref[j : j + 1, :]).astype(BF16).reshape(2, SLOTS, D)
        )
        results[j, 2 * pair : 2 * pair + 2, :, D:] = backs.astype(BF16).reshape(2, SLOTS, D)
        if pair == 0:
            returned_ref[me, j] = results[j, 0]
            back_copy(1, j).start()

    def seal(j):
        for tile in range(FF // D):
            at = slice(tile * D, (tile + 1) * D)
            chunks[2 * j, at, :] = up_sum[j, :, at].astype(BF16)
            chunks[2 * j + 1, at, :] = down_sum[j, :, at].T.astype(BF16)
            biases[8 * j + tile : 8 * j + tile + 1, :] = up_bias_sum[j : j + 1, at]
        biases[8 * j + 4 : 8 * j + 5, :] = down_bias_sum[j : j + 1, :]
        biases[8 * j + 5 : 8 * j + 8, :] = jnp.zeros((3, D), F32)

    streams = []
    for c in range(2 * local):
        early = c < 2 * (local - 1)
        parts = chunks.at[c], shares.at[c] if early else held_ref.at[c], CHUNK, work.at[c], landing.at[c]
        semaphores = chunk_sends.at[c], chunk_recvs.at[c]
        if early:
            depth, share = len(bits[c]), shares.shape[1]
            semaphores_back = chunk_sends.at[c, pl.ds(depth, 1)], chunk_recvs.at[c, pl.ds(depth, 1)]
            back = Gather(shares.at[c], held_ref.at[c], 2 * share, *semaphores_back, bits[c][-1:])
            streams.append(Chain(Scatter(*parts, *semaphores, bits[c]), back))
        else:
            streams.append(Scatter(*parts, *semaphores, bits[c][:-1]))
    runner = Runner()
    far = range(2, members)
    for j in range(local):
        compute(0, j)
        for hop in far:
            out_copy(hop, j).wait_send()
        for hop in far:
            if j + 1 < local:
                out_copy(hop, j + 1).start()
            else:
                for held in range(j):
                    back_copy(hop, held).start()
        for pair in range(1, members // 2):
            compute(pair, j)
        if j == local - 1:
            for hop in far:
                back_copy(hop, j).start()
        seal(j)
        if j < local - 1:
            runner.advance(*streams[2 * j : 2 * j + 2])
    small = Doubling(biases, biases_ref, bias_landing, bias_sends, bias_recvs, copy_bits(copies)[0])
    early, late = streams[: 2 * (local - 1)], streams[2 * (local - 1) :]
    for turn in (early, early, late, early, late, early):
        runner.advance(small, *turn)
    runner.complete(small, *early, *late)
    for j in range(local):
        out_copy(1, j).wait_send()
        for hop in range(1, members):
            back_copy(hop, j).wait()


def finish_kernel(
    up_tile_ref, down_tile_ref, biases_ref, shared_ref, small_ref,
    up_ref, down_ref, up_bias_ref, down_bias_ref, qkv_ref, out_ref, router_ref, table_ref, *vector_refs,
):
    for tile in range(up_tile_ref.shape[1] // D):
        at = slice(tile * D, (tile + 1) * D)
        up_ref[0, :, at] = up_tile_ref[0, at, :].astype(F32)
    down_ref[0] = down_tile_ref[0].astype(F32)

    @pl.when((pl.program_id(0) == 0) & (pl.program_id(1) == 0))
    def _():
        for j in range(up_bias_ref.shape[0]):
            for tile in range(FF // D):
                row = 8 * j + tile
                up_bias_ref[j : j + 1, tile * D : (tile + 1) * D] = biases_ref[row : row + 1, :]
            down_bias_ref[j : j + 1, :] = biases_ref[8 * j + 4 : 8 * j + 5, :]
        for third in range(3):
            at = slice(third * D, (third + 1) * D)
            qkv_ref[:, at] = shared_ref[at, :].astype(F32)
        out_ref[...] = shared_ref[3 * D :, :].astype(F32)
        router_ref[...] = small_ref[8:16, :]
        table_ref[...] = small_ref[16 : 16 + HEADS, :TABLE]
        for ref, row in zip(vector_refs, (3, 4, 5, 7, 2, 0, 1)):
            ref[...] = small_ref[row, :]


def whole(shape):
    return pl.BlockSpec(shape, lambda *_: (0,) * len(shape))


def per_step(rows, columns):
    return pl.BlockSpec((rows, columns), lambda i: (i, 0))


def shards(
    tokens, ln1_gain, ln1_bias, qkv_weight, q_bias, v_bias, bias_table, out_weight, out_bias, ln2_gain, ln2_bias,
    router_weight, up_weight, up_bias, down_weight, down_bias, expert_of, slot_of, grad_output,
):
    members = lax.axis_size("expert")
    local = up_weight.shape[0]
    count = tokens.shape[0]
    images = count // IMAGE
    framed = images * FRAME
    params = pltpu.CompilerParams(dimension_semantics=("arbitrary",), vmem_limit_bytes=60 * 2**20)

    source = jnp.asarray(source_cells())
    masks = jnp.asarray(window_masks())
    hot = jnp.asarray(offset_onehot().astype(BF16))
    route = jnp.stack([expert_of, slot_of + 1]).astype(BF16).reshape(2, images, IMAGE).transpose(1, 0, 2)
    route = jnp.pad(route, ((0, 0), (0, 6), (0, FRAME - IMAGE)))
    vectors = (ln1_gain, ln1_bias, q_bias, v_bias, out_bias, ln2_gain, ln2_bias)
    router = router_weight.T
    vmem = pl.BlockSpec(memory_space=pltpu.VMEM)
    anywhere = pl.BlockSpec(memory_space=pl.ANY)
    dma = pltpu.SemaphoreType.DMA

    projected, weights, attended, residual, rows, place, aux = pl.pallas_call(
        with_vectors(forward_kernel, 4),
        grid=(images // PAIR,),
        in_specs=[
            whole((count, D)), anywhere, pl.BlockSpec((PAIR, 8, FRAME), lambda i: (i, 0, 0)),
            whole((FRAME, 1)), *[whole((D,))] * len(VECTORS), whole((D, 3 * D)), whole((HEADS, TABLE)), anywhere,
            whole((4, ROWS, WIDE)), whole((D, D)), whole((EXPERTS, D)),
        ],
        out_specs=[
            per_step(SPREAD, 3 * D), per_step(4 * PAIR * GROUPS * ROWS, WIDE), per_step(SPREAD, D), per_step(SPREAD, D),
            per_step(SPREAD, 2 * D), pl.BlockSpec((PAIR, 8, FRAME), lambda i: (i, 0, 0)), per_step(SPREAD, 128),
        ],
        out_shape=[
            jax.ShapeDtypeStruct((framed, 3 * D), BF16),
            jax.ShapeDtypeStruct((images * 4 * GROUPS * ROWS, WIDE), BF16),
            jax.ShapeDtypeStruct((framed, D), BF16),
            jax.ShapeDtypeStruct((framed, D), F32),
            jax.ShapeDtypeStruct((framed, 2 * D), BF16),
            jax.ShapeDtypeStruct((images, 8, FRAME), jnp.int32),
            jax.ShapeDtypeStruct((framed, 128), F32),
        ],
        scratch_shapes=[
            pltpu.VMEM((ROWS, HEADS * ROWS), F32), pltpu.VMEM((TABLE, ROWS * ROWS), BF16), pltpu.VMEM((count, D), BF16),
            dma((2,)),
        ],
        compiler_params=params,
        name="forward",
    )(tokens, grad_output, route, source, *vectors, qkv_weight, bias_table.T, hot, masks, out_weight, router)

    copies = lax.axis_size("dp")
    depth = len(strides(copies))
    total = depth + len(strides(members))
    pieces = 2 * local
    share = halvings(CHUNK, depth)[-1][0]
    returned, held, biases = pl.pallas_call(
        partial(experts_kernel, copies, members, local),
        in_specs=[vmem, vmem, pl.BlockSpec(memory_space=pl.ANY), vmem, pl.BlockSpec(memory_space=pl.ANY), vmem],
        out_specs=[vmem] * 3,
        out_shape=[
            jax.ShapeDtypeStruct((members, local, SLOTS, 2 * D), BF16),
            jax.ShapeDtypeStruct((pieces, 2 * share, D), BF16),
            jax.ShapeDtypeStruct((8 * local, D), F32),
        ],
        scratch_shapes=[
            pltpu.VMEM((local, D, FF), BF16),
            pltpu.VMEM((local, FF, D), BF16),
            pltpu.VMEM((local, members, SLOTS, 2 * D), BF16),
            pltpu.VMEM((local, members, SLOTS, 2 * D), BF16),
            pltpu.VMEM((local, members, SLOTS, 2 * D), BF16),
            pltpu.VMEM((local, D, FF), F32),
            pltpu.VMEM((local, D, FF), F32),
            pltpu.VMEM((local, FF), F32),
            pltpu.VMEM((local, D), F32),
            pltpu.VMEM((pieces, CHUNK, D), BF16),
            pltpu.VMEM((8 * local, D), F32),
            pltpu.VMEM((pieces, CHUNK // 2, D), BF16),
            pltpu.VMEM((pieces, landing_rows(CHUNK, depth), D), BF16),
            pltpu.VMEM((pieces, share, D), BF16),
            pltpu.VMEM((depth, 8 * local, D), F32),
            dma((local, members)), dma((local, members)), dma((local, members)), dma((local, members)),
            dma((pieces, depth + 1)), dma((pieces, depth + 1)), dma((depth,)), dma((depth,)), dma((2,)),
        ],
        compiler_params=pltpu.CompilerParams(
            collective_id=1, has_side_effects=True, vmem_limit_bytes=60 * 2**20
        ),
        name="experts",
    )(place, rows, up_weight, up_bias, down_weight, down_bias)
    returned = returned.reshape(EXPERTS * SLOTS, 2 * D)

    output, grad_tokens, chunks, shared, small = pl.pallas_call(
        with_vectors(partial(backward_kernel, copies, members, local), 3),
        grid=(images // PAIR,),
        in_specs=[
            anywhere, whole((count, D)), whole((FRAME, 1)), *[whole((D,))] * len(VECTORS), whole((D, 3 * D)),
            whole((D, D)), whole((EXPERTS, D)), anywhere,
            per_step(SPREAD, 3 * D), per_step(4 * PAIR * GROUPS * ROWS, WIDE), per_step(SPREAD, D), per_step(SPREAD, D),
            per_step(SPREAD, 128), whole((EXPERTS * SLOTS, 2 * D)), anywhere,
        ],
        out_specs=[
            anywhere, anywhere, anywhere, anywhere, whole((32, D)),
        ],
        out_shape=[
            jax.ShapeDtypeStruct((count, D), BF16),
            jax.ShapeDtypeStruct((count, D), F32),
            jax.ShapeDtypeStruct((pieces, CHUNK, D), BF16),
            jax.ShapeDtypeStruct((CHUNK, D), BF16),
            jax.ShapeDtypeStruct((32, D), F32),
        ],
        scratch_shapes=[
            pltpu.VMEM((framed, 3 * D), BF16), pltpu.VMEM((SPREAD, D), BF16), pltpu.VMEM((framed, D), F32),
            pltpu.VMEM((framed, D), BF16),
            pltpu.VMEM((D, 3 * D), F32), pltpu.VMEM((D, D), F32),
            pltpu.VMEM((ROWS, HEADS * ROWS), F32),
            pltpu.VMEM((16, ROWS * ROWS), F32),
            pltpu.VMEM((CHUNK, D), BF16),
            pltpu.VMEM((32, D), F32),
            pltpu.VMEM((PARTS, PART // 2, D), BF16),
            pltpu.VMEM((PARTS, landing_rows(PART, total), D), BF16),
            pltpu.VMEM((PARTS, halvings(PART, total)[-1][0], D), BF16),
            pltpu.VMEM((total, 32, D), F32),
            pltpu.VMEM((pieces, 2 * share, D), BF16),
            pltpu.VMEM((pieces, share, D), BF16),
            pltpu.VMEM((pieces, share, D), BF16),
            pltpu.VMEM((pieces, CHUNK, D), BF16),
            pltpu.VMEM((CHUNK, D), BF16),
            pltpu.VMEM((32, D), F32),
            pltpu.VMEM((count, D), BF16),
            pltpu.VMEM((TABLE, ROWS * ROWS), BF16),
            pltpu.VMEM((count, D), BF16),
            pltpu.VMEM((count, D), F32),
            dma((3,)),
            dma((pieces, depth + 1)), dma((pieces, depth + 1)), dma((PARTS, total)), dma((PARTS, total)),
            dma((PARTS, total)), dma((PARTS, total)), dma((total,)), dma((total,)), dma((pieces, LAST_PARTS)), dma((pieces, LAST_PARTS)),
            dma((pieces + 3,)),
        ],
        compiler_params=pltpu.CompilerParams(
            dimension_semantics=("arbitrary",), collective_id=2, has_side_effects=True, vmem_limit_bytes=60 * 2**20
        ),
        name="backward",
    )(
        tokens, grad_output, source, *vectors, qkv_weight, out_weight, router, hot, projected, weights,
        attended, residual, aux, returned, held,
    )

    results = pl.pallas_call(
        finish_kernel,
        grid=(local, 2),
        in_specs=[
            pl.BlockSpec((1, FF // 2, D), lambda j, t: (2 * j, t, 0)),
            pl.BlockSpec((1, FF // 2, D), lambda j, t: (2 * j + 1, t, 0)),
            whole((8 * local, D)), whole((CHUNK, D)), whole((32, D)),
        ],
        out_specs=[
            pl.BlockSpec((1, D, FF // 2), lambda j, t: (j, 0, t)), pl.BlockSpec((1, FF // 2, D), lambda j, t: (j, t, 0)),
            whole((local, FF)), whole((local, D)), whole((D, 3 * D)), whole((D, D)), whole((EXPERTS, D)),
            whole((HEADS, TABLE)), *[whole((D,))] * 7,
        ],
        out_shape=[
            jax.ShapeDtypeStruct(shape, F32)
            for shape in (
                (local, D, FF), (local, FF, D), (local, FF), (local, D), (D, 3 * D), (D, D), (EXPERTS, D),
                (HEADS, TABLE), *[(D,)] * 7,
            )
        ],
        compiler_params=pltpu.CompilerParams(
            dimension_semantics=("arbitrary", "arbitrary"), vmem_limit_bytes=60 * 2**20
        ),
        name="finish",
    )(chunks, chunks, biases, shared, small)
    grad_up, grad_down, grad_up_bias, grad_down_bias, grad_qkv, grad_out, grad_router, grad_table = results[:8]
    grad_gain1, grad_bias1, grad_q, grad_v, grad_out_bias, grad_gain2, grad_bias2 = results[8:]
    return (
        output, grad_tokens, grad_gain1, grad_bias1, grad_qkv, grad_q, grad_v, grad_table.T, grad_out, grad_out_bias,
        grad_gain2, grad_bias2, grad_router.T, grad_up, grad_up_bias, grad_down, grad_down_bias,
    )


def solution(mesh):
    tokens = P(("dp", "expert"), None)
    expert = P("expert", None, None)
    expert_bias = P("expert", None)
    routes = P(("dp", "expert"))
    return jax.shard_map(
        shards,
        mesh=mesh,
        in_specs=(
            tokens, P(), P(), P(), P(), P(), P(), P(), P(), P(), P(), P(), expert, expert_bias, expert, expert_bias,
            routes, routes, tokens,
        ),
        out_specs=(
            tokens, tokens, P(), P(), P(), P(), P(), P(), P(), P(), P(), P(), P(), expert, expert_bias, expert,
            expert_bias,
        ),
        check_vma=False,
    )
```

```python
from functools import partial

import jax
import jax.numpy as jnp
import numpy as np
from jax import lax
from jax.experimental import pallas as pl
from jax.experimental.pallas import tpu as pltpu
from jax.sharding import PartitionSpec as P

D = 384
HEADS = 12
HEAD = 32
FF = 1536
EXPERTS = 8
WINDOW = 7
SIDE = 14
SHIFT = 3
CAP = 245
CELLS = WINDOW * WINDOW
IMAGE = SIDE * SIDE
TABLE = (2 * WINDOW - 1) ** 2

ROWS = 64
SLOTS = 256
FRAME = 4 * ROWS
SPAN = 208
GROUP = 4
GROUPS = HEADS // GROUP
LANES = GROUP * HEAD
WIDE = GROUP * ROWS

EPSILON = 1e-05
MASK_NEG = -100.0
SCALE = HEAD ** (-0.5)
HIGHEST = lax.Precision.HIGHEST
F32 = jnp.float32
BF16 = jnp.bfloat16


def source_cells():
    source = np.full((FRAME, 1), -1000, np.int32)
    for row in range(FRAME):
        window, cell = divmod(row, ROWS)
        if cell < CELLS:
            down = (window // 2) * WINDOW + cell // WINDOW
            across = (window % 2) * WINDOW + cell % WINDOW
            source[row, 0] = ((down + SHIFT) % SIDE) * SIDE + (across + SHIFT) % SIDE
    return source


def window_masks():
    places = np.arange(SIDE)
    bands = (places >= SIDE - WINDOW).astype(np.int32) + (places >= SIDE - SHIFT)
    masks = np.zeros((4, ROWS, ROWS), np.float32)
    for window in range(4):
        rows = bands[(window // 2) * WINDOW : (window // 2 + 1) * WINDOW]
        cols = bands[(window % 2) * WINDOW : (window % 2 + 1) * WINDOW]
        labels = (rows[:, None] * 3 + cols[None, :]).reshape(-1)
        masks[window, :CELLS, :CELLS] = np.where(labels[:, None] != labels[None, :], MASK_NEG, 0.0)
    masks[:, CELLS:, :] = -1e30
    return np.tile(masks, (1, 1, GROUP))


def offset_onehot():
    hot = np.zeros((TABLE, ROWS, ROWS), np.float32)
    for q in range(CELLS):
        for p in range(CELLS):
            entry = (p // WINDOW - q // WINDOW + WINDOW - 1) * (2 * WINDOW - 1)
            entry += p % WINDOW - q % WINDOW + WINDOW - 1
            hot[entry, q, p] = 1.0
    return hot.reshape(TABLE, ROWS * ROWS)


def mm(left, right):
    return jnp.dot(left, right, preferred_element_type=F32)


def mm_nt(left, right):
    return lax.dot_general(left, right, (((1,), (1,)), ((), ())), preferred_element_type=F32)


def mm_tn(left, right):
    return lax.dot_general(left, right, (((0,), (0,)), ((), ())), preferred_element_type=F32)


def permutation(source, offset, width):
    places = lax.broadcasted_iota(jnp.int32, (FRAME, width), 1)
    return jnp.where(source + offset == places, 1.0, 0.0).astype(BF16)


def normalize(values):
    center = values - jnp.mean(values, axis=-1, keepdims=True)
    inverse = lax.rsqrt(jnp.mean(center * center, axis=-1, keepdims=True) + EPSILON)
    return center * inverse, inverse


def normalize_pull(grad, hat, inverse, gain):
    scaled = grad * gain
    first = jnp.mean(scaled, axis=-1, keepdims=True)
    second = jnp.mean(scaled * hat, axis=-1, keepdims=True)
    return (scaled - first - hat * second) * inverse


def spread_heads(block):
    heads = lax.broadcasted_iota(jnp.int32, block.shape, 1) // HEAD
    return jnp.concatenate(
        [jnp.where(heads == h, block, jnp.zeros_like(block)) for h in range(GROUP)], axis=0
    )


def pick_heads(wide):
    heads = lax.broadcasted_iota(jnp.int32, (ROWS, LANES), 1) // HEAD
    picked = wide[:ROWS]
    for h in range(1, GROUP):
        picked = jnp.where(heads == h, wide[h * ROWS : (h + 1) * ROWS], picked)
    return picked


def image_span(image):
    offset = lax.rem(image * (IMAGE % 16), 16)
    return pl.multiple_of(image * IMAGE - offset, 16), offset


def split_three(values):
    high = values.astype(BF16)
    rest = values - high.astype(F32)
    middle = rest.astype(BF16)
    return high, middle, (rest - middle.astype(F32)).astype(BF16)


VECTORS = ("ln1_gain", "ln1_bias", "q_bias", "v_bias", "out_bias", "ln2_gain", "ln2_bias")


def vector(refs, name):
    return refs[name][...][None, :]


def with_vectors(kernel, at):
    def wrapped(*refs):
        after = at + len(VECTORS)
        return kernel(*refs[:at], dict(zip(VECTORS, refs[at:after])), *refs[after:])

    return wrapped


PAIR = 2
SPREAD = PAIR * FRAME


def orders(step, source):
    found = []
    for k in range(PAIR):
        start, offset = image_span(step * PAIR + k)
        found.append((pl.ds(start, SPAN), permutation(source, offset, SPAN)))
    return found


def arranged(ref, order):
    return jnp.concatenate([mm(hot, ref[rows, :]) for rows, hot in order], axis=0)


def windows_of_step():
    return [(w % 4, slice(w * ROWS, (w + 1) * ROWS)) for w in range(4 * PAIR)]


def group_cols(third, group):
    return slice(third * D + group * LANES, third * D + (group + 1) * LANES)


def forward_kernel(
    tokens_ref, grad_ref, route_ref, source_ref, vectors_ref, qkv_ref, table_ref, hot_ref, mask_ref, out_weight_ref, router_ref,
    projected_ref, weights_ref, attended_ref, residual_ref, rows_ref, place_ref, aux_ref,
    relative, hot_copy, grad_copy, fetches,
):
    fetched = [
        pltpu.make_async_copy(hot_ref, hot_copy, fetches.at[0]), pltpu.make_async_copy(grad_ref, grad_copy, fetches.at[1])
    ]

    @pl.when(pl.program_id(0) == 0)
    def _():
        for copy in fetched:
            copy.start()

    source = source_ref[...]
    order = orders(pl.program_id(0), source)
    inputs = arranged(tokens_ref, order)

    hat, _ = normalize(inputs)
    normed = (hat * vector(vectors_ref, "ln1_gain") + vector(vectors_ref, "ln1_bias")).astype(BF16)
    for third, name in enumerate(("q_bias", "k_bias", "v_bias")):
        at = slice(third * D, (third + 1) * D)
        part = mm(normed, qkv_ref[:, at])
        if name in VECTORS:
            part = part + vector(vectors_ref, name)
        projected_ref[:, at] = part.astype(BF16)

    @pl.when(pl.program_id(0) == 0)
    def _():
        relative[...] = jnp.zeros_like(relative)
        for copy in fetched:
            copy.wait()
        flat = sum(mm(part, hot_copy[...]) for part in split_three(table_ref[...]))
        for q in range(CELLS):
            for h in range(HEADS):
                relative[q : q + 1, h * ROWS : (h + 1) * ROWS] = flat[h : h + 1, q * ROWS : (q + 1) * ROWS]

    for index, (window, rows) in enumerate(windows_of_step()):
        scores = []
        for group in range(GROUPS):
            queries = projected_ref[rows, group_cols(0, group)]
            scores.append(mm_nt(projected_ref[rows, group_cols(1, group)], spread_heads(queries)))
        for group in range(GROUPS):
            wide = slice(group * WIDE, (group + 1) * WIDE)
            full = scores[group] * SCALE + (relative[:, wide] + mask_ref[window])
            powers = jnp.exp(full - jnp.max(full, axis=0, keepdims=True))
            weights = (powers * (1.0 / jnp.sum(powers, axis=0, keepdims=True))).astype(BF16)
            place = (index * GROUPS + group) * ROWS
            weights_ref[place : place + ROWS, :] = weights
            mixed = mm_tn(weights, projected_ref[rows, group_cols(2, group)])
            attended_ref[rows, group_cols(0, group)] = pick_heads(mixed).astype(BF16)

    plain = permutation(source, 0, FRAME)
    chosen_cols, place_cols = [], []
    for k in range(PAIR):
        route = route_ref[k]
        cols = mm_nt(plain, route)
        rows = mm_nt(route, plain)
        place_row = jnp.where(rows[1:2] > 0.5, rows[0:1] * SLOTS + rows[1:2] - 1.0, -1.0)
        place_ref[k] = jnp.broadcast_to(place_row, (8, FRAME)).astype(jnp.int32)
        chosen_cols.append(cols[:, 0:1])
        place_cols.append(jnp.where(cols[:, 1:2] > 0.5, cols[:, 0:1] * SLOTS + cols[:, 1:2] - 1.0, -1.0))
    chosen = jnp.concatenate(chosen_cols, axis=0)

    residual = inputs + (mm(attended_ref[...], out_weight_ref[...]) + vector(vectors_ref, "out_bias"))
    residual_ref[...] = residual
    hat, _ = normalize(residual)
    normed = (hat * vector(vectors_ref, "ln2_gain") + vector(vectors_ref, "ln2_bias")).astype(BF16)
    logits = sum(mm_nt(normed, part) for part in split_three(router_ref[...]))
    logits = jnp.exp(logits - jnp.max(logits, axis=-1, keepdims=True))
    probs = logits / jnp.sum(logits, axis=-1, keepdims=True)
    experts = lax.broadcasted_iota(jnp.int32, (SPREAD, EXPERTS), 1).astype(F32)
    gate = jnp.sum(jnp.where(experts == chosen, probs, 0.0), axis=-1, keepdims=True)
    rows_ref[:, :D] = normed
    rows_ref[:, D:] = (gate * arranged(grad_copy, order)).astype(BF16)
    aux_ref[:, 0:EXPERTS] = probs
    aux_ref[:, EXPERTS : EXPERTS + 1] = gate
    aux_ref[:, EXPERTS + 1 : EXPERTS + 2] = jnp.concatenate(place_cols, axis=0)
    aux_ref[:, EXPERTS + 2 : EXPERTS + 3] = chosen


def backward_kernel(
    copies, members, local, tokens_ref, grad_ref, source_ref, vectors_ref, qkv_ref, out_weight_ref, router_ref, hot_ref,
    projected_ref, weights_ref, attended_ref, residual_ref, aux_ref, returned_ref, held_ref,
    output_ref, grad_tokens_ref, chunks_ref, shared_ref, small_ref,
    grad_projected, grad_attended, grad_residual, outputs, grad_qkv, grad_out, totals, flat, shared, small,
    work, landing, shard, small_landing, held, late_landing, shares, chunks, shared_sum, small_sum,
    tokens, hot_table, output_sum, grad_tokens, fetches,
    chunk_sends, chunk_recvs, scatter_sends, scatter_recvs, gather_sends, gather_recvs, small_sends, small_recvs, part_sends, part_recvs,
    writes,
):
    step = pl.program_id(0)
    steps = IMAGES // PAIR
    everyone = [("expert", s) for s in strides(members)] + copy_bits(copies)[0]
    gathers, late = [], []
    share = shares.shape[1]
    for c, bits in enumerate(chunk_bits(copies, 2 * local)):
        depth = len(bits)
        if c < 2 * (local - 1):
            semaphores = chunk_sends.at[c], chunk_recvs.at[c]
            gathers.append(Gather(held.at[c], chunks.at[c], CHUNK, *semaphores, bits, skip=1))
        else:
            last = chunk_sends.at[c, pl.ds(depth, 1)], chunk_recvs.at[c, pl.ds(depth, 1)]
            scatter = Scatter(held.at[c], shares.at[c], 2 * share, None, late_landing.at[c], *last, bits[-1:])
            semaphores = chunk_sends.at[c], chunk_recvs.at[c]
            gathers.append(Chain(scatter, Gather(shares.at[c], chunks.at[c], CHUNK, *semaphores, bits)))
            late.append(c)
    small_stream = Doubling(small, small_sum, small_landing, small_sends, small_recvs, everyone)
    shared_streams = []
    for part, bits in enumerate(part_bits(copies, members)):
        rows = pl.ds(part * PART, PART)
        scatter = Scatter(
            shared.at[rows], shard.at[part], PART, work.at[part], landing.at[part],
            scatter_sends.at[part], scatter_recvs.at[part], bits,
        )
        gather = Gather(shard.at[part], shared_sum.at[rows], PART, gather_sends.at[part], gather_recvs.at[part], bits)
        shared_streams.append(Chain(scatter, gather))
    runner = Runner()
    plan = {}
    for c, gather in enumerate(gathers):
        for stage, place in enumerate(PLACES.get(gather.steps, ())):
            plan.setdefault(place, []).append((c, stage))
    planned = [pair for pairs in plan.values() for pair in pairs]

    def advance(c, stage):
        if stage:
            gathers[c].finish(stage - 1)
        gathers[c].start(stage)
        gathers[c].settle(stage)

    def last_part(c, part):
        return gathers[c].second.last_part(part, part_sends.at[c], part_recvs.at[c])

    def exchange_at(phase):
        for s in range(steps):
            if due := plan.get(s * PHASES + phase):

                @pl.when(step == s)
                def _(due=due):
                    for c, stage in due:
                        advance(c, stage)

    fetched = [
        pltpu.make_async_copy(source, target, fetches.at[i])
        for i, (source, target) in enumerate(((held_ref, held), (tokens_ref, tokens), (hot_ref, hot_table)))
    ]

    @pl.when(step == 0)
    def _():
        greet([partner(*bit)[1] for bit in everyone])
        for copy in fetched:
            copy.start()
        for ref in (output_sum, grad_tokens, grad_qkv, grad_out, totals, small):
            ref[...] = jnp.zeros_like(ref)
        fetched[0].wait()

    exchange_at(0)
    order = orders(step, source_ref[...])
    upstream = arranged(grad_ref, order)
    residual = residual_ref[...]
    aux = aux_ref[...]
    probs = aux[:, 0:EXPERTS]
    gate = aux[:, EXPERTS : EXPERTS + 1]
    place = aux[:, EXPERTS + 1 : EXPERTS + 2].astype(jnp.int32)
    chosen = aux[:, EXPERTS + 2 : EXPERTS + 3]

    slots = lax.broadcasted_iota(jnp.int32, (SPREAD, EXPERTS * SLOTS), 1)
    hot = jnp.where(slots == place, 1.0, 0.0).astype(BF16)
    gathered = mm(hot, returned_ref[...])
    combined = gathered[:, :D]
    output = (residual + gate * combined).astype(BF16)
    of_step = pl.ds(pl.multiple_of(step * SPREAD, SPREAD), SPREAD)
    outputs[of_step, :] = output

    hat2, inverse2 = normalize(residual)
    normed2 = (hat2 * vector(vectors_ref, "ln2_gain") + vector(vectors_ref, "ln2_bias")).astype(BF16)
    gate_grad = jnp.sum(upstream * combined, axis=-1, keepdims=True)
    experts = lax.broadcasted_iota(jnp.int32, (SPREAD, EXPERTS), 1).astype(F32)
    grad_logits = gate_grad * gate * (jnp.where(experts == chosen, 1.0, 0.0) - probs)
    logits_high, logits_low, _ = split_three(grad_logits)
    small[8:16, :] += mm_tn(logits_high, normed2) + mm_tn(logits_low, normed2)
    router_high, router_low, _ = split_three(router_ref[...])
    grad_normed = (
        gathered[:, D:] + mm(logits_high, router_high) + mm(logits_low, router_high) + mm(logits_high, router_low)
    )
    small[0:1, :] += jnp.sum(grad_normed * hat2, axis=0, keepdims=True)
    small[1:2, :] += jnp.sum(grad_normed, axis=0, keepdims=True)
    grad_mixed = upstream + normalize_pull(grad_normed, hat2, inverse2, vector(vectors_ref, "ln2_gain"))
    grad_residual[of_step, :] = grad_mixed
    grad_mixed = grad_mixed.astype(BF16)
    grad_out[...] += mm_tn(attended_ref[...], grad_mixed)
    small[2:3, :] += jnp.sum(grad_mixed.astype(F32), axis=0, keepdims=True)
    grad_attended[...] = mm_nt(grad_mixed, out_weight_ref[...]).astype(BF16)

    exchange_at(1)
    for index, (_, rows) in enumerate(windows_of_step()):
        if index == 2 * PAIR:
            exchange_at(2)
        out_rows = pl.ds(pl.multiple_of(step * SPREAD + index * ROWS, ROWS), ROWS)
        spread_grads = [spread_heads(grad_attended[rows, group_cols(0, g)]) for g in range(GROUPS)]
        grad_weights = [
            mm_nt(projected_ref[rows, group_cols(2, g)], spread_grads[g]) for g in range(GROUPS)
        ]
        for g in range(GROUPS):
            at = (index * GROUPS + g) * ROWS
            weights = weights_ref[at : at + ROWS, :]
            exact = weights.astype(F32)
            scores = exact * (grad_weights[g] - jnp.sum(exact * grad_weights[g], axis=0, keepdims=True))
            scores = scores.astype(BF16)
            totals[:, g * WIDE : (g + 1) * WIDE] += scores.astype(F32)
            grad_projected[out_rows, group_cols(2, g)] = mm(weights, spread_grads[g]).astype(BF16)
            grad_keys = mm(scores, spread_heads(projected_ref[rows, group_cols(0, g)]))
            grad_projected[out_rows, group_cols(1, g)] = (grad_keys * SCALE).astype(BF16)
            grad_queries = pick_heads(mm_tn(scores, projected_ref[rows, group_cols(1, g)]))
            grad_projected[out_rows, group_cols(0, g)] = (grad_queries * SCALE).astype(BF16)

    exchange_at(3)

    @pl.when(step == 0)
    def _():
        for copy in fetched[1:]:
            copy.wait()

    grads = grad_projected[of_step, :]
    hat1, _ = normalize(arranged(tokens, order))
    normed1 = (hat1 * vector(vectors_ref, "ln1_gain") + vector(vectors_ref, "ln1_bias")).astype(BF16)
    grad_qkv[...] += mm_tn(normed1, grads)
    column_sums = jnp.sum(grads.astype(F32), axis=0, keepdims=True)
    for third in range(3):
        small[5 + third : 6 + third, :] += column_sums[:, third * D : (third + 1) * D]

    def first_norm_back(step):
        of_step = slice(step * SPREAD, (step + 1) * SPREAD)
        order = orders(step, source_ref[...])
        hat, inverse = normalize(arranged(tokens, order))
        grad_normed = mm_nt(grad_projected[of_step, :], qkv_ref[...])
        pulled = normalize_pull(grad_normed, hat, inverse, vector(vectors_ref, "ln1_gain"))
        high, low, _ = split_three(grad_residual[of_step, :] + pulled)
        for k, (rows, hot) in enumerate(order):
            of_image = slice(k * FRAME, (k + 1) * FRAME)
            grad_tokens[rows, :] += mm_tn(hot, high[of_image]) + mm_tn(hot, low[of_image])
            output_sum[rows, :] += mm_tn(hot, outputs[of_step, :][of_image]).astype(BF16)

    def first_norm_sums():
        ones = jnp.ones((8, D), BF16)
        of_bias = of_normed = 0.0
        for third in range(3):
            at = slice(third * D, (third + 1) * D)
            weight = qkv_ref[:, at]
            sums = jnp.broadcast_to(small[5 + third : 6 + third, :], (8, D))
            of_bias += sum(mm_nt(part, weight) for part in split_three(sums))
            of_normed += sum(mm_nt(ones, part) for part in split_three(weight.astype(F32) * grad_qkv[:, at]))
        of_bias, of_normed = of_bias[0:1], of_normed[0:1]
        shift = vector(vectors_ref, "ln1_bias") * of_bias
        small[3:4, :] = (of_normed - shift) / vector(vectors_ref, "ln1_gain")
        small[4:5, :] = of_bias

    @pl.when(step == steps - 1)
    def _():
        for third in range(3):
            at = slice(third * D, (third + 1) * D)
            shared[at, :] = grad_qkv[:, at].astype(BF16)
        shared[3 * D :, :] = grad_out[...].astype(BF16)
        runner.advance(*shared_streams)
        flat[...] = jnp.zeros_like(flat)
        for q in range(CELLS):
            for h in range(HEADS):
                flat[h : h + 1, q * ROWS : (q + 1) * ROWS] = totals[q : q + 1, h * ROWS : (h + 1) * ROWS]
        table = sum(mm_nt(part, hot_table[...]) for part in split_three(flat[...]))
        small[16:32, : table.shape[1]] = table
        first_norm_sums()
        runner.advance(small_stream)
        for c, gather in enumerate(gathers):
            for stage in range(gather.steps - (c in late)):
                if (c, stage) not in planned:
                    advance(c, stage)
        for c in late:
            gathers[c].finish(gathers[c].steps - 2)
        for done in range(max(steps, LAST_PARTS)):
            if done < LAST_PARTS:
                for c in late:
                    last_part(c, done).start()
            if done < steps:
                first_norm_back(done)
            runner.advance(small_stream, *shared_streams)
        copies_out = [
            pltpu.make_async_copy(output_sum, output_ref, writes.at[len(gathers) + 1]),
            pltpu.make_async_copy(grad_tokens, grad_tokens_ref, writes.at[len(gathers) + 2]),
        ]
        for c, gather in enumerate(gathers):
            if c not in late:
                gather.finish(gather.steps - 1)
                copies_out.append(pltpu.make_async_copy(chunks.at[c], chunks_ref.at[c], writes.at[c]))
        for copy in copies_out:
            copy.start()
        runner.complete(*shared_streams, small_stream)
        small_ref[...] = small_sum[...]
        ends = [pltpu.make_async_copy(shared_sum, shared_ref, writes.at[len(gathers)])]
        for c in late:
            for part in range(LAST_PARTS):
                last_part(c, part).wait()
            ends.append(pltpu.make_async_copy(chunks.at[c], chunks_ref.at[c], writes.at[c]))
        for copy in ends:
            copy.start()
        copies_out += ends
        for copy in copies_out:
            copy.wait()


PHASES = 4


PLACES = {2: (0, 7), 4: (0, 8, 14), 6: (0, 5, 8, 10, 12)}


IMAGES = 8
CHUNK = 4 * D
PARTS = 3
PART = CHUNK // PARTS
LAST_PARTS = 4
MESH = pl.DeviceIdType.MESH


def add_rows(left, left_at, right, rights_at, out, out_at, count):
    step = next(s for s in (64, 48, 32, 16) if count % s == 0)

    def body(i, carry):
        here = i * step
        total = left[pl.ds(pl.multiple_of(left_at + here, 16), step), :].astype(F32)
        for right_at in rights_at:
            total = total + right[pl.ds(pl.multiple_of(right_at + here, 16), step), :].astype(F32)
        out[pl.ds(pl.multiple_of(out_at + here, 16), step), :] = total.astype(out.dtype)
        return carry

    lax.fori_loop(0, count // step, body, 0)


def partner(axis, stride):
    index = lax.axis_index(axis)
    bit = lax.rem(lax.div(index, stride), 2)
    return bit, {axis: index + stride - 2 * stride * bit}


def neighbours(group):
    place, others = 0, []
    for axis, stride in group:
        place = 2 * place + partner(axis, stride)[0]
    for flips in range(1, 2 ** len(group)):
        other, device = 0, {}
        for i, (axis, stride) in enumerate(group):
            bit = partner(axis, stride)[0]
            flip = flips >> i & 1
            other = 2 * other + (1 - bit if flip else bit)
            index = device.get(axis, lax.axis_index(axis))
            device[axis] = index + stride - 2 * stride * bit if flip else index
        others.append((other, device))
    return place, others


def stages_of(rows, bits):
    stages = []
    for item in bits:
        if isinstance(item, list) and rows % 64 == 0:
            rows //= 4
            stages.append((item, rows, True))
            continue
        for bit in item if isinstance(item, list) else [item]:
            halved = rows % 32 == 0
            rows = rows // 2 if halved else rows
            stages.append(([bit], rows, halved))
    return stages


def kept_rows(rows, bits):
    return stages_of(rows, bits)[-1][1]


def landing_rows(rows, bits):
    return sum(size * (2 ** len(group) - 1) for group, size, _ in stages_of(rows, bits))


def copies_of(bits):
    return sum(3 if isinstance(item, list) else 1 for item in bits)


def exchange(src, dst, sends, recvs, step, device):
    return pltpu.make_async_remote_copy(
        src_ref=src, dst_ref=dst, send_sem=sends.at[step], recv_sem=recvs.at[step], device_id=device, device_id_type=MESH
    )


def rows_at(ref, start, size):
    return ref.at[pl.ds(pl.multiple_of(start, 16), size)]


class Scatter:
    def __init__(self, source, out, rows, work, landing, sends, recvs, bits):
        self.source, self.out, self.work, self.landing = source, out, work, landing
        self.sends, self.recvs = sends, recvs
        self.plan = []
        at = land = semaphore = 0
        for step, (group, size, shared) in enumerate(stages_of(rows, bits)):
            place, others = neighbours(group)
            keep = at + place * size if shared else at
            copies = []
            for other, device in others:
                copies.append((at + other * size if shared else at, land, semaphore, device))
                land, semaphore = land + size, semaphore + 1
            self.plan.append((keep, size, copies))
            at = keep if step else 0
        self.steps = len(self.plan)

    def copies(self, step):
        _, size, copies = self.plan[step]
        mine = self.work if step else self.source
        return [
            exchange(
                rows_at(mine, give, size), self.landing.at[pl.ds(land, size)], self.sends, self.recvs, semaphore, device
            )
            for give, land, semaphore, device in copies
        ]

    def add(self, step, start, size):
        keep, _, copies = self.plan[step]
        mine = self.work if step else self.source
        if step == self.steps - 1:
            out, out_at = self.out, 0
        else:
            out, out_at = self.work, keep if step else 0
        landings = [land + start for _, land, _, _ in copies]
        add_rows(mine, keep + start, self.landing, landings, out, out_at + start, size)

    def splits(self, step):
        return 0 <= step < self.steps - 1 and 2 * self.plan[step + 1][1] == self.plan[step][1]

    def start(self, step):
        for copy in self.copies(step):
            copy.start()

    def settle(self, step):
        if self.splits(step - 1):
            keep, size, _ = self.plan[step]
            self.add(step - 1, keep - (self.plan[step - 1][0] if step > 1 else 0), size)

    def finish(self, step):
        for copy in self.copies(step):
            copy.wait()
        if self.splits(step):
            _, size, copies = self.plan[step + 1]
            self.add(step, copies[0][0] - (self.plan[step][0] if step else 0), size)
        else:
            self.add(step, 0, self.plan[step][1])


class Gather:
    def __init__(self, share, out, rows, sends, recvs, bits, skip=0):
        self.share, self.out, self.sends, self.recvs = share, out, sends, recvs
        self.plan = []
        start = 0
        for group, size, shared in stages_of(rows, bits):
            place, others = neighbours(group)
            start = start + place * size if shared else start
            if shared:
                self.plan.insert(0, (start, size, [device for _, device in others]))
        self.plan = self.plan[skip:]
        self.steps = len(self.plan)

    def copies(self, step):
        start, size, devices = self.plan[step]
        first = sum(len(others) for _, _, others in self.plan[:step])
        rows = rows_at(self.out, start, size)
        return [
            exchange(rows, rows, self.sends, self.recvs, first + i, device) for i, device in enumerate(devices)
        ]

    def last_part(self, part, sends, recvs):
        start, size, (device,) = self.plan[-1]
        size = size // LAST_PARTS
        rows = rows_at(self.out, start + part * size, size)
        return exchange(rows, rows, sends, recvs, part, device)

    def start(self, step):
        if step == 0:
            start, size, _ = self.plan[0]
            self.out[pl.ds(pl.multiple_of(start, 16), size), :] = self.share[...]
        for copy in self.copies(step):
            copy.start()

    def settle(self, step):
        pass

    def finish(self, step):
        for copy in self.copies(step):
            copy.wait()


class Chain:
    def __init__(self, first, second):
        self.first, self.second, self.steps = first, second, first.steps + second.steps

    def of(self, step):
        return (self.first, step) if step < self.first.steps else (self.second, step - self.first.steps)

    def start(self, step):
        stream, step = self.of(step)
        stream.start(step)

    def settle(self, step):
        stream, step = self.of(step)
        stream.settle(step)

    def finish(self, step):
        stream, step = self.of(step)
        stream.finish(step)


class Doubling:
    def __init__(self, source, out, landing, sends, recvs, bits):
        self.source, self.out, self.landing = source, out, landing
        self.sends, self.recvs, self.bits = sends, recvs, bits
        self.steps = len(bits)

    def copy(self, step):
        device = partner(*self.bits[step])[1]
        return exchange(self.out, self.landing.at[step], self.sends, self.recvs, step, device)

    def start(self, step):
        if step == 0:
            self.out[...] = self.source[...]
        self.copy(step).start()

    def settle(self, step):
        pass

    def finish(self, step):
        self.copy(step).wait()
        self.out[...] = self.out[...] + self.landing[step]


class Runner:
    def __init__(self):
        self.at = {}

    def advance(self, *streams):
        begun = []
        for stream in streams:
            step = self.at.get(stream, -1)
            if step < stream.steps:
                if step >= 0:
                    stream.finish(step)
                self.at[stream] = step = step + 1
                if step < stream.steps:
                    stream.start(step)
                    begun.append((stream, step))
        for stream, step in begun:
            stream.settle(step)

    def complete(self, *streams):
        while any(self.at.get(s, -1) < s.steps for s in streams):
            self.advance(*streams)


def strides(size):
    return [2**k for k in range(size.bit_length() - 1)]


def copy_bits(copies):
    low = len(strides(copies)) // 2
    all_bits = [("dp", s) for s in strides(copies)]
    return all_bits, all_bits[low : low + 1] + all_bits[:low] + all_bits[low + 1 :]


def part_bits(copies, members):
    chips = [("expert", s) for s in strides(members)]
    bits = copy_bits(copies)[0]
    rest = [*chips[1:], *bits[:-2], bits[-2:]]
    turns = [part * len(rest) // PARTS for part in range(PARTS)]
    return [chips[:1] + rest[turn:] + rest[:turn] for turn in turns]


def chunk_bits(copies, count):
    first, second = copy_bits(copies)
    return [second if c % 2 else first for c in range(count)]


def greet(devices):
    barrier = pltpu.get_barrier_semaphore()
    for device in devices:
        pl.semaphore_signal(barrier, inc=1, device_id=device, device_id_type=MESH)
    pl.semaphore_wait(barrier, len(devices))


def member_at(members, hop, sign):
    index = lax.axis_index("expert")
    chips = members // 2
    chip = lax.rem(lax.div(index, 2) + sign * (hop // 2) + chips, chips)
    return chip * 2 + lax.rem(lax.rem(index, 2) + hop % 2, 2)


TILE = 512


def experts_kernel(
    copies, members, local, place_ref, rows_ref, up_ref, up_bias_ref, down_ref, down_bias_ref,
    returned_ref, held_ref, biases_ref,
    up, down, outbox, inbox, results, up_sum, down_sum, up_bias_sum, down_bias_sum, chunks, biases, work, landing, shares,
    bias_landing,
    out_sends, out_recvs, back_sends, back_recvs, chunk_sends, chunk_recvs, bias_sends, bias_recvs, fetches,
):
    me = lax.axis_index("expert")
    fetched = [
        pltpu.make_async_copy(up_ref, up, fetches.at[0]), pltpu.make_async_copy(down_ref, down, fetches.at[1])
    ]
    for copy in fetched:
        copy.start()
    bits = chunk_bits(copies, 2 * local)
    greet(
        [{"expert": member_at(members, hop, 1)} for hop in range(1, members)]
        + [partner(*bit)[1] for bit in copy_bits(copies)[0]]
    )
    places = jnp.concatenate([place_ref[i, 0:1, :] for i in range(place_ref.shape[0])], axis=1)

    def out_copy(hop, j):
        return pltpu.make_async_remote_copy(
            src_ref=outbox.at[j, hop], dst_ref=inbox.at[j, hop],
            send_sem=out_sends.at[j, hop], recv_sem=out_recvs.at[j, hop],
            device_id={"expert": member_at(members, hop, 1)}, device_id_type=MESH,
        )

    def back_copy(hop, j):
        return pltpu.make_async_remote_copy(
            src_ref=results.at[j, hop], dst_ref=returned_ref.at[me, j],
            send_sem=back_sends.at[j, hop], recv_sem=back_recvs.at[j, hop],
            device_id={"expert": member_at(members, hop, -1)}, device_id_type=MESH,
        )

    def dispatch(hop, j):
        expert = member_at(members, hop, 1) * local + j
        slots = lax.broadcasted_iota(jnp.int32, (SLOTS, places.shape[1]), 0) + expert * SLOTS
        hot = jnp.where(slots == places, 1.0, 0.0).astype(BF16)
        return mm(hot, rows_ref[...]).astype(BF16)

    order = [(hop, j) for j in range(local) for hop in range(members - 1, 1, -1)]
    order += [(hop, j) for j in range(local) for hop in (1, 0)]
    for hop, j in order:
        if hop:
            outbox[j, hop] = dispatch(hop, j)
            if hop == 1 or j == 0:
                out_copy(hop, j).start()
        else:
            inbox[j, 0] = dispatch(0, j)

    for copy in fetched:
        copy.wait()
    up_sum[...] = jnp.zeros_like(up_sum)
    down_sum[...] = jnp.zeros_like(down_sum)
    up_bias_sum[...] = jnp.zeros_like(up_bias_sum)
    down_bias_sum[...] = jnp.zeros_like(down_bias_sum)

    def compute(pair, j):
        hops = (2 * pair, 2 * pair + 1)
        for hop in hops:
            if hop:
                out_copy(hop, j).wait_recv()
        inputs = inbox[j, 2 * pair : 2 * pair + 2, :, :D].reshape(2 * SLOTS, D)
        grads = inbox[j, 2 * pair : 2 * pair + 2, :, D:].reshape(2 * SLOTS, D)
        inputs_t = inputs.T
        grads_t = grads.T
        outs = jnp.zeros((2 * SLOTS, D), F32)
        backs = jnp.zeros((2 * SLOTS, D), F32)
        for tile in range(FF // TILE):
            at = slice(tile * TILE, (tile + 1) * TILE)
            pre = mm(inputs, up[j, :, at]) + up_bias_ref[j : j + 1, at]
            grad_hidden = mm_nt(grads, down[j, at, :])
            share = 0.5 + 0.5 * lax.erf(pre * 0.7071067811865476)
            density = jnp.exp(pre * pre * -0.5) * 0.3989422804014327
            hidden = (pre * share).astype(BF16)
            grad_pre = (grad_hidden * (share + pre * density)).astype(BF16)
            outs += mm(hidden, down[j, at, :])
            backs += mm_nt(grad_pre, up[j, :, at])
            down_sum[j, :, at] += mm(grads_t, hidden)
            up_sum[j, :, at] += mm(inputs_t, grad_pre)
            up_bias_sum[j : j + 1, at] += jnp.sum(grad_pre.astype(F32), axis=0, keepdims=True)
        down_bias_sum[j : j + 1, :] += jnp.sum(grads.astype(F32), axis=0, keepdims=True)
        results[j, 2 * pair : 2 * pair + 2, :, :D] = (
            (outs + down_bias_ref[j : j + 1, :]).astype(BF16).reshape(2, SLOTS, D)
        )
        results[j, 2 * pair : 2 * pair + 2, :, D:] = backs.astype(BF16).reshape(2, SLOTS, D)
        if pair == 0:
            returned_ref[me, j] = results[j, 0]
            back_copy(1, j).start()

    def seal(j):
        for tile in range(FF // D):
            at = slice(tile * D, (tile + 1) * D)
            chunks[2 * j, at, :] = up_sum[j, :, at].astype(BF16)
            chunks[2 * j + 1, at, :] = down_sum[j, :, at].T.astype(BF16)
            biases[8 * j + tile : 8 * j + tile + 1, :] = up_bias_sum[j : j + 1, at]
        biases[8 * j + 4 : 8 * j + 5, :] = down_bias_sum[j : j + 1, :]
        biases[8 * j + 5 : 8 * j + 8, :] = jnp.zeros((3, D), F32)

    streams = []
    for c in range(2 * local):
        early = c < 2 * (local - 1)
        parts = chunks.at[c], shares.at[c] if early else held_ref.at[c], CHUNK, work.at[c], landing.at[c]
        semaphores = chunk_sends.at[c], chunk_recvs.at[c]
        if early:
            depth, share = len(bits[c]), shares.shape[1]
            semaphores_back = chunk_sends.at[c, pl.ds(depth, 1)], chunk_recvs.at[c, pl.ds(depth, 1)]
            back = Gather(shares.at[c], held_ref.at[c], 2 * share, *semaphores_back, bits[c][-1:])
            streams.append(Chain(Scatter(*parts, *semaphores, bits[c]), back))
        else:
            streams.append(Scatter(*parts, *semaphores, bits[c][:-1]))
    runner = Runner()
    far = range(2, members)
    for j in range(local):
        compute(0, j)
        for hop in far:
            out_copy(hop, j).wait_send()
        for hop in far:
            if j + 1 < local:
                out_copy(hop, j + 1).start()
            else:
                for held in range(j):
                    back_copy(hop, held).start()
        for pair in range(1, members // 2):
            compute(pair, j)
        if j == local - 1:
            for hop in far:
                back_copy(hop, j).start()
        seal(j)
        if j < local - 1:
            runner.advance(*streams[2 * j : 2 * j + 2])
    small = Doubling(biases, biases_ref, bias_landing, bias_sends, bias_recvs, copy_bits(copies)[0])
    early, late = streams[: 2 * (local - 1)], streams[2 * (local - 1) :]
    for turn in (early, early, late, early, late, early):
        runner.advance(small, *turn)
    runner.complete(small, *early, *late)
    for j in range(local):
        out_copy(1, j).wait_send()
        for hop in range(1, members):
            back_copy(hop, j).wait()


def finish_kernel(
    up_tile_ref, down_tile_ref, biases_ref, shared_ref, small_ref,
    up_ref, down_ref, up_bias_ref, down_bias_ref, qkv_ref, out_ref, router_ref, table_ref, *vector_refs,
):
    for tile in range(up_tile_ref.shape[1] // D):
        at = slice(tile * D, (tile + 1) * D)
        up_ref[0, :, at] = up_tile_ref[0, at, :].astype(F32)
    down_ref[0] = down_tile_ref[0].astype(F32)

    @pl.when((pl.program_id(0) == 0) & (pl.program_id(1) == 0))
    def _():
        for j in range(up_bias_ref.shape[0]):
            for tile in range(FF // D):
                row = 8 * j + tile
                up_bias_ref[j : j + 1, tile * D : (tile + 1) * D] = biases_ref[row : row + 1, :]
            down_bias_ref[j : j + 1, :] = biases_ref[8 * j + 4 : 8 * j + 5, :]
        for third in range(3):
            at = slice(third * D, (third + 1) * D)
            qkv_ref[:, at] = shared_ref[at, :].astype(F32)
        out_ref[...] = shared_ref[3 * D :, :].astype(F32)
        router_ref[...] = small_ref[8:16, :]
        table_ref[...] = small_ref[16 : 16 + HEADS, :TABLE]
        for ref, row in zip(vector_refs, (3, 4, 5, 7, 2, 0, 1)):
            ref[...] = small_ref[row, :]


def whole(shape):
    return pl.BlockSpec(shape, lambda *_: (0,) * len(shape))


def per_step(rows, columns):
    return pl.BlockSpec((rows, columns), lambda i: (i, 0))


def shards(
    tokens, ln1_gain, ln1_bias, qkv_weight, q_bias, v_bias, bias_table, out_weight, out_bias, ln2_gain, ln2_bias,
    router_weight, up_weight, up_bias, down_weight, down_bias, expert_of, slot_of, grad_output,
):
    members = lax.axis_size("expert")
    local = up_weight.shape[0]
    count = tokens.shape[0]
    images = count // IMAGE
    framed = images * FRAME
    params = pltpu.CompilerParams(dimension_semantics=("arbitrary",), vmem_limit_bytes=60 * 2**20)

    source = jnp.asarray(source_cells())
    masks = jnp.asarray(window_masks())
    hot = jnp.asarray(offset_onehot().astype(BF16))
    route = jnp.stack([expert_of, slot_of + 1]).astype(BF16).reshape(2, images, IMAGE).transpose(1, 0, 2)
    route = jnp.pad(route, ((0, 0), (0, 6), (0, FRAME - IMAGE)))
    vectors = (ln1_gain, ln1_bias, q_bias, v_bias, out_bias, ln2_gain, ln2_bias)
    router = router_weight.T
    vmem = pl.BlockSpec(memory_space=pltpu.VMEM)
    anywhere = pl.BlockSpec(memory_space=pl.ANY)
    dma = pltpu.SemaphoreType.DMA

    projected, weights, attended, residual, rows, place, aux = pl.pallas_call(
        with_vectors(forward_kernel, 4),
        grid=(images // PAIR,),
        in_specs=[
            whole((count, D)), anywhere, pl.BlockSpec((PAIR, 8, FRAME), lambda i: (i, 0, 0)),
            whole((FRAME, 1)), *[whole((D,))] * len(VECTORS), whole((D, 3 * D)), whole((HEADS, TABLE)), anywhere,
            whole((4, ROWS, WIDE)), whole((D, D)), whole((EXPERTS, D)),
        ],
        out_specs=[
            per_step(SPREAD, 3 * D), per_step(4 * PAIR * GROUPS * ROWS, WIDE), per_step(SPREAD, D), per_step(SPREAD, D),
            per_step(SPREAD, 2 * D), pl.BlockSpec((PAIR, 8, FRAME), lambda i: (i, 0, 0)), per_step(SPREAD, 128),
        ],
        out_shape=[
            jax.ShapeDtypeStruct((framed, 3 * D), BF16),
            jax.ShapeDtypeStruct((images * 4 * GROUPS * ROWS, WIDE), BF16),
            jax.ShapeDtypeStruct((framed, D), BF16),
            jax.ShapeDtypeStruct((framed, D), F32),
            jax.ShapeDtypeStruct((framed, 2 * D), BF16),
            jax.ShapeDtypeStruct((images, 8, FRAME), jnp.int32),
            jax.ShapeDtypeStruct((framed, 128), F32),
        ],
        scratch_shapes=[
            pltpu.VMEM((ROWS, HEADS * ROWS), F32), pltpu.VMEM((TABLE, ROWS * ROWS), BF16), pltpu.VMEM((count, D), BF16),
            dma((2,)),
        ],
        compiler_params=params,
        name="forward",
    )(tokens, grad_output, route, source, *vectors, qkv_weight, bias_table.T, hot, masks, out_weight, router)

    copies = lax.axis_size("dp")
    depth = len(strides(copies))
    total = depth + len(strides(members))
    pieces = 2 * local
    share = kept_rows(CHUNK, copy_bits(copies)[0])
    paths = part_bits(copies, members)
    moves = max(copies_of(path) for path in paths)
    returned, held, biases = pl.pallas_call(
        partial(experts_kernel, copies, members, local),
        in_specs=[vmem, vmem, pl.BlockSpec(memory_space=pl.ANY), vmem, pl.BlockSpec(memory_space=pl.ANY), vmem],
        out_specs=[vmem] * 3,
        out_shape=[
            jax.ShapeDtypeStruct((members, local, SLOTS, 2 * D), BF16),
            jax.ShapeDtypeStruct((pieces, 2 * share, D), BF16),
            jax.ShapeDtypeStruct((8 * local, D), F32),
        ],
        scratch_shapes=[
            pltpu.VMEM((local, D, FF), BF16),
            pltpu.VMEM((local, FF, D), BF16),
            pltpu.VMEM((local, members, SLOTS, 2 * D), BF16),
            pltpu.VMEM((local, members, SLOTS, 2 * D), BF16),
            pltpu.VMEM((local, members, SLOTS, 2 * D), BF16),
            pltpu.VMEM((local, D, FF), F32),
            pltpu.VMEM((local, D, FF), F32),
            pltpu.VMEM((local, FF), F32),
            pltpu.VMEM((local, D), F32),
            pltpu.VMEM((pieces, CHUNK, D), BF16),
            pltpu.VMEM((8 * local, D), F32),
            pltpu.VMEM((pieces, CHUNK // 2, D), BF16),
            pltpu.VMEM((pieces, landing_rows(CHUNK, copy_bits(copies)[0]), D), BF16),
            pltpu.VMEM((pieces, share, D), BF16),
            pltpu.VMEM((depth, 8 * local, D), F32),
            dma((local, members)), dma((local, members)), dma((local, members)), dma((local, members)),
            dma((pieces, depth + 1)), dma((pieces, depth + 1)), dma((depth,)), dma((depth,)), dma((2,)),
        ],
        compiler_params=pltpu.CompilerParams(
            collective_id=1, has_side_effects=True, vmem_limit_bytes=60 * 2**20
        ),
        name="experts",
    )(place, rows, up_weight, up_bias, down_weight, down_bias)
    returned = returned.reshape(EXPERTS * SLOTS, 2 * D)

    output, grad_tokens, chunks, shared, small = pl.pallas_call(
        with_vectors(partial(backward_kernel, copies, members, local), 3),
        grid=(images // PAIR,),
        in_specs=[
            anywhere, whole((count, D)), whole((FRAME, 1)), *[whole((D,))] * len(VECTORS), whole((D, 3 * D)),
            whole((D, D)), whole((EXPERTS, D)), anywhere,
            per_step(SPREAD, 3 * D), per_step(4 * PAIR * GROUPS * ROWS, WIDE), per_step(SPREAD, D), per_step(SPREAD, D),
            per_step(SPREAD, 128), whole((EXPERTS * SLOTS, 2 * D)), anywhere,
        ],
        out_specs=[
            anywhere, anywhere, anywhere, anywhere, whole((32, D)),
        ],
        out_shape=[
            jax.ShapeDtypeStruct((count, D), BF16),
            jax.ShapeDtypeStruct((count, D), F32),
            jax.ShapeDtypeStruct((pieces, CHUNK, D), BF16),
            jax.ShapeDtypeStruct((CHUNK, D), BF16),
            jax.ShapeDtypeStruct((32, D), F32),
        ],
        scratch_shapes=[
            pltpu.VMEM((framed, 3 * D), BF16), pltpu.VMEM((SPREAD, D), BF16), pltpu.VMEM((framed, D), F32),
            pltpu.VMEM((framed, D), BF16),
            pltpu.VMEM((D, 3 * D), F32), pltpu.VMEM((D, D), F32),
            pltpu.VMEM((ROWS, HEADS * ROWS), F32),
            pltpu.VMEM((16, ROWS * ROWS), F32),
            pltpu.VMEM((CHUNK, D), BF16),
            pltpu.VMEM((32, D), F32),
            pltpu.VMEM((PARTS, PART // 2, D), BF16),
            pltpu.VMEM((PARTS, max(landing_rows(PART, path) for path in paths), D), BF16),
            pltpu.VMEM((PARTS, kept_rows(PART, paths[0]), D), BF16),
            pltpu.VMEM((total, 32, D), F32),
            pltpu.VMEM((pieces, 2 * share, D), BF16),
            pltpu.VMEM((pieces, share, D), BF16),
            pltpu.VMEM((pieces, share, D), BF16),
            pltpu.VMEM((pieces, CHUNK, D), BF16),
            pltpu.VMEM((CHUNK, D), BF16),
            pltpu.VMEM((32, D), F32),
            pltpu.VMEM((count, D), BF16),
            pltpu.VMEM((TABLE, ROWS * ROWS), BF16),
            pltpu.VMEM((count, D), BF16),
            pltpu.VMEM((count, D), F32),
            dma((3,)),
            dma((pieces, depth + 1)), dma((pieces, depth + 1)), dma((PARTS, moves)), dma((PARTS, moves)),
            dma((PARTS, moves)), dma((PARTS, moves)), dma((total,)), dma((total,)), dma((pieces, LAST_PARTS)), dma((pieces, LAST_PARTS)),
            dma((pieces + 3,)),
        ],
        compiler_params=pltpu.CompilerParams(
            dimension_semantics=("arbitrary",), collective_id=2, has_side_effects=True, vmem_limit_bytes=60 * 2**20
        ),
        name="backward",
    )(
        tokens, grad_output, source, *vectors, qkv_weight, out_weight, router, hot, projected, weights,
        attended, residual, aux, returned, held,
    )

    results = pl.pallas_call(
        finish_kernel,
        grid=(local, 2),
        in_specs=[
            pl.BlockSpec((1, FF // 2, D), lambda j, t: (2 * j, t, 0)),
            pl.BlockSpec((1, FF // 2, D), lambda j, t: (2 * j + 1, t, 0)),
            whole((8 * local, D)), whole((CHUNK, D)), whole((32, D)),
        ],
        out_specs=[
            pl.BlockSpec((1, D, FF // 2), lambda j, t: (j, 0, t)), pl.BlockSpec((1, FF // 2, D), lambda j, t: (j, t, 0)),
            whole((local, FF)), whole((local, D)), whole((D, 3 * D)), whole((D, D)), whole((EXPERTS, D)),
            whole((HEADS, TABLE)), *[whole((D,))] * 7,
        ],
        out_shape=[
            jax.ShapeDtypeStruct(shape, F32)
            for shape in (
                (local, D, FF), (local, FF, D), (local, FF), (local, D), (D, 3 * D), (D, D), (EXPERTS, D),
                (HEADS, TABLE), *[(D,)] * 7,
            )
        ],
        compiler_params=pltpu.CompilerParams(
            dimension_semantics=("arbitrary", "arbitrary"), vmem_limit_bytes=60 * 2**20
        ),
        name="finish",
    )(chunks, chunks, biases, shared, small)
    grad_up, grad_down, grad_up_bias, grad_down_bias, grad_qkv, grad_out, grad_router, grad_table = results[:8]
    grad_gain1, grad_bias1, grad_q, grad_v, grad_out_bias, grad_gain2, grad_bias2 = results[8:]
    return (
        output, grad_tokens, grad_gain1, grad_bias1, grad_qkv, grad_q, grad_v, grad_table.T, grad_out, grad_out_bias,
        grad_gain2, grad_bias2, grad_router.T, grad_up, grad_up_bias, grad_down, grad_down_bias,
    )


def solution(mesh):
    tokens = P(("dp", "expert"), None)
    expert = P("expert", None, None)
    expert_bias = P("expert", None)
    routes = P(("dp", "expert"))
    return jax.shard_map(
        shards,
        mesh=mesh,
        in_specs=(
            tokens, P(), P(), P(), P(), P(), P(), P(), P(), P(), P(), P(), expert, expert_bias, expert, expert_bias,
            routes, routes, tokens,
        ),
        out_specs=(
            tokens, tokens, P(), P(), P(), P(), P(), P(), P(), P(), P(), P(), P(), expert, expert_bias, expert,
            expert_bias,
        ),
        check_vma=False,
    )
```

```python
from functools import partial

import jax
import jax.numpy as jnp
import numpy as np
from jax import lax
from jax.experimental import pallas as pl
from jax.experimental.pallas import tpu as pltpu
from jax.sharding import PartitionSpec as P

D = 384
HEADS = 12
HEAD = 32
FF = 1536
EXPERTS = 8
WINDOW = 7
SIDE = 14
SHIFT = 3
CAP = 245
CELLS = WINDOW * WINDOW
IMAGE = SIDE * SIDE
TABLE = (2 * WINDOW - 1) ** 2

ROWS = 64
SLOTS = 256
FRAME = 4 * ROWS
SPAN = 208
GROUP = 4
GROUPS = HEADS // GROUP
LANES = GROUP * HEAD
WIDE = GROUP * ROWS

EPSILON = 1e-05
MASK_NEG = -100.0
SCALE = HEAD ** (-0.5)
HIGHEST = lax.Precision.HIGHEST
F32 = jnp.float32
BF16 = jnp.bfloat16


def source_cells():
    source = np.full((FRAME, 1), -1000, np.int32)
    for row in range(FRAME):
        window, cell = divmod(row, ROWS)
        if cell < CELLS:
            down = (window // 2) * WINDOW + cell // WINDOW
            across = (window % 2) * WINDOW + cell % WINDOW
            source[row, 0] = ((down + SHIFT) % SIDE) * SIDE + (across + SHIFT) % SIDE
    return source


def window_masks():
    places = np.arange(SIDE)
    bands = (places >= SIDE - WINDOW).astype(np.int32) + (places >= SIDE - SHIFT)
    masks = np.zeros((4, ROWS, ROWS), np.float32)
    for window in range(4):
        rows = bands[(window // 2) * WINDOW : (window // 2 + 1) * WINDOW]
        cols = bands[(window % 2) * WINDOW : (window % 2 + 1) * WINDOW]
        labels = (rows[:, None] * 3 + cols[None, :]).reshape(-1)
        masks[window, :CELLS, :CELLS] = np.where(labels[:, None] != labels[None, :], MASK_NEG, 0.0)
    masks[:, CELLS:, :] = -1e30
    return np.tile(masks, (1, 1, GROUP))


def offset_onehot():
    hot = np.zeros((TABLE, ROWS, ROWS), np.float32)
    for q in range(CELLS):
        for p in range(CELLS):
            entry = (p // WINDOW - q // WINDOW + WINDOW - 1) * (2 * WINDOW - 1)
            entry += p % WINDOW - q % WINDOW + WINDOW - 1
            hot[entry, q, p] = 1.0
    return hot.reshape(TABLE, ROWS * ROWS)


def mm(left, right):
    return jnp.dot(left, right, preferred_element_type=F32)


def mm_nt(left, right):
    return lax.dot_general(left, right, (((1,), (1,)), ((), ())), preferred_element_type=F32)


def mm_tn(left, right):
    return lax.dot_general(left, right, (((0,), (0,)), ((), ())), preferred_element_type=F32)


def permutation(source, offset, width):
    places = lax.broadcasted_iota(jnp.int32, (FRAME, width), 1)
    return jnp.where(source + offset == places, 1.0, 0.0).astype(BF16)


def normalize(values):
    center = values - jnp.mean(values, axis=-1, keepdims=True)
    inverse = lax.rsqrt(jnp.mean(center * center, axis=-1, keepdims=True) + EPSILON)
    return center * inverse, inverse


def normalize_pull(grad, hat, inverse, gain):
    scaled = grad * gain
    first = jnp.mean(scaled, axis=-1, keepdims=True)
    second = jnp.mean(scaled * hat, axis=-1, keepdims=True)
    return (scaled - first - hat * second) * inverse


def spread_heads(block):
    heads = lax.broadcasted_iota(jnp.int32, block.shape, 1) // HEAD
    return jnp.concatenate(
        [jnp.where(heads == h, block, jnp.zeros_like(block)) for h in range(GROUP)], axis=0
    )


def pick_heads(wide):
    heads = lax.broadcasted_iota(jnp.int32, (ROWS, LANES), 1) // HEAD
    picked = wide[:ROWS]
    for h in range(1, GROUP):
        picked = jnp.where(heads == h, wide[h * ROWS : (h + 1) * ROWS], picked)
    return picked


def image_span(image):
    offset = lax.rem(image * (IMAGE % 16), 16)
    return pl.multiple_of(image * IMAGE - offset, 16), offset


def split_three(values):
    high = values.astype(BF16)
    rest = values - high.astype(F32)
    middle = rest.astype(BF16)
    return high, middle, (rest - middle.astype(F32)).astype(BF16)


VECTORS = ("ln1_gain", "ln1_bias", "q_bias", "v_bias", "out_bias", "ln2_gain", "ln2_bias")


def vector(refs, name):
    return refs[name][...][None, :]


def with_vectors(kernel, at):
    def wrapped(*refs):
        after = at + len(VECTORS)
        return kernel(*refs[:at], dict(zip(VECTORS, refs[at:after])), *refs[after:])

    return wrapped


PAIR = 2
SPREAD = PAIR * FRAME


def orders(step, source):
    found = []
    for k in range(PAIR):
        start, offset = image_span(step * PAIR + k)
        found.append((pl.ds(start, SPAN), permutation(source, offset, SPAN)))
    return found


def arranged(ref, order):
    return jnp.concatenate([mm(hot, ref[rows, :]) for rows, hot in order], axis=0)


def windows_of_step():
    return [(w % 4, slice(w * ROWS, (w + 1) * ROWS)) for w in range(4 * PAIR)]


def group_cols(third, group):
    return slice(third * D + group * LANES, third * D + (group + 1) * LANES)


def forward_kernel(
    tokens_ref, grad_ref, route_ref, source_ref, vectors_ref, qkv_ref, table_ref, hot_ref, mask_ref, out_weight_ref, router_ref,
    projected_ref, weights_ref, attended_ref, residual_ref, rows_ref, place_ref, aux_ref,
    relative, hot_copy, grad_copy, fetches,
):
    fetched = [
        pltpu.make_async_copy(hot_ref, hot_copy, fetches.at[0]), pltpu.make_async_copy(grad_ref, grad_copy, fetches.at[1])
    ]

    @pl.when(pl.program_id(0) == 0)
    def _():
        for copy in fetched:
            copy.start()

    source = source_ref[...]
    order = orders(pl.program_id(0), source)
    inputs = arranged(tokens_ref, order)

    hat, _ = normalize(inputs)
    normed = (hat * vector(vectors_ref, "ln1_gain") + vector(vectors_ref, "ln1_bias")).astype(BF16)
    for third, name in enumerate(("q_bias", "k_bias", "v_bias")):
        at = slice(third * D, (third + 1) * D)
        part = mm(normed, qkv_ref[:, at])
        if name in VECTORS:
            part = part + vector(vectors_ref, name)
        projected_ref[:, at] = part.astype(BF16)

    @pl.when(pl.program_id(0) == 0)
    def _():
        relative[...] = jnp.zeros_like(relative)
        for copy in fetched:
            copy.wait()
        flat = sum(mm(part, hot_copy[...]) for part in split_three(table_ref[...]))
        for q in range(CELLS):
            for h in range(HEADS):
                relative[q : q + 1, h * ROWS : (h + 1) * ROWS] = flat[h : h + 1, q * ROWS : (q + 1) * ROWS]

    for index, (window, rows) in enumerate(windows_of_step()):
        scores = []
        for group in range(GROUPS):
            queries = projected_ref[rows, group_cols(0, group)]
            scores.append(mm_nt(projected_ref[rows, group_cols(1, group)], spread_heads(queries)))
        for group in range(GROUPS):
            wide = slice(group * WIDE, (group + 1) * WIDE)
            full = scores[group] * SCALE + (relative[:, wide] + mask_ref[window])
            powers = jnp.exp(full - jnp.max(full, axis=0, keepdims=True))
            weights = (powers * (1.0 / jnp.sum(powers, axis=0, keepdims=True))).astype(BF16)
            place = (index * GROUPS + group) * ROWS
            weights_ref[place : place + ROWS, :] = weights
            mixed = mm_tn(weights, projected_ref[rows, group_cols(2, group)])
            attended_ref[rows, group_cols(0, group)] = pick_heads(mixed).astype(BF16)

    plain = permutation(source, 0, FRAME)
    chosen_cols, place_cols = [], []
    for k in range(PAIR):
        route = route_ref[k]
        cols = mm_nt(plain, route)
        rows = mm_nt(route, plain)
        place_row = jnp.where(rows[1:2] > 0.5, rows[0:1] * SLOTS + rows[1:2] - 1.0, -1.0)
        place_ref[k] = jnp.broadcast_to(place_row, (8, FRAME)).astype(jnp.int32)
        chosen_cols.append(cols[:, 0:1])
        place_cols.append(jnp.where(cols[:, 1:2] > 0.5, cols[:, 0:1] * SLOTS + cols[:, 1:2] - 1.0, -1.0))
    chosen = jnp.concatenate(chosen_cols, axis=0)

    residual = inputs + (mm(attended_ref[...], out_weight_ref[...]) + vector(vectors_ref, "out_bias"))
    residual_ref[...] = residual
    hat, _ = normalize(residual)
    normed = (hat * vector(vectors_ref, "ln2_gain") + vector(vectors_ref, "ln2_bias")).astype(BF16)
    logits = sum(mm_nt(normed, part) for part in split_three(router_ref[...]))
    logits = jnp.exp(logits - jnp.max(logits, axis=-1, keepdims=True))
    probs = logits / jnp.sum(logits, axis=-1, keepdims=True)
    experts = lax.broadcasted_iota(jnp.int32, (SPREAD, EXPERTS), 1).astype(F32)
    gate = jnp.sum(jnp.where(experts == chosen, probs, 0.0), axis=-1, keepdims=True)
    rows_ref[:, :D] = normed
    rows_ref[:, D:] = (gate * arranged(grad_copy, order)).astype(BF16)
    aux_ref[:, 0:EXPERTS] = probs
    aux_ref[:, EXPERTS : EXPERTS + 1] = gate
    aux_ref[:, EXPERTS + 1 : EXPERTS + 2] = jnp.concatenate(place_cols, axis=0)
    aux_ref[:, EXPERTS + 2 : EXPERTS + 3] = chosen


def backward_kernel(
    copies, members, local, tokens_ref, grad_ref, source_ref, vectors_ref, qkv_ref, out_weight_ref, router_ref, hot_ref,
    projected_ref, weights_ref, attended_ref, residual_ref, aux_ref, returned_ref, held_ref,
    output_ref, grad_tokens_ref, chunks_ref, shared_ref, small_ref,
    grad_projected, grad_attended, grad_residual, outputs, grad_qkv, grad_out, totals, flat, shared, small,
    work, landing, shard, small_landing, held, late_landing, shares, chunks, shared_sum, small_sum,
    tokens, hot_table, output_sum, grad_tokens, fetches,
    chunk_sends, chunk_recvs, scatter_sends, scatter_recvs, gather_sends, gather_recvs, small_sends, small_recvs, part_sends, part_recvs,
    writes,
):
    step = pl.program_id(0)
    steps = IMAGES // PAIR
    everyone = [("expert", s) for s in strides(members)] + copy_bits(copies)[0]
    gathers, late = [], []
    share = shares.shape[1]
    for c, bits in enumerate(chunk_bits(copies, 2 * local)):
        depth = len(bits)
        if c < 2 * (local - 1):
            semaphores = chunk_sends.at[c], chunk_recvs.at[c]
            gathers.append(Gather(held.at[c], chunks.at[c], CHUNK, *semaphores, bits, skip=1))
        else:
            last = chunk_sends.at[c, pl.ds(depth, 1)], chunk_recvs.at[c, pl.ds(depth, 1)]
            scatter = Scatter(held.at[c], shares.at[c], 2 * share, None, late_landing.at[c], *last, bits[-1:])
            semaphores = chunk_sends.at[c], chunk_recvs.at[c]
            gathers.append(Chain(scatter, Gather(shares.at[c], chunks.at[c], CHUNK, *semaphores, bits)))
            late.append(c)
    small_stream = Doubling(small, small_sum, small_landing, small_sends, small_recvs, everyone)
    shared_streams = []
    for part, bits in enumerate(part_bits(copies, members)):
        rows = pl.ds(part * PART, PART)
        scatter = Scatter(
            shared.at[rows], shard.at[part], PART, work.at[part], landing.at[part],
            scatter_sends.at[part], scatter_recvs.at[part], bits,
        )
        gather = Gather(shard.at[part], shared_sum.at[rows], PART, gather_sends.at[part], gather_recvs.at[part], bits)
        shared_streams.append(Chain(scatter, gather))
    runner = Runner()
    plan = {}
    for c, gather in enumerate(gathers):
        for stage, place in enumerate(PLACES.get(gather.steps, ())):
            plan.setdefault(place, []).append((c, stage))
    planned = [pair for pairs in plan.values() for pair in pairs]

    def advance(c, stage):
        if stage:
            gathers[c].finish(stage - 1)
        gathers[c].start(stage)
        gathers[c].settle(stage)

    def last_part(c, part):
        return gathers[c].second.last_part(part, part_sends.at[c], part_recvs.at[c])

    def exchange_at(phase):
        for s in range(steps):
            if due := plan.get(s * PHASES + phase):

                @pl.when(step == s)
                def _(due=due):
                    for c, stage in due:
                        advance(c, stage)

    fetched = [
        pltpu.make_async_copy(source, target, fetches.at[i])
        for i, (source, target) in enumerate(((held_ref, held), (tokens_ref, tokens), (hot_ref, hot_table)))
    ]

    @pl.when(step == 0)
    def _():
        greet([partner(*bit)[1] for bit in everyone])
        for copy in fetched:
            copy.start()
        for ref in (output_sum, grad_tokens, grad_qkv, grad_out, totals, small):
            ref[...] = jnp.zeros_like(ref)
        fetched[0].wait()

    exchange_at(0)
    order = orders(step, source_ref[...])
    upstream = arranged(grad_ref, order)
    residual = residual_ref[...]
    aux = aux_ref[...]
    probs = aux[:, 0:EXPERTS]
    gate = aux[:, EXPERTS : EXPERTS + 1]
    place = aux[:, EXPERTS + 1 : EXPERTS + 2].astype(jnp.int32)
    chosen = aux[:, EXPERTS + 2 : EXPERTS + 3]

    slots = lax.broadcasted_iota(jnp.int32, (SPREAD, EXPERTS * SLOTS), 1)
    hot = jnp.where(slots == place, 1.0, 0.0).astype(BF16)
    gathered = mm(hot, returned_ref[...])
    combined = gathered[:, :D]
    output = (residual + gate * combined).astype(BF16)
    of_step = pl.ds(pl.multiple_of(step * SPREAD, SPREAD), SPREAD)
    outputs[of_step, :] = output

    hat2, inverse2 = normalize(residual)
    normed2 = (hat2 * vector(vectors_ref, "ln2_gain") + vector(vectors_ref, "ln2_bias")).astype(BF16)
    gate_grad = jnp.sum(upstream * combined, axis=-1, keepdims=True)
    experts = lax.broadcasted_iota(jnp.int32, (SPREAD, EXPERTS), 1).astype(F32)
    grad_logits = gate_grad * gate * (jnp.where(experts == chosen, 1.0, 0.0) - probs)
    logits_high, logits_low, _ = split_three(grad_logits)
    small[8:16, :] += mm_tn(logits_high, normed2) + mm_tn(logits_low, normed2)
    router_high, router_low, _ = split_three(router_ref[...])
    grad_normed = (
        gathered[:, D:] + mm(logits_high, router_high) + mm(logits_low, router_high) + mm(logits_high, router_low)
    )
    small[0:1, :] += jnp.sum(grad_normed * hat2, axis=0, keepdims=True)
    small[1:2, :] += jnp.sum(grad_normed, axis=0, keepdims=True)
    grad_mixed = upstream + normalize_pull(grad_normed, hat2, inverse2, vector(vectors_ref, "ln2_gain"))
    grad_residual[of_step, :] = grad_mixed
    grad_mixed = grad_mixed.astype(BF16)
    grad_out[...] += mm_tn(attended_ref[...], grad_mixed)
    small[2:3, :] += jnp.sum(grad_mixed.astype(F32), axis=0, keepdims=True)
    grad_attended[...] = mm_nt(grad_mixed, out_weight_ref[...]).astype(BF16)

    exchange_at(1)
    for index, (_, rows) in enumerate(windows_of_step()):
        if index == 2 * PAIR:
            exchange_at(2)
        out_rows = pl.ds(pl.multiple_of(step * SPREAD + index * ROWS, ROWS), ROWS)
        spread_grads = [spread_heads(grad_attended[rows, group_cols(0, g)]) for g in range(GROUPS)]
        grad_weights = [
            mm_nt(projected_ref[rows, group_cols(2, g)], spread_grads[g]) for g in range(GROUPS)
        ]
        for g in range(GROUPS):
            at = (index * GROUPS + g) * ROWS
            weights = weights_ref[at : at + ROWS, :]
            exact = weights.astype(F32)
            scores = exact * (grad_weights[g] - jnp.sum(exact * grad_weights[g], axis=0, keepdims=True))
            scores = scores.astype(BF16)
            totals[:, g * WIDE : (g + 1) * WIDE] += scores.astype(F32)
            grad_projected[out_rows, group_cols(2, g)] = mm(weights, spread_grads[g]).astype(BF16)
            grad_keys = mm(scores, spread_heads(projected_ref[rows, group_cols(0, g)]))
            grad_projected[out_rows, group_cols(1, g)] = (grad_keys * SCALE).astype(BF16)
            grad_queries = pick_heads(mm_tn(scores, projected_ref[rows, group_cols(1, g)]))
            grad_projected[out_rows, group_cols(0, g)] = (grad_queries * SCALE).astype(BF16)

    exchange_at(3)

    @pl.when(step == 0)
    def _():
        for copy in fetched[1:]:
            copy.wait()

    grads = grad_projected[of_step, :]
    hat1, _ = normalize(arranged(tokens, order))
    normed1 = (hat1 * vector(vectors_ref, "ln1_gain") + vector(vectors_ref, "ln1_bias")).astype(BF16)
    grad_qkv[...] += mm_tn(normed1, grads)
    column_sums = jnp.sum(grads.astype(F32), axis=0, keepdims=True)
    for third in range(3):
        small[5 + third : 6 + third, :] += column_sums[:, third * D : (third + 1) * D]

    def first_norm_back(step):
        of_step = slice(step * SPREAD, (step + 1) * SPREAD)
        order = orders(step, source_ref[...])
        hat, inverse = normalize(arranged(tokens, order))
        grad_normed = mm_nt(grad_projected[of_step, :], qkv_ref[...])
        pulled = normalize_pull(grad_normed, hat, inverse, vector(vectors_ref, "ln1_gain"))
        high, low, _ = split_three(grad_residual[of_step, :] + pulled)
        for k, (rows, hot) in enumerate(order):
            of_image = slice(k * FRAME, (k + 1) * FRAME)
            grad_tokens[rows, :] += mm_tn(hot, high[of_image]) + mm_tn(hot, low[of_image])
            output_sum[rows, :] += mm_tn(hot, outputs[of_step, :][of_image]).astype(BF16)

    def first_norm_sums():
        ones = jnp.ones((8, D), BF16)
        of_bias = of_normed = 0.0
        for third in range(3):
            at = slice(third * D, (third + 1) * D)
            weight = qkv_ref[:, at]
            sums = jnp.broadcast_to(small[5 + third : 6 + third, :], (8, D))
            of_bias += sum(mm_nt(part, weight) for part in split_three(sums))
            of_normed += sum(mm_nt(ones, part) for part in split_three(weight.astype(F32) * grad_qkv[:, at]))
        of_bias, of_normed = of_bias[0:1], of_normed[0:1]
        shift = vector(vectors_ref, "ln1_bias") * of_bias
        small[3:4, :] = (of_normed - shift) / vector(vectors_ref, "ln1_gain")
        small[4:5, :] = of_bias

    @pl.when(step == steps - 1)
    def _():
        for third in range(3):
            at = slice(third * D, (third + 1) * D)
            shared[at, :] = grad_qkv[:, at].astype(BF16)
        shared[3 * D :, :] = grad_out[...].astype(BF16)
        runner.advance(*shared_streams)
        flat[...] = jnp.zeros_like(flat)
        for q in range(CELLS):
            for h in range(HEADS):
                flat[h : h + 1, q * ROWS : (q + 1) * ROWS] = totals[q : q + 1, h * ROWS : (h + 1) * ROWS]
        table = sum(mm_nt(part, hot_table[...]) for part in split_three(flat[...]))
        small[16:32, : table.shape[1]] = table
        first_norm_sums()
        runner.advance(small_stream)
        for c, gather in enumerate(gathers):
            for stage in range(gather.steps - (c in late)):
                if (c, stage) not in planned:
                    advance(c, stage)
        for c in late:
            gathers[c].finish(gathers[c].steps - 2)
        for done in range(max(steps, LAST_PARTS)):
            if done < LAST_PARTS:
                for c in late:
                    last_part(c, done).start()
            if done < steps:
                first_norm_back(done)
            runner.advance(small_stream, *shared_streams)
        copies_out = [
            pltpu.make_async_copy(output_sum, output_ref, writes.at[len(gathers) + 1]),
            pltpu.make_async_copy(grad_tokens, grad_tokens_ref, writes.at[len(gathers) + 2]),
        ]
        for c, gather in enumerate(gathers):
            if c not in late:
                gather.finish(gather.steps - 1)
                copies_out.append(pltpu.make_async_copy(chunks.at[c], chunks_ref.at[c], writes.at[c]))
        for copy in copies_out:
            copy.start()
        runner.complete(*shared_streams, small_stream)
        small_ref[...] = small_sum[...]
        ends = [pltpu.make_async_copy(shared_sum, shared_ref, writes.at[len(gathers)])]
        for c in late:
            for part in range(LAST_PARTS):
                last_part(c, part).wait()
            ends.append(pltpu.make_async_copy(chunks.at[c], chunks_ref.at[c], writes.at[c]))
        for copy in ends:
            copy.start()
        copies_out += ends
        for copy in copies_out:
            copy.wait()


PHASES = 4


PLACES = {2: (0, 7), 4: (0, 8, 14), 6: (0, 5, 8, 10, 12)}


IMAGES = 8
CHUNK = 4 * D
PARTS = 3
PART = CHUNK // PARTS
LAST_PARTS = 4
MESH = pl.DeviceIdType.MESH


def add_rows(left, left_at, right, rights_at, out, out_at, count):
    step = next(s for s in (64, 48, 32, 16) if count % s == 0)

    def body(i, carry):
        here = i * step
        total = left[pl.ds(pl.multiple_of(left_at + here, 16), step), :].astype(F32)
        for right_at in rights_at:
            total = total + right[pl.ds(pl.multiple_of(right_at + here, 16), step), :].astype(F32)
        out[pl.ds(pl.multiple_of(out_at + here, 16), step), :] = total.astype(out.dtype)
        return carry

    lax.fori_loop(0, count // step, body, 0)


def partner(axis, stride):
    index = lax.axis_index(axis)
    bit = lax.rem(lax.div(index, stride), 2)
    return bit, {axis: index + stride - 2 * stride * bit}


def neighbours(group):
    place, others = 0, []
    for axis, stride in group:
        place = 2 * place + partner(axis, stride)[0]
    for flips in range(1, 2 ** len(group)):
        other, device = 0, {}
        for i, (axis, stride) in enumerate(group):
            bit = partner(axis, stride)[0]
            flip = flips >> i & 1
            other = 2 * other + (1 - bit if flip else bit)
            index = device.get(axis, lax.axis_index(axis))
            device[axis] = index + stride - 2 * stride * bit if flip else index
        others.append((other, device))
    return place, others


def stages_of(rows, bits):
    stages = []
    for item in bits:
        if isinstance(item, list) and rows % 64 == 0:
            rows //= 4
            stages.append((item, rows, True))
            continue
        for bit in item if isinstance(item, list) else [item]:
            halved = rows % 32 == 0
            rows = rows // 2 if halved else rows
            stages.append(([bit], rows, halved))
    return stages


def kept_rows(rows, bits):
    return stages_of(rows, bits)[-1][1]


def landing_rows(rows, bits):
    return sum(size * (2 ** len(group) - 1) for group, size, _ in stages_of(rows, bits))


def copies_of(bits):
    return sum(3 if isinstance(item, list) else 1 for item in bits)


def exchange(src, dst, sends, recvs, step, device):
    return pltpu.make_async_remote_copy(
        src_ref=src, dst_ref=dst, send_sem=sends.at[step], recv_sem=recvs.at[step], device_id=device, device_id_type=MESH
    )


def rows_at(ref, start, size):
    return ref.at[pl.ds(pl.multiple_of(start, 16), size)]


class Scatter:
    def __init__(self, source, out, rows, work, landing, sends, recvs, bits):
        self.source, self.out, self.work, self.landing = source, out, work, landing
        self.sends, self.recvs = sends, recvs
        self.plan = []
        at = land = semaphore = 0
        for step, (group, size, shared) in enumerate(stages_of(rows, bits)):
            place, others = neighbours(group)
            keep = at + place * size if shared else at
            copies = []
            for other, device in others:
                copies.append((at + other * size if shared else at, land, semaphore, device))
                land, semaphore = land + size, semaphore + 1
            self.plan.append((keep, size, copies))
            at = keep if step else 0
        self.steps = len(self.plan)

    def copies(self, step):
        _, size, copies = self.plan[step]
        mine = self.work if step else self.source
        return [
            exchange(
                rows_at(mine, give, size), self.landing.at[pl.ds(land, size)], self.sends, self.recvs, semaphore, device
            )
            for give, land, semaphore, device in copies
        ]

    def add(self, step, start, size):
        keep, _, copies = self.plan[step]
        mine = self.work if step else self.source
        if step == self.steps - 1:
            out, out_at = self.out, 0
        else:
            out, out_at = self.work, keep if step else 0
        landings = [land + start for _, land, _, _ in copies]
        add_rows(mine, keep + start, self.landing, landings, out, out_at + start, size)

    def splits(self, step):
        return 0 <= step < self.steps - 1 and 2 * self.plan[step + 1][1] == self.plan[step][1]

    def start(self, step):
        for copy in self.copies(step):
            copy.start()

    def settle(self, step):
        if self.splits(step - 1):
            keep, size, _ = self.plan[step]
            self.add(step - 1, keep - (self.plan[step - 1][0] if step > 1 else 0), size)

    def finish(self, step):
        for copy in self.copies(step):
            copy.wait()
        if self.splits(step):
            _, size, copies = self.plan[step + 1]
            self.add(step, copies[0][0] - (self.plan[step][0] if step else 0), size)
        else:
            self.add(step, 0, self.plan[step][1])


class Gather:
    def __init__(self, share, out, rows, sends, recvs, bits, skip=0):
        self.share, self.out, self.sends, self.recvs = share, out, sends, recvs
        self.plan = []
        start = 0
        for group, size, shared in stages_of(rows, bits):
            place, others = neighbours(group)
            start = start + place * size if shared else start
            if shared:
                self.plan.insert(0, (start, size, [device for _, device in others]))
        self.plan = self.plan[skip:]
        self.steps = len(self.plan)

    def copies(self, step):
        start, size, devices = self.plan[step]
        first = sum(len(others) for _, _, others in self.plan[:step])
        rows = rows_at(self.out, start, size)
        return [
            exchange(rows, rows, self.sends, self.recvs, first + i, device) for i, device in enumerate(devices)
        ]

    def last_part(self, part, sends, recvs):
        start, size, (device,) = self.plan[-1]
        size = size // LAST_PARTS
        rows = rows_at(self.out, start + part * size, size)
        return exchange(rows, rows, sends, recvs, part, device)

    def start(self, step):
        if step == 0:
            start, size, _ = self.plan[0]
            self.out[pl.ds(pl.multiple_of(start, 16), size), :] = self.share[...]
        for copy in self.copies(step):
            copy.start()

    def settle(self, step):
        pass

    def finish(self, step):
        for copy in self.copies(step):
            copy.wait()


class Chain:
    def __init__(self, first, second):
        self.first, self.second, self.steps = first, second, first.steps + second.steps

    def of(self, step):
        return (self.first, step) if step < self.first.steps else (self.second, step - self.first.steps)

    def start(self, step):
        stream, step = self.of(step)
        stream.start(step)

    def settle(self, step):
        stream, step = self.of(step)
        stream.settle(step)

    def finish(self, step):
        stream, step = self.of(step)
        stream.finish(step)


class Doubling:
    def __init__(self, source, out, landing, sends, recvs, bits):
        self.source, self.out, self.landing = source, out, landing
        self.sends, self.recvs, self.bits = sends, recvs, bits
        self.steps = len(bits)

    def copy(self, step):
        device = partner(*self.bits[step])[1]
        return exchange(self.out, self.landing.at[step], self.sends, self.recvs, step, device)

    def start(self, step):
        if step == 0:
            self.out[...] = self.source[...]
        self.copy(step).start()

    def settle(self, step):
        pass

    def finish(self, step):
        self.copy(step).wait()
        self.out[...] = self.out[...] + self.landing[step]


class Runner:
    def __init__(self):
        self.at = {}

    def advance(self, *streams):
        begun = []
        for stream in streams:
            step = self.at.get(stream, -1)
            if step < stream.steps:
                if step >= 0:
                    stream.finish(step)
                self.at[stream] = step = step + 1
                if step < stream.steps:
                    stream.start(step)
                    begun.append((stream, step))
        for stream, step in begun:
            stream.settle(step)

    def complete(self, *streams):
        while any(self.at.get(s, -1) < s.steps for s in streams):
            self.advance(*streams)


def strides(size):
    return [2**k for k in range(size.bit_length() - 1)]


def copy_bits(copies):
    low = len(strides(copies)) // 2
    all_bits = [("dp", s) for s in strides(copies)]
    return all_bits, all_bits[low : low + 1] + all_bits[:low] + all_bits[low + 1 :]


def part_bits(copies, members):
    chips = [("expert", s) for s in strides(members)]
    bits = copy_bits(copies)[0]
    rest = [*chips[1:], *bits[:-2], bits[-2:]]
    turns = [part * len(rest) // PARTS for part in range(PARTS)]
    return [chips[:1] + rest[turn:] + rest[:turn] for turn in turns]


def chunk_bits(copies, count):
    first, second = copy_bits(copies)
    return [second if c % 2 else first for c in range(count)]


def greet(devices):
    barrier = pltpu.get_barrier_semaphore()
    for device in devices:
        pl.semaphore_signal(barrier, inc=1, device_id=device, device_id_type=MESH)
    pl.semaphore_wait(barrier, len(devices))


def member_at(members, hop, sign):
    index = lax.axis_index("expert")
    chips = members // 2
    chip = lax.rem(lax.div(index, 2) + sign * (hop // 2) + chips, chips)
    return chip * 2 + lax.rem(lax.rem(index, 2) + hop % 2, 2)


TILE = 512


def experts_kernel(
    copies, members, local, place_ref, rows_ref, up_ref, up_bias_ref, down_ref, down_bias_ref,
    returned_ref, held_ref, biases_ref,
    up, down, outbox, inbox, results, up_sum, down_sum, up_bias_sum, down_bias_sum, chunks, biases, work, landing, shares,
    bias_landing,
    out_sends, out_recvs, back_sends, back_recvs, chunk_sends, chunk_recvs, bias_sends, bias_recvs, fetches,
):
    me = lax.axis_index("expert")
    fetched = [
        pltpu.make_async_copy(up_ref, up, fetches.at[0]), pltpu.make_async_copy(down_ref, down, fetches.at[1])
    ]
    for copy in fetched:
        copy.start()
    bits = chunk_bits(copies, 2 * local)
    greet(
        [{"expert": member_at(members, hop, 1)} for hop in range(1, members)]
        + [partner(*bit)[1] for bit in copy_bits(copies)[0]]
    )
    places = jnp.concatenate([place_ref[i, 0:1, :] for i in range(place_ref.shape[0])], axis=1)

    def out_copy(hop, j):
        return pltpu.make_async_remote_copy(
            src_ref=outbox.at[j, hop], dst_ref=inbox.at[j, hop],
            send_sem=out_sends.at[j, hop], recv_sem=out_recvs.at[j, hop],
            device_id={"expert": member_at(members, hop, 1)}, device_id_type=MESH,
        )

    def back_copy(hop, j):
        return pltpu.make_async_remote_copy(
            src_ref=results.at[j, hop], dst_ref=returned_ref.at[me, j],
            send_sem=back_sends.at[j, hop], recv_sem=back_recvs.at[j, hop],
            device_id={"expert": member_at(members, hop, -1)}, device_id_type=MESH,
        )

    def dispatch(hop, j):
        expert = member_at(members, hop, 1) * local + j
        slots = lax.broadcasted_iota(jnp.int32, (SLOTS, places.shape[1]), 0) + expert * SLOTS
        hot = jnp.where(slots == places, 1.0, 0.0).astype(BF16)
        return mm(hot, rows_ref[...]).astype(BF16)

    order = [(hop, j) for j in range(local) for hop in range(members - 1, 1, -1)]
    order += [(hop, j) for j in range(local) for hop in (1, 0)]
    for hop, j in order:
        if hop:
            outbox[j, hop] = dispatch(hop, j)
            if hop == 1 or j == 0:
                out_copy(hop, j).start()
        else:
            inbox[j, 0] = dispatch(0, j)

    for copy in fetched:
        copy.wait()
    up_sum[...] = jnp.zeros_like(up_sum)
    down_sum[...] = jnp.zeros_like(down_sum)
    up_bias_sum[...] = jnp.zeros_like(up_bias_sum)
    down_bias_sum[...] = jnp.zeros_like(down_bias_sum)

    def compute(pair, j):
        hops = (2 * pair, 2 * pair + 1)
        for hop in hops:
            if hop:
                out_copy(hop, j).wait_recv()
        inputs = inbox[j, 2 * pair : 2 * pair + 2, :, :D].reshape(2 * SLOTS, D)
        grads = inbox[j, 2 * pair : 2 * pair + 2, :, D:].reshape(2 * SLOTS, D)
        inputs_t = inputs.T
        grads_t = grads.T
        outs = jnp.zeros((2 * SLOTS, D), F32)
        backs = jnp.zeros((2 * SLOTS, D), F32)
        for tile in range(FF // TILE):
            at = slice(tile * TILE, (tile + 1) * TILE)
            pre = mm(inputs, up[j, :, at]) + up_bias_ref[j : j + 1, at]
            grad_hidden = mm_nt(grads, down[j, at, :])
            share = 0.5 + 0.5 * lax.erf(pre * 0.7071067811865476)
            density = jnp.exp(pre * pre * -0.5) * 0.3989422804014327
            hidden = (pre * share).astype(BF16)
            grad_pre = (grad_hidden * (share + pre * density)).astype(BF16)
            outs += mm(hidden, down[j, at, :])
            backs += mm_nt(grad_pre, up[j, :, at])
            down_sum[j, :, at] += mm(grads_t, hidden)
            up_sum[j, :, at] += mm(inputs_t, grad_pre)
            up_bias_sum[j : j + 1, at] += jnp.sum(grad_pre.astype(F32), axis=0, keepdims=True)
        down_bias_sum[j : j + 1, :] += jnp.sum(grads.astype(F32), axis=0, keepdims=True)
        results[j, 2 * pair : 2 * pair + 2, :, :D] = (
            (outs + down_bias_ref[j : j + 1, :]).astype(BF16).reshape(2, SLOTS, D)
        )
        results[j, 2 * pair : 2 * pair + 2, :, D:] = backs.astype(BF16).reshape(2, SLOTS, D)
        if pair == 0:
            returned_ref[me, j] = results[j, 0]
            back_copy(1, j).start()

    def seal(j):
        for tile in range(FF // D):
            at = slice(tile * D, (tile + 1) * D)
            chunks[2 * j, at, :] = up_sum[j, :, at].astype(BF16)
            chunks[2 * j + 1, at, :] = down_sum[j, :, at].T.astype(BF16)
            biases[8 * j + tile : 8 * j + tile + 1, :] = up_bias_sum[j : j + 1, at]
        biases[8 * j + 4 : 8 * j + 5, :] = down_bias_sum[j : j + 1, :]
        biases[8 * j + 5 : 8 * j + 8, :] = jnp.zeros((3, D), F32)

    streams = []
    for c in range(2 * local):
        early = c < 2 * (local - 1)
        parts = chunks.at[c], shares.at[c] if early else held_ref.at[c], CHUNK, work.at[c], landing.at[c]
        semaphores = chunk_sends.at[c], chunk_recvs.at[c]
        if early:
            depth, share = len(bits[c]), shares.shape[1]
            semaphores_back = chunk_sends.at[c, pl.ds(depth, 1)], chunk_recvs.at[c, pl.ds(depth, 1)]
            back = Gather(shares.at[c], held_ref.at[c], 2 * share, *semaphores_back, bits[c][-1:])
            streams.append(Chain(Scatter(*parts, *semaphores, bits[c]), back))
        else:
            streams.append(Scatter(*parts, *semaphores, bits[c][:-1]))
    runner = Runner()
    far = range(2, members)
    for j in range(local):
        compute(0, j)
        for hop in far:
            out_copy(hop, j).wait_send()
        for hop in far:
            if j + 1 < local:
                out_copy(hop, j + 1).start()
            else:
                for held in range(j):
                    back_copy(hop, held).start()
        for pair in range(1, members // 2):
            compute(pair, j)
        if j == local - 1:
            for hop in far:
                back_copy(hop, j).start()
        seal(j)
        if j < local - 1:
            runner.advance(*streams[2 * j : 2 * j + 2])
    small = Doubling(biases, biases_ref, bias_landing, bias_sends, bias_recvs, copy_bits(copies)[0])
    early, late = streams[: 2 * (local - 1)], streams[2 * (local - 1) :]
    for turn in (early, late, early, late, early, late, early):
        runner.advance(small, *turn)
    runner.complete(small, *early, *late)
    for j in range(local):
        out_copy(1, j).wait_send()
        for hop in range(1, members):
            back_copy(hop, j).wait()


def finish_kernel(
    up_tile_ref, down_tile_ref, biases_ref, shared_ref, small_ref,
    up_ref, down_ref, up_bias_ref, down_bias_ref, qkv_ref, out_ref, router_ref, table_ref, *vector_refs,
):
    for tile in range(up_tile_ref.shape[1] // D):
        at = slice(tile * D, (tile + 1) * D)
        up_ref[0, :, at] = up_tile_ref[0, at, :].astype(F32)
    down_ref[0] = down_tile_ref[0].astype(F32)

    @pl.when(pl.program_id(0) == 0)
    def _():
        for j in range(up_bias_ref.shape[0]):
            for tile in range(FF // D):
                row = 8 * j + tile
                up_bias_ref[j : j + 1, tile * D : (tile + 1) * D] = biases_ref[row : row + 1, :]
            down_bias_ref[j : j + 1, :] = biases_ref[8 * j + 4 : 8 * j + 5, :]
        for third in range(3):
            at = slice(third * D, (third + 1) * D)
            qkv_ref[:, at] = shared_ref[at, :].astype(F32)
        out_ref[...] = shared_ref[3 * D :, :].astype(F32)
        router_ref[...] = small_ref[8:16, :]
        table_ref[...] = small_ref[16 : 16 + HEADS, :TABLE]
        for ref, row in zip(vector_refs, (3, 4, 5, 7, 2, 0, 1)):
            ref[...] = small_ref[row, :]


def whole(shape):
    return pl.BlockSpec(shape, lambda *_: (0,) * len(shape))


def per_step(rows, columns):
    return pl.BlockSpec((rows, columns), lambda i: (i, 0))


def shards(
    tokens, ln1_gain, ln1_bias, qkv_weight, q_bias, v_bias, bias_table, out_weight, out_bias, ln2_gain, ln2_bias,
    router_weight, up_weight, up_bias, down_weight, down_bias, expert_of, slot_of, grad_output,
):
    members = lax.axis_size("expert")
    local = up_weight.shape[0]
    count = tokens.shape[0]
    images = count // IMAGE
    framed = images * FRAME
    params = pltpu.CompilerParams(dimension_semantics=("arbitrary",), vmem_limit_bytes=60 * 2**20)

    source = jnp.asarray(source_cells())
    masks = jnp.asarray(window_masks())
    hot = jnp.asarray(offset_onehot().astype(BF16))
    route = jnp.stack([expert_of, slot_of + 1]).astype(BF16).reshape(2, images, IMAGE).transpose(1, 0, 2)
    route = jnp.pad(route, ((0, 0), (0, 6), (0, FRAME - IMAGE)))
    vectors = (ln1_gain, ln1_bias, q_bias, v_bias, out_bias, ln2_gain, ln2_bias)
    router = router_weight.T
    vmem = pl.BlockSpec(memory_space=pltpu.VMEM)
    anywhere = pl.BlockSpec(memory_space=pl.ANY)
    dma = pltpu.SemaphoreType.DMA

    projected, weights, attended, residual, rows, place, aux = pl.pallas_call(
        with_vectors(forward_kernel, 4),
        grid=(images // PAIR,),
        in_specs=[
            whole((count, D)), anywhere, pl.BlockSpec((PAIR, 8, FRAME), lambda i: (i, 0, 0)),
            whole((FRAME, 1)), *[whole((D,))] * len(VECTORS), whole((D, 3 * D)), whole((HEADS, TABLE)), anywhere,
            whole((4, ROWS, WIDE)), whole((D, D)), whole((EXPERTS, D)),
        ],
        out_specs=[
            per_step(SPREAD, 3 * D), per_step(4 * PAIR * GROUPS * ROWS, WIDE), per_step(SPREAD, D), per_step(SPREAD, D),
            per_step(SPREAD, 2 * D), pl.BlockSpec((PAIR, 8, FRAME), lambda i: (i, 0, 0)), per_step(SPREAD, 128),
        ],
        out_shape=[
            jax.ShapeDtypeStruct((framed, 3 * D), BF16),
            jax.ShapeDtypeStruct((images * 4 * GROUPS * ROWS, WIDE), BF16),
            jax.ShapeDtypeStruct((framed, D), BF16),
            jax.ShapeDtypeStruct((framed, D), F32),
            jax.ShapeDtypeStruct((framed, 2 * D), BF16),
            jax.ShapeDtypeStruct((images, 8, FRAME), jnp.int32),
            jax.ShapeDtypeStruct((framed, 128), F32),
        ],
        scratch_shapes=[
            pltpu.VMEM((ROWS, HEADS * ROWS), F32), pltpu.VMEM((TABLE, ROWS * ROWS), BF16), pltpu.VMEM((count, D), BF16),
            dma((2,)),
        ],
        compiler_params=params,
        name="forward",
    )(tokens, grad_output, route, source, *vectors, qkv_weight, bias_table.T, hot, masks, out_weight, router)

    copies = lax.axis_size("dp")
    depth = len(strides(copies))
    total = depth + len(strides(members))
    pieces = 2 * local
    share = kept_rows(CHUNK, copy_bits(copies)[0])
    paths = part_bits(copies, members)
    moves = max(copies_of(path) for path in paths)
    returned, held, biases = pl.pallas_call(
        partial(experts_kernel, copies, members, local),
        in_specs=[vmem, vmem, pl.BlockSpec(memory_space=pl.ANY), vmem, pl.BlockSpec(memory_space=pl.ANY), vmem],
        out_specs=[vmem] * 3,
        out_shape=[
            jax.ShapeDtypeStruct((members, local, SLOTS, 2 * D), BF16),
            jax.ShapeDtypeStruct((pieces, 2 * share, D), BF16),
            jax.ShapeDtypeStruct((8 * local, D), F32),
        ],
        scratch_shapes=[
            pltpu.VMEM((local, D, FF), BF16),
            pltpu.VMEM((local, FF, D), BF16),
            pltpu.VMEM((local, members, SLOTS, 2 * D), BF16),
            pltpu.VMEM((local, members, SLOTS, 2 * D), BF16),
            pltpu.VMEM((local, members, SLOTS, 2 * D), BF16),
            pltpu.VMEM((local, D, FF), F32),
            pltpu.VMEM((local, D, FF), F32),
            pltpu.VMEM((local, FF), F32),
            pltpu.VMEM((local, D), F32),
            pltpu.VMEM((pieces, CHUNK, D), BF16),
            pltpu.VMEM((8 * local, D), F32),
            pltpu.VMEM((pieces, CHUNK // 2, D), BF16),
            pltpu.VMEM((pieces, landing_rows(CHUNK, copy_bits(copies)[0]), D), BF16),
            pltpu.VMEM((pieces, share, D), BF16),
            pltpu.VMEM((depth, 8 * local, D), F32),
            dma((local, members)), dma((local, members)), dma((local, members)), dma((local, members)),
            dma((pieces, depth + 1)), dma((pieces, depth + 1)), dma((depth,)), dma((depth,)), dma((2,)),
        ],
        compiler_params=pltpu.CompilerParams(
            collective_id=1, has_side_effects=True, vmem_limit_bytes=60 * 2**20
        ),
        name="experts",
    )(place, rows, up_weight, up_bias, down_weight, down_bias)
    returned = returned.reshape(EXPERTS * SLOTS, 2 * D)

    output, grad_tokens, chunks, shared, small = pl.pallas_call(
        with_vectors(partial(backward_kernel, copies, members, local), 3),
        grid=(images // PAIR,),
        in_specs=[
            anywhere, whole((count, D)), whole((FRAME, 1)), *[whole((D,))] * len(VECTORS), whole((D, 3 * D)),
            whole((D, D)), whole((EXPERTS, D)), anywhere,
            per_step(SPREAD, 3 * D), per_step(4 * PAIR * GROUPS * ROWS, WIDE), per_step(SPREAD, D), per_step(SPREAD, D),
            per_step(SPREAD, 128), whole((EXPERTS * SLOTS, 2 * D)), anywhere,
        ],
        out_specs=[
            anywhere, anywhere, anywhere, anywhere, whole((32, D)),
        ],
        out_shape=[
            jax.ShapeDtypeStruct((count, D), BF16),
            jax.ShapeDtypeStruct((count, D), F32),
            jax.ShapeDtypeStruct((pieces, CHUNK, D), BF16),
            jax.ShapeDtypeStruct((CHUNK, D), BF16),
            jax.ShapeDtypeStruct((32, D), F32),
        ],
        scratch_shapes=[
            pltpu.VMEM((framed, 3 * D), BF16), pltpu.VMEM((SPREAD, D), BF16), pltpu.VMEM((framed, D), F32),
            pltpu.VMEM((framed, D), BF16),
            pltpu.VMEM((D, 3 * D), F32), pltpu.VMEM((D, D), F32),
            pltpu.VMEM((ROWS, HEADS * ROWS), F32),
            pltpu.VMEM((16, ROWS * ROWS), F32),
            pltpu.VMEM((CHUNK, D), BF16),
            pltpu.VMEM((32, D), F32),
            pltpu.VMEM((PARTS, PART // 2, D), BF16),
            pltpu.VMEM((PARTS, max(landing_rows(PART, path) for path in paths), D), BF16),
            pltpu.VMEM((PARTS, kept_rows(PART, paths[0]), D), BF16),
            pltpu.VMEM((total, 32, D), F32),
            pltpu.VMEM((pieces, 2 * share, D), BF16),
            pltpu.VMEM((pieces, share, D), BF16),
            pltpu.VMEM((pieces, share, D), BF16),
            pltpu.VMEM((pieces, CHUNK, D), BF16),
            pltpu.VMEM((CHUNK, D), BF16),
            pltpu.VMEM((32, D), F32),
            pltpu.VMEM((count, D), BF16),
            pltpu.VMEM((TABLE, ROWS * ROWS), BF16),
            pltpu.VMEM((count, D), BF16),
            pltpu.VMEM((count, D), F32),
            dma((3,)),
            dma((pieces, depth + 1)), dma((pieces, depth + 1)), dma((PARTS, moves)), dma((PARTS, moves)),
            dma((PARTS, moves)), dma((PARTS, moves)), dma((total,)), dma((total,)), dma((pieces, LAST_PARTS)), dma((pieces, LAST_PARTS)),
            dma((pieces + 3,)),
        ],
        compiler_params=pltpu.CompilerParams(
            dimension_semantics=("arbitrary",), collective_id=2, has_side_effects=True, vmem_limit_bytes=60 * 2**20
        ),
        name="backward",
    )(
        tokens, grad_output, source, *vectors, qkv_weight, out_weight, router, hot, projected, weights,
        attended, residual, aux, returned, held,
    )

    results = pl.pallas_call(
        finish_kernel,
        grid=(local,),
        in_specs=[
            pl.BlockSpec((1, FF, D), lambda j: (2 * j, 0, 0)),
            pl.BlockSpec((1, FF, D), lambda j: (2 * j + 1, 0, 0)),
            whole((8 * local, D)), whole((CHUNK, D)), whole((32, D)),
        ],
        out_specs=[
            pl.BlockSpec((1, D, FF), lambda j: (j, 0, 0)), pl.BlockSpec((1, FF, D), lambda j: (j, 0, 0)),
            whole((local, FF)), whole((local, D)), whole((D, 3 * D)), whole((D, D)), whole((EXPERTS, D)),
            whole((HEADS, TABLE)), *[whole((D,))] * 7,
        ],
        out_shape=[
            jax.ShapeDtypeStruct(shape, F32)
            for shape in (
                (local, D, FF), (local, FF, D), (local, FF), (local, D), (D, 3 * D), (D, D), (EXPERTS, D),
                (HEADS, TABLE), *[(D,)] * 7,
            )
        ],
        compiler_params=params,
        name="finish",
    )(chunks, chunks, biases, shared, small)
    grad_up, grad_down, grad_up_bias, grad_down_bias, grad_qkv, grad_out, grad_router, grad_table = results[:8]
    grad_gain1, grad_bias1, grad_q, grad_v, grad_out_bias, grad_gain2, grad_bias2 = results[8:]
    return (
        output, grad_tokens, grad_gain1, grad_bias1, grad_qkv, grad_q, grad_v, grad_table.T, grad_out, grad_out_bias,
        grad_gain2, grad_bias2, grad_router.T, grad_up, grad_up_bias, grad_down, grad_down_bias,
    )


def solution(mesh):
    tokens = P(("dp", "expert"), None)
    expert = P("expert", None, None)
    expert_bias = P("expert", None)
    routes = P(("dp", "expert"))
    return jax.shard_map(
        shards,
        mesh=mesh,
        in_specs=(
            tokens, P(), P(), P(), P(), P(), P(), P(), P(), P(), P(), P(), expert, expert_bias, expert, expert_bias,
            routes, routes, tokens,
        ),
        out_specs=(
            tokens, tokens, P(), P(), P(), P(), P(), P(), P(), P(), P(), P(), P(), expert, expert_bias, expert,
            expert_bias,
        ),
        check_vma=False,
    )
```
